32 devices in a mesh: dp: 8 (over z, y), mp: 4 (over x, core).
Axes of the slice: x: 2, y: 2, z: 4, core: 2. Of those that a mesh axis runs over, the one named last changes fastest.
Arguments:
- tokens: bfloat16 [16384, 1024], P('dp'), may hold values from -6 to 6
- cotangent: float32 [16384, 1024], P('dp'), may hold values from -6 to 6
- lengths: int32 [8], P('dp'), may hold values from 409 to 2048, as said below
- qkv_weight: float32 [1024, 3, 1024], P('dp', None, 'mp'), may hold values from -0.1875 to 0.1875
- qkv_first: float32 [1024, 3, 1024], P('dp', None, 'mp')
- qkv_second: float32 [1024, 3, 1024], P('dp', None, 'mp'), as said below
- out_weight: float32 [1024, 1024], P('mp', 'dp'), may hold values from -0.5 to 0.5
- out_first: float32 [1024, 1024], P('mp', 'dp')
- out_second: float32 [1024, 1024], P('mp', 'dp'), as said below
- up_weight: float32 [1024, 4, 1024], P('dp', None, 'mp'), may hold values from -0.1875 to 0.1875
- up_first: float32 [1024, 4, 1024], P('dp', None, 'mp')
- up_second: float32 [1024, 4, 1024], P('dp', None, 'mp'), as said below
- down_weight: float32 [4, 1024, 1024], P(None, 'mp', 'dp'), may hold values from -0.09375 to 0.09375
- down_first: float32 [4, 1024, 1024], P(None, 'mp', 'dp')
- down_second: float32 [4, 1024, 1024], P(None, 'mp', 'dp'), as said below
- row_vectors: float32 [6, 1024], replicated, as said below
- row_first: float32 [6, 1024], replicated
- row_second: float32 [6, 1024], replicated, as said below
- col_bias: float32 [6, 1024], P(None, 'mp'), may hold values from -4 to 4
- col_first: float32 [6, 1024], P(None, 'mp')
- col_second: float32 [6, 1024], P(None, 'mp'), as said below
Outputs:
- outputs: float32 [16384, 1024], P('dp')
- input_grad: float32 [16384, 1024], P('dp')
- rms_stats: float32 [3], replicated
- qkv_first_new: float32 [1024, 3, 1024], P('dp', None, 'mp')
- qkv_second_new: float32 [1024, 3, 1024], P('dp', None, 'mp')
- qkv_weight_new: float32 [1024, 3, 1024], P('dp', None, 'mp')
- out_first_new: float32 [1024, 1024], P('mp', 'dp')
- out_second_new: float32 [1024, 1024], P('mp', 'dp')
- out_weight_new: float32 [1024, 1024], P('mp', 'dp')
- up_first_new: float32 [1024, 4, 1024], P('dp', None, 'mp')
- up_second_new: float32 [1024, 4, 1024], P('dp', None, 'mp')
- up_weight_new: float32 [1024, 4, 1024], P('dp', None, 'mp')
- down_first_new: float32 [4, 1024, 1024], P(None, 'mp', 'dp')
- down_second_new: float32 [4, 1024, 1024], P(None, 'mp', 'dp')
- down_weight_new: float32 [4, 1024, 1024], P(None, 'mp', 'dp')
- row_first_new: float32 [6, 1024], replicated
- row_second_new: float32 [6, 1024], replicated
- row_vectors_new: float32 [6, 1024], replicated
- col_first_new: float32 [6, 1024], P(None, 'mp')
- col_second_new: float32 [6, 1024], P(None, 'mp')
- col_bias_new: float32 [6, 1024], P(None, 'mp')
The draws below stay inside these ranges and needn't reach their ends.
Inputs may be any that keep to these rules, and one draw needn't show every extreme that they name: lengths of the valid prefixes; some sequence is full. `qkv_second`: every entry is positive. `out_second`: every entry is positive. `up_second`: every entry is positive. `down_second`: every entry is positive. `row_second`: every entry is positive. `col_second`: every entry is positive. `row_vectors`: gains of the norms near one in rows 0 and 3, biases in the other rows.
All inputs are finite; a program needn't handle non-finite values.
Results may differ from the reference program's by a relative error of at most 0.018.
Values may be sent and summed in bfloat16 or wider, within the bound.
No kernel may reach another device: no remote copies, remote signals or barrier semaphores. Data moves between devices by JAX's collectives and lax.ppermute only.
A program may use at most 192 MiB of HBM per device.

```python
import math
from functools import partial
import jax
import jax.numpy as jnp
from jax import lax

D = 1024
HEADS = 16
HEAD_DIM = 64
FF = 4096
LENGTH = 2048
STEP = 5
SEQS = 8
TOKENS = 16384


def first_moment(key, shape, spread):
    return spread * jax.random.normal(key, shape, jnp.float32)


def second_moment(key, shape, spread):
    factor = jax.random.uniform(key, shape, jnp.float32, 0.0, math.log(4.0))
    return spread * spread * jnp.exp(factor)


def draw_lengths(key, part):
    key = jax.random.fold_in(key, 3)
    jitter_key, chosen_key = jax.random.split(key)
    position = jnp.arange(SEQS)
    centre = (LENGTH + 2 * LENGTH * position // max(SEQS - 1, 1)) // 3
    jitter = jax.random.randint(jitter_key, (SEQS,), -(LENGTH // 6), LENGTH // 6 + 1)
    clipped = jnp.clip(centre + jitter, LENGTH // 5, LENGTH)
    chosen = jax.random.randint(chosen_key, (), 0, SEQS)
    return jnp.where(position == chosen, LENGTH, clipped).astype(jnp.int32)


def draw_row_vectors(key, part):
    key = jax.random.fold_in(key, 5)
    noise = jax.random.normal(key, (6, D), jnp.float32)
    row_ids = jnp.arange(6)[:, None]
    is_gain = (row_ids == 0) | (row_ids == 3)
    return jnp.where(is_gain, 1.0 + 0.15 * jnp.clip(noise, -3.0, 3.0), 0.3 * noise)


def draw_qkv_first(key, part):
    key = jax.random.fold_in(key, 11)
    return first_moment(key, (D, 3, D), math.sqrt(TOKENS))


def draw_qkv_second(key, part):
    key = jax.random.fold_in(key, 12)
    return second_moment(key, (D, 3, D), math.sqrt(TOKENS))


def draw_out_first(key, part):
    key = jax.random.fold_in(key, 13)
    return first_moment(key, (D, D), 0.6 * math.sqrt(TOKENS))


def draw_out_second(key, part):
    key = jax.random.fold_in(key, 14)
    return second_moment(key, (D, D), 0.6 * math.sqrt(TOKENS))


def draw_up_first(key, part):
    key = jax.random.fold_in(key, 15)
    return first_moment(key, (D, FF // D, D), 0.3 * math.sqrt(TOKENS))


def draw_up_second(key, part):
    key = jax.random.fold_in(key, 16)
    return second_moment(key, (D, FF // D, D), 0.3 * math.sqrt(TOKENS))


def draw_down_first(key, part):
    key = jax.random.fold_in(key, 17)
    return first_moment(key, (FF // D, D, D), 0.6 * math.sqrt(TOKENS))


def draw_down_second(key, part):
    key = jax.random.fold_in(key, 18)
    return second_moment(key, (FF // D, D, D), 0.6 * math.sqrt(TOKENS))


def draw_row_first(key, part):
    key = jax.random.fold_in(key, 19)
    return first_moment(key, (6, D), math.sqrt(TOKENS))


def draw_row_second(key, part):
    key = jax.random.fold_in(key, 20)
    return second_moment(key, (6, D), math.sqrt(TOKENS))


def draw_col_first(key, part):
    key = jax.random.fold_in(key, 21)
    return first_moment(key, (2 + FF // D, D), 0.5 * math.sqrt(TOKENS))


def draw_col_second(key, part):
    key = jax.random.fold_in(key, 22)
    return second_moment(key, (2 + FF // D, D), 0.5 * math.sqrt(TOKENS))


def block_levels(rng, dims, cuts, least, high):
    loudness, own = 1.0, jax.random.fold_in(rng, 6)
    for dim, parts in cuts:
        draws = jnp.exp(jax.random.uniform(jax.random.fold_in(own, dim), (parts,), jnp.float32, least / len(cuts), high / len(cuts)))
        loudness = loudness * jnp.repeat(draws, dims[dim] // parts).reshape([-1 if axis == dim else 1 for axis in range(len(dims))])
    return loudness


def gaussian(own_key, shape, width, reach, pieces=(), dtype=jnp.bfloat16):
    factor_of = block_levels(own_key, shape, pieces, -0.22, 0.18) if pieces else 1.0
    array = jax.random.normal(own_key, shape, jnp.float32) * width * factor_of
    return jnp.minimum(jnp.maximum(array, -reach), reach).astype(dtype)


def setup_inputs(seed: int = 0) -> dict:
    seeds = jax.random.split(jax.random.key(seed), 22)
    return {
        "tokens": gaussian(seeds[0], (TOKENS, D), 1.0, 6.0, ((0, 8),)),
        "cotangent": gaussian(seeds[1], (TOKENS, D), 1.0, 6.0, ((0, 8),), jnp.float32),
        "lengths": draw_lengths(jax.random.fold_in(seeds[21], 71), 0),
        "qkv_weight": gaussian(seeds[3], (D, 3, D), D ** -0.5, 0.1875, ((0, 8), (2, 4)), jnp.float32),
        "qkv_first": draw_qkv_first(jax.random.fold_in(seeds[21], 71), 0),
        "qkv_second": draw_qkv_second(jax.random.fold_in(seeds[21], 71), 0),
        "out_weight": gaussian(seeds[6], (D, D), (D // 8) ** -0.5, 0.5, ((0, 4), (1, 8)), jnp.float32),
        "out_first": draw_out_first(jax.random.fold_in(seeds[21], 71), 0),
        "out_second": draw_out_second(jax.random.fold_in(seeds[21], 71), 0),
        "up_weight": gaussian(seeds[9], (D, FF // D, D), D ** -0.5, 0.1875, ((0, 8), (2, 4)), jnp.float32),
        "up_first": draw_up_first(jax.random.fold_in(seeds[21], 71), 0),
        "up_second": draw_up_second(jax.random.fold_in(seeds[21], 71), 0),
        "down_weight": gaussian(seeds[12], (FF // D, D, D), FF ** -0.5, 0.09375, ((1, 4), (2, 8)), jnp.float32),
        "down_first": draw_down_first(jax.random.fold_in(seeds[21], 71), 0),
        "down_second": draw_down_second(jax.random.fold_in(seeds[21], 71), 0),
        "row_vectors": draw_row_vectors(jax.random.fold_in(seeds[21], 71), 0),
        "row_first": draw_row_first(jax.random.fold_in(seeds[21], 71), 0),
        "row_second": draw_row_second(jax.random.fold_in(seeds[21], 71), 0),
        "col_bias": gaussian(seeds[18], (2 + FF // D, D), 0.3, 4.0, ((1, 4),), jnp.float32),
        "col_first": draw_col_first(jax.random.fold_in(seeds[21], 71), 0),
        "col_second": draw_col_second(jax.random.fold_in(seeds[21], 71), 0),
    }


norm_eps = 1e-05
masked_score = -1e+30
first_decay = 0.5
second_decay = 0.5
matrix_rate = 0.03
vector_rate = 0.4
weight_decay = 0.1
adam_eps = 1e-08

@jax.custom_vjp
def low(v):
    return lax.optimization_barrier(v.astype(jnp.bfloat16)).astype(jnp.float32)

@jax.custom_vjp
def low_back(v):
    return v

def low_keep(v):
    return (low(v), None)

def low_pass(kept, grad):
    return (grad,)

def back_keep(v):
    return (v, None)

def back_low(kept, grad):
    return (low(grad),)
low.defvjp(low_keep, low_pass)
low_back.defvjp(back_keep, back_low)

def product(left, right):
    return jnp.dot(left, right, precision=lax.Precision.HIGHEST, preferred_element_type=jnp.float32)

def layer_norm(values_in, gain, shift):
    average = lax.optimization_barrier(jnp.mean(values_in, axis=-1, keepdims=True))
    centred = values_in - average
    variance = lax.optimization_barrier(jnp.mean(centred * centred, axis=-1, keepdims=True))
    return centred * lax.rsqrt(variance + norm_eps) * gain + shift

def gelu_tanh(hidden):
    return 0.5 * hidden * (1.0 + jnp.tanh(0.7978845608028654 * (hidden + 0.044715 * hidden * hidden * hidden)))

def adamw(weight, moment_one, moment_two, gradient, learn_rate, decay_rate):
    moment_one = first_decay * moment_one + (1.0 - first_decay) * gradient
    moment_two = second_decay * moment_two + (1.0 - second_decay) * gradient * gradient
    correct_one = 1.0 - first_decay ** STEP
    correct_two = 1.0 - second_decay ** STEP
    direction = moment_one / correct_one / (jnp.sqrt(moment_two / correct_two) + adam_eps)
    return (moment_one, moment_two, weight - learn_rate * (direction + decay_rate * weight))

def attend_one(element):
    queries, key_rows, values, length = element
    scores = jnp.einsum('qhd,khd->hqk', queries, key_rows, precision=lax.Precision.HIGHEST) * HEAD_DIM ** (-0.5)
    head_ids = jnp.arange(HEADS).astype(jnp.float32)
    slopes = jnp.exp2(-8.0 * (head_ids + 1.0) / HEADS)
    places = jnp.arange(LENGTH)
    offset = (places[None, :] - places[:, None]).astype(jnp.float32)
    scores = scores + slopes[:, None, None] * offset[None]
    allowed = (places[None, :] <= places[:, None]) & (places[None, :] < length)
    scores = low_back(jnp.where(allowed[None], scores, masked_score))
    highest = lax.optimization_barrier(jnp.max(scores, axis=-1, keepdims=True))
    exponent = jnp.exp(scores - highest)
    probabilities = low(exponent / lax.optimization_barrier(jnp.sum(exponent, axis=-1, keepdims=True)))
    return jnp.einsum('hqk,khd->qhd', probabilities, values, precision=lax.Precision.HIGHEST)

def forward(lengths, inputs, qkv_weight, out_weight, up_weight, down_weight, row_vectors, col_bias):
    normed_one = low(layer_norm(inputs, row_vectors[0], row_vectors[1]))
    projected = product(normed_one, low(qkv_weight).reshape(D, 3 * D)).reshape(TOKENS, 3, D)
    queries = low(low_back(projected[:, 0] + col_bias[0]))
    key_rows = low(low_back(projected[:, 1]))
    values = low(low_back(projected[:, 2] + col_bias[1]))
    head_shape = (SEQS, LENGTH, HEADS, HEAD_DIM)
    attended = lax.map(jax.checkpoint(attend_one), (queries.reshape(head_shape), key_rows.reshape(head_shape), values.reshape(head_shape), lengths))
    attended = low(low_back(attended.reshape(TOKENS, D)))
    branch_a = low_back(product(attended, low(out_weight)) + row_vectors[2])
    resid = inputs + branch_a
    normed_two = low(layer_norm(resid, row_vectors[3], row_vectors[4]))
    hidden = low_back(product(normed_two, low(up_weight).reshape(D, FF)) + col_bias[2:].reshape(FF))
    active = low(gelu_tanh(hidden))
    branch_m = low_back(product(active, low(down_weight).reshape(FF, D)) + row_vectors[5])
    return (resid + branch_m, (branch_a, branch_m))

def reference(tokens, cotangent, lengths, qkv_weight, qkv_first, qkv_second, out_weight, out_first, out_second, up_weight, up_first, up_second, down_weight, down_first, down_second, row_vectors, row_first, row_second, col_bias, col_first, col_second):
    inputs = tokens.astype(jnp.float32)
    outputs, pullback, branches = jax.vjp(partial(forward, lengths), inputs, qkv_weight, out_weight, up_weight, down_weight, row_vectors, col_bias, has_aux=True)
    gradients = pullback(cotangent)
    valid_rows = (jnp.arange(LENGTH)[None, :] < lengths[:, None]).reshape(TOKENS).astype(jnp.float32)[:, None]
    counted = jnp.sum(valid_rows) * D
    rms_stats = jnp.stack([jnp.sqrt(jnp.sum(valid_rows * outputs * outputs) / counted), jnp.sqrt(jnp.sum(valid_rows * branches[0] * branches[0]) / counted), jnp.sqrt(jnp.sum(valid_rows * branches[1] * branches[1]) / counted)])
    qkv_new = adamw(qkv_weight, qkv_first, qkv_second, gradients[1], matrix_rate, weight_decay)
    out_new = adamw(out_weight, out_first, out_second, gradients[2], matrix_rate, weight_decay)
    up_new = adamw(up_weight, up_first, up_second, gradients[3], matrix_rate, weight_decay)
    down_new = adamw(down_weight, down_first, down_second, gradients[4], matrix_rate, weight_decay)
    row_new = adamw(row_vectors, row_first, row_second, gradients[5], vector_rate, 0.0)
    col_new = adamw(col_bias, col_first, col_second, gradients[6], vector_rate, 0.0)
    return (outputs, gradients[0], rms_stats, qkv_new[0], qkv_new[1], qkv_new[2], out_new[0], out_new[1], out_new[2], up_new[0], up_new[1], up_new[2], down_new[0], down_new[1], down_new[2], row_new[0], row_new[1], row_new[2], col_new[0], col_new[1], col_new[2])
```

```python
import functools

import jax
import jax.numpy as jnp
from jax import lax
from jax.experimental import pallas as pl
from jax.experimental.pallas import tpu as pltpu
from jax.sharding import PartitionSpec as P

HEADS = 16
HEAD_DIM = 64
STEP = 5

norm_eps = 1e-05
masked_score = -1e30
first_decay = 0.5
second_decay = 0.5
matrix_rate = 0.03
vector_rate = 0.4
weight_decay = 0.1
adam_eps = 1e-08
gelu_scale = 0.7978845608028654
gelu_cubic = 0.044715

F32 = jnp.float32
BF = jnp.bfloat16
NN = (((1,), (0,)), ((), ()))
NT = (((1,), (1,)), ((), ()))
TN = (((0,), (0,)), ((), ()))
MIB = 2**20


def dot(a, b, dims=NN):
    return lax.dot_general(a, b, dims, preferred_element_type=F32)


def adamw(weight, moment_one, moment_two, gradient, learn_rate, decay_rate):
    moment_one = first_decay * moment_one + (1.0 - first_decay) * gradient
    moment_two = second_decay * moment_two + (1.0 - second_decay) * gradient * gradient
    correct_one = 1.0 - first_decay**STEP
    correct_two = 1.0 - second_decay**STEP
    direction = moment_one / correct_one / (jnp.sqrt(moment_two / correct_two) + adam_eps)
    return (moment_one, moment_two, weight - learn_rate * (direction + decay_rate * weight))


def to_core(x):
    return lax.ppermute(x, "mp", [(i, i ^ 1) for i in range(lax.axis_size("mp"))])


def to_chip(x):
    return lax.ppermute(x, "mp", [(i, i ^ 2) for i in range(lax.axis_size("mp"))])


def to_all(x):
    return lax.all_to_all(x, "mp", split_axis=0, concat_axis=0, tiled=True)


def ring_order(n):
    return [0, 2, 4, 6, 7, 5, 3, 1] if n == 8 else list(range(n))


def ring_perms(n):
    order = ring_order(n)
    up = [(order[p], order[(p + 1) % n]) for p in range(n)]
    down = [(order[p], order[(p - 1) % n]) for p in range(n)]
    return up, down


def ring_index(n):
    order = ring_order(n)
    place = jnp.array([order.index(i) for i in range(n)], jnp.int32)[lax.axis_index("dp")]
    return jnp.array(order, jnp.int32)[(place + jnp.arange(n)) % n]


class Gather:
    def __init__(self, piece):
        self.n = lax.axis_size("dp")
        self.perms = ring_perms(self.n)
        self.pieces = [piece] + [None] * (self.n - 1)
        self.up = self.down = piece
        self.done = 0

    def hop(self, *gates):
        if self.done == self.n // 2:
            return
        self.done += 1
        self.up = self.pieces[self.n - self.done] = lax.ppermute(after(self.up, *gates), "dp", self.perms[0])
        if self.done <= (self.n - 1) // 2:
            self.down = self.pieces[self.done] = lax.ppermute(after(self.down, *gates), "dp", self.perms[1])

    def finish(self):
        while self.done < self.n // 2:
            self.hop()
        return self.pieces


class Reduce:
    def __init__(self, total, index):
        self.n = lax.axis_size("dp")
        self.perms = ring_perms(self.n)
        self.total, self.index = total, index
        self.rows = total.shape[0] // self.n
        self.up = self.down = None
        self.done = 0

    def block(self, k):
        return lax.dynamic_slice_in_dim(self.total, self.index[k % self.n] * self.rows, self.rows, 0)

    def add(self, x, k):
        if x is None:
            return self.block(k)
        return (x.astype(F32) + self.block(k).astype(F32)).astype(BF)

    def hop(self, *gates):
        ups, downs = self.n // 2, (self.n - 1) // 2
        if self.done == ups:
            return
        up = after(self.add(self.up, ups - self.done), *gates)
        if self.done < downs:
            down = after(self.add(self.down, self.done - downs), *gates)
            self.down = lax.ppermute(down, "dp", self.perms[1])
        self.up = lax.ppermute(up, "dp", self.perms[0])
        self.done += 1

    def finish(self):
        while self.done < self.n // 2:
            self.hop()
        return self.block(0).astype(F32) + self.up.astype(F32) + self.down.astype(F32)


def after(x, *others):
    return lax.optimization_barrier((x, *others))[0] if others else x


def cost(flops, nbytes):
    return pl.CostEstimate(flops=int(flops), bytes_accessed=int(nbytes), transcendentals=0)


def whole(shape):
    return pl.BlockSpec(shape, lambda *_: (0,) * len(shape), pipeline_mode=pl.Buffered(1))


def assemble_kernel(index_ref, pieces, out_ref, at):
    rows, cols = pieces[0].shape
    for k, piece in enumerate(pieces):
        row = pl.multiple_of(index_ref[k] * rows, rows)
        out_ref[pl.ds(row, rows), at : at + cols] = piece[...]


def assemble(index, *groups):
    n = len(groups[0])
    shapes = [group[0].shape for group in groups]
    shape = (n * shapes[0][0], sum(cols for _, cols in shapes))

    def kernel(index_ref, *refs):
        at = 0
        for k, (_, cols) in enumerate(shapes):
            assemble_kernel(index_ref, refs[k * n : (k + 1) * n], refs[-1], at)
            at += cols

    return pl.pallas_call(
        kernel,
        out_shape=jax.ShapeDtypeStruct(shape, BF),
        grid=(1,),
        in_specs=[pl.BlockSpec(memory_space=pltpu.SMEM)]
        + [whole(piece.shape) for group in groups for piece in group],
        out_specs=whole(shape),
        compiler_params=pltpu.CompilerParams(vmem_limit_bytes=16 * MIB),
        cost_estimate=cost(0, 4 * shape[0] * shape[1]),
        name="assemble",
    )(index, *[piece for group in groups for piece in group])


def split3(x):
    hi = x.astype(BF).astype(F32)
    rest = x - hi
    mid = rest.astype(BF).astype(F32)
    return hi, mid, rest - mid


def put3(base, lane, first, x):
    hi, mid, lo = split3(x)
    return jnp.where(
        lane == first,
        hi,
        jnp.where(lane == first + 1, mid, jnp.where(lane == first + 2, lo, base)),
    )


def project_kernel(index_ref, slope_ref, length_ref, n_ref, bias_ref, *refs, heads):
    *pieces, q_ref, k_ref, v_ref, w_ref = refs

    @pl.when(pl.program_id(0) == 0)
    def _():
        assemble_kernel(index_ref, pieces, w_ref, 0)

    rows = n_ref.shape[0]
    width = heads * HEAD_DIM
    out = dot(n_ref[...], w_ref[...])
    query = (out[:, :width] + bias_ref[0:1, :]).astype(BF).astype(F32) * (HEAD_DIM**-0.5)
    key = out[:, width : 2 * width]
    value = out[:, 2 * width :] + bias_ref[1:2, :]
    lane = lax.broadcasted_iota(jnp.int32, (rows, 128), 1)
    at = lax.broadcasted_iota(jnp.int32, (rows, 128), 0) + pl.program_id(0) * rows
    ones = ((lane >= 64) & (lane < 67)).astype(F32)
    more = ((lane >= 67) & (lane < 70)).astype(F32)
    seen = at < length_ref[0]
    zero = jnp.zeros((rows, 64), F32)
    for h in range(heads):
        cols = slice(h * HEAD_DIM, (h + 1) * HEAD_DIM)
        slope = jnp.where(seen, at.astype(F32) * slope_ref[h], masked_score)
        q_ref[h] = (jnp.concatenate([query[:, cols], zero], axis=1) + ones).astype(BF)
        wide = jnp.concatenate([key[:, cols], zero], axis=1) + more
        k_ref[h] = put3(wide, lane, 64, slope).astype(BF)
        v_ref[h] = (jnp.concatenate([value[:, cols], zero], axis=1) + ones).astype(BF)


def project(normed, index, pieces, col_bias, slopes, length):
    span, depth = normed.shape
    cols = pieces[0].shape[1]
    heads = slopes.shape[0]
    tile = 256
    shape = jax.ShapeDtypeStruct((heads, span, 128), BF)
    return pl.pallas_call(
        functools.partial(project_kernel, heads=heads),
        out_shape=(shape,) * 3 + (jax.ShapeDtypeStruct((depth, cols), BF),),
        grid=(span // tile,),
        in_specs=[pl.BlockSpec(memory_space=pltpu.SMEM)] * 3
        + [pl.BlockSpec((tile, depth), lambda i: (i, 0)), whole(col_bias.shape)]
        + [whole(piece.shape) for piece in pieces],
        out_specs=[pl.BlockSpec((heads, tile, 128), lambda i: (0, i, 0))] * 3
        + [whole((depth, cols))],
        compiler_params=pltpu.CompilerParams(vmem_limit_bytes=40 * MIB),
        cost_estimate=cost(2 * span * depth * cols, 12 * MIB),
        name="project",
    )(index, slopes, length, normed, col_bias, *pieces)


def attend_forward_kernel(q_ref, k_ref, v_ref, o_ref, qb_ref, send_ref, *, bq, span):
    lane = lax.broadcasted_iota(jnp.int32, (bq, 128), 1)
    row = lax.broadcasted_iota(jnp.int32, (bq, bq), 0)
    causal = row >= lax.broadcasted_iota(jnp.int32, (bq, bq), 1)
    for i in range(span // bq):
        outs = []
        here = pl.ds(i * bq, bq)
        for h in range(2):
            q = q_ref[h, here, :]
            near = jnp.where(causal, dot(q, k_ref[h, here, :], NT), masked_score)
            highest = jnp.max(near, axis=1, keepdims=True)
            if i:
                before = pl.ds(0, i * bq)
                far = dot(q, k_ref[h, before, :], NT)
                highest = jnp.maximum(highest, jnp.max(far, axis=1, keepdims=True))
            acc = dot(jnp.exp(near - highest).astype(BF), v_ref[h, here, :])
            if i:
                acc = acc + dot(jnp.exp(far - highest).astype(BF), v_ref[h, before, :])
            total = acc[:, 64:65]
            outs.append((acc[:, :64] * (1.0 / total)).astype(BF))
            log_sum = highest + jnp.log(total)
            qb_ref[h, here, :] = put3(q.astype(F32), lane, 67, -log_sum).astype(BF)
        o_ref[here, :] = jnp.concatenate(outs, axis=1)
    half = span // 2
    for j in range(4):
        send_ref[j] = o_ref[pl.ds(j % 2 * half, half), :]


def pair_spec(span, pair):
    return pl.BlockSpec((2, span, 128), lambda i: (pair, 0, 0), pipeline_mode=pl.Buffered(1))


def attend_forward(q, k, v, pair):
    span = q.shape[1]
    shapes = [(span, 128), (2, span, 128), (4, span // 2, 128)]
    return pl.pallas_call(
        functools.partial(attend_forward_kernel, bq=min(512, span), span=span),
        out_shape=[jax.ShapeDtypeStruct(x, BF) for x in shapes],
        grid=(1,),
        in_specs=[pair_spec(span, pair)] * 3,
        out_specs=[whole(x) for x in shapes],
        compiler_params=pltpu.CompilerParams(vmem_limit_bytes=50 * MIB),
        cost_estimate=cost(12e9, 5 * MIB),
        name="attend_forward",
    )(q, k, v)


def attend_backward_kernel(half_ref, q_ref, k_ref, v_ref, o_ref, *refs, bk, span, chunks):
    partials, (d_ref, sib_ref, sum_ref, do_ref, doa_ref, dq_ref) = refs[:-6], refs[-6:]
    half = span // 2
    rows = half // chunks
    for c, part in enumerate(partials):
        for side in range(2):
            total = part[side].astype(F32) + part[2 + side].astype(F32)
            do_ref[pl.ds(side * half + c * rows, rows), :] = total.astype(BF)
    lane = lax.broadcasted_iota(jnp.int32, (span, 128), 1)
    row = lax.broadcasted_iota(jnp.int32, (bk, bk), 0)
    causal = row <= lax.broadcasted_iota(jnp.int32, (bk, bk), 1)
    grad = do_ref[...].astype(F32)
    prod = grad * o_ref[...].astype(F32)
    for h in range(2):
        cols = slice(h * HEAD_DIM, (h + 1) * HEAD_DIM)
        delta = jnp.sum(prod[:, cols], axis=1, keepdims=True)
        base = jnp.concatenate([grad[:, cols], jnp.zeros((span, 64), F32)], axis=1)
        doa_ref[h] = put3(base, lane, 64, -delta).astype(BF)
    dq_ref[...] = jnp.zeros_like(dq_ref)
    value_sums = jnp.zeros((1, 128), F32)
    for j in range(span // bk):
        dks, dvs = [], []
        here = pl.ds(j * bk, bk)
        rest = pl.ds(j * bk, span - j * bk)
        for h in range(2):
            k = k_ref[h, here, :]
            q = q_ref[h, rest, :]
            do = doa_ref[h, rest, :]
            p = jnp.exp(dot(k, q, NT))
            near = jnp.where(causal, p[:, :bk], 0.0)
            p = jnp.concatenate([near, p[:, bk:]], axis=1) if rest.size > bk else near
            ds = (p * dot(v_ref[h, here, :], do, NT)).astype(BF)
            dvs.append(dot(p.astype(BF), do)[:, :64])
            dks.append(dot(ds, q)[:, :64])
            dq_ref[h, :, rest] += dot(k[:, :64], ds, TN)
        d_ref[1, here, :] = jnp.concatenate(dks, axis=1).astype(BF)
        value_grad = jnp.concatenate(dvs, axis=1).astype(BF)
        d_ref[2, here, :] = value_grad
        value_sums += jnp.sum(value_grad.astype(F32), axis=0, keepdims=True)
    dq = jnp.concatenate([dq_ref[0], dq_ref[1]], axis=0).T * (HEAD_DIM**-0.5)
    dq = dq.astype(BF)
    d_ref[0] = dq
    sum_ref[0:1, :] = jnp.sum(dq.astype(F32), axis=0, keepdims=True)
    sum_ref[1:2, :] = value_sums
    for kind in range(3):
        sib_ref[kind] = d_ref[kind, pl.ds(pl.multiple_of((1 - half_ref[0]) * half, half), half), :]


def attend_backward(scalars, qb, k, v, o, partials, pair):
    span = qb.shape[1]
    chunks = len(partials)
    part = pl.BlockSpec((4, span // 2 // chunks, 128), lambda i: (0, 0, pair), pipeline_mode=pl.Buffered(1))
    shapes = [((3, span, 128), BF), ((3, span // 2, 128), BF), ((2, 128), F32)]
    return pl.pallas_call(
        functools.partial(attend_backward_kernel, bk=min(256, span), span=span, chunks=chunks),
        out_shape=[jax.ShapeDtypeStruct(*x) for x in shapes],
        grid=(1,),
        in_specs=[
            pl.BlockSpec(memory_space=pltpu.SMEM),
            pair_spec(span, 0),
            pair_spec(span, pair),
            pair_spec(span, pair),
            whole((span, 128)),
        ]
        + [part] * chunks,
        out_specs=[whole(x[0]) for x in shapes],
        scratch_shapes=[
            pltpu.VMEM((span, 128), BF),
            pltpu.VMEM((2, span, 128), BF),
            pltpu.VMEM((2, 64, span), F32),
        ],
        compiler_params=pltpu.CompilerParams(vmem_limit_bytes=50 * MIB),
        cost_estimate=cost(18e9, 6 * MIB),
        name="attend_backward",
    )(scalars, qb, k, v, o, *partials)


def norm_parts(x):
    average = jnp.mean(x, axis=-1, keepdims=True)
    centred = x - average
    variance = jnp.mean(centred * centred, axis=-1, keepdims=True)
    scale = lax.rsqrt(variance + norm_eps)
    return centred * scale, scale


def norm_back(grad, unit, scale, gain):
    weighted = grad * gain
    mean_one = jnp.mean(weighted, axis=-1, keepdims=True)
    mean_two = jnp.mean(weighted * unit, axis=-1, keepdims=True)
    return scale * (weighted - mean_one - unit * mean_two)


def middle_kernel(
    scalar_ref,
    o0_ref,
    o1_ref,
    tokens_ref,
    cot_ref,
    first_own_ref,
    first_sib_ref,
    late_own_ref,
    late_sib_ref,
    row_ref,
    bias_ref,
    *refs,
    chunk,
):
    (resid_ref, n2_ref, g_ref, du_ref, da_ref, dr_ref, mlp_ref, do_ref, sum_ref,
     up_sum_ref, out_w) = refs[-11:]
    step = pl.program_id(0)
    tile, depth = tokens_ref.shape

    @pl.when(step == 0)
    def _():
        for k, ref in enumerate((first_own_ref, first_sib_ref)):
            for chip in range(2):
                for pair in range(2):
                    at = (pair * 4 + (scalar_ref[3] ^ (k + 2 * chip))) * 128
                    cols = slice(256 * chip + 128 * pair, 256 * chip + 128 * (pair + 1))
                    out_w[:, pl.ds(pl.multiple_of(at, 128), 128)] = ref[:, cols]
        sum_ref[...] = jnp.zeros_like(sum_ref)
        up_sum_ref[...] = jnp.zeros_like(up_sum_ref)

    heads = jnp.concatenate([ref[j] for ref in (o0_ref, o1_ref) for j in range(4)], axis=1)
    branch = dot(heads, out_w[...], NT) + row_ref[2:3, :]
    resid = tokens_ref[...].astype(F32) + branch
    resid_ref[...] = resid
    at = lax.broadcasted_iota(jnp.int32, (tile, 1), 0) + (
        scalar_ref[0] * scalar_ref[1] + (chunk * pl.num_programs(0) + step) * tile
    )
    valid = (at < scalar_ref[2]).astype(F32)
    unit, scale = norm_parts(resid)
    n2 = (unit * row_ref[3:4, :] + row_ref[4:5, :]).astype(BF)
    n2_ref[...] = n2
    cot = cot_ref[...]
    dm = cot.astype(BF)
    mlp = None
    hid = late_own_ref.shape[1] // 2
    for half, late in enumerate((late_own_ref, late_sib_ref)):
        up, down = late.at[:, :hid], late.at[:, hid:]
        cols = slice(half * hid, (half + 1) * hid)
        u = dot(n2, up[...]) + bias_ref[half : half + 1, :]
        square = u * u
        t = jnp.tanh(gelu_scale * (u + gelu_cubic * square * u))
        plus = 0.5 * (1.0 + t)
        g = (u * plus).astype(BF)
        slope = plus + (0.5 * gelu_scale) * u * (1.0 - t * t) * (1.0 + 3.0 * gelu_cubic * square)
        du_wide = (dot(dm, down[...]) * slope).astype(BF)
        g_ref[:, cols] = g
        du_ref[:, cols] = du_wide
        up_sum_ref[half : half + 1, :] += jnp.sum(du_wide.astype(F32), axis=0, keepdims=True)
        m = dot(g, down[...], NT)
        d = dot(du_wide, up[...], NT)
        mlp, dn2 = (m, d) if mlp is None else (mlp + m, dn2 + d)
    mlp_ref[...] = mlp.astype(BF)
    dr = norm_back(dn2, unit, scale, row_ref[3:4, :]) + 0.5 * cot
    dr_ref[...] = dr
    da = dr.astype(BF)
    da_ref[...] = da
    do = dot(da, out_w[...]).astype(BF)
    for j in range(4):
        do_ref[j] = jnp.concatenate([do[:, 128 * (j + 4 * p) : 128 * (j + 4 * p + 1)] for p in range(2)], axis=1)
    for k, x in enumerate(
        (dn2 * unit, dn2, da.astype(F32), 0.5 * dm.astype(F32), valid * branch * branch)
    ):
        sum_ref[k : k + 1, :] += jnp.sum(x, axis=0, keepdims=True)


def middle(chunk, chunks, scalars, heads_in, tokens, cotangent, weights, row_vectors, up_bias, before):
    depth = tokens.shape[1]
    half = tokens.shape[0] // 2
    tile = 256
    steps = half // chunks // tile
    hidden = weights[2].shape[1]
    own = lambda i, s: (chunk * steps + i, 0)
    absolute = lambda i, s: (s[0] * (half // tile) + chunk * steps + i, 0)
    part = lambda i, s: (i, 0)
    kept = [(depth, F32), (depth, BF), (hidden, BF), (hidden, BF), (depth, BF), (depth, F32)]
    n_in = 10
    return pl.pallas_call(
        functools.partial(middle_kernel, chunk=chunk),
        out_shape=[jax.ShapeDtypeStruct((half, w), t) for w, t in kept]
        + [
            jax.ShapeDtypeStruct((half // chunks, depth), BF),
            jax.ShapeDtypeStruct((4, half // chunks, 256), BF),
        ]
        + [jax.ShapeDtypeStruct((8, depth), F32), jax.ShapeDtypeStruct((2, hidden // 2), F32)],
        grid_spec=pltpu.PrefetchScalarGridSpec(
            num_scalar_prefetch=1,
            grid=(steps,),
            in_specs=[pl.BlockSpec((4, tile, 128), lambda i, s: (0, *own(i, s)))] * 2
            + [pl.BlockSpec((tile, depth), absolute)] * 2
            + [whole(w.shape) for w in weights]
            + [whole(row_vectors.shape), whole(up_bias.shape)]
            + [pl.BlockSpec(memory_space=pl.ANY)] * len(before),
            out_specs=[pl.BlockSpec((tile, w), own) for w, _ in kept]
            + [
                pl.BlockSpec((tile, depth), part),
                pl.BlockSpec((4, tile, 256), lambda i, s: (0, i, 0)),
            ]
            + [whole((8, depth)), whole((2, hidden // 2))],
            scratch_shapes=[
                pltpu.VMEM((depth, 1024), BF),
            ],
        ),
        input_output_aliases={n_in + 1 + k: k for k in range(len(before))},
        compiler_params=pltpu.CompilerParams(vmem_limit_bytes=56 * MIB),
        cost_estimate=cost(21e9 / chunks, 24 * MIB),
        name="middle",
    )(scalars, *heads_in, tokens, cotangent, *weights, row_vectors, up_bias, *before)


def last_kernel(
    scalar_ref, o0_ref, o1_ref, s0_ref, s1_ref, w_own_ref, w_sib_ref, tokens_ref, dr_ref, row_ref, ig_ref, sum_ref,
):
    @pl.when(pl.program_id(0) == 0)
    def _():
        sum_ref[...] = jnp.zeros_like(sum_ref)

    def side(x, y):
        return jnp.concatenate([r[k] for k in range(3) for r in (x, y)], axis=1)

    dn1 = dot(side(o0_ref, o1_ref), w_own_ref[...], NT) + dot(side(s0_ref, s1_ref), w_sib_ref[...], NT)
    unit, scale = norm_parts(tokens_ref[...].astype(F32))
    ig_ref[...] = (dr_ref[...] + norm_back(dn1, unit, scale, row_ref[0:1, :])).astype(BF)
    sum_ref[0:1, :] += jnp.sum(dn1 * unit, axis=0, keepdims=True)
    sum_ref[1:2, :] += jnp.sum(dn1, axis=0, keepdims=True)


def last(chunk, chunks, scalars, own, sibling, w_own, w_sib, tokens, dr, row_vectors):
    depth = tokens.shape[1]
    half = tokens.shape[0] // 2
    tile = 256
    steps = half // chunks // tile
    absolute = lambda i, s: (s[0] * (half // tile) + chunk * steps + i, 0)
    return pl.pallas_call(
        last_kernel,
        out_shape=[
            jax.ShapeDtypeStruct((half // chunks, depth), BF),
            jax.ShapeDtypeStruct((8, depth), F32),
        ],
        grid_spec=pltpu.PrefetchScalarGridSpec(
            num_scalar_prefetch=1,
            grid=(steps,),
            in_specs=[pl.BlockSpec((3, tile, 128), lambda i, s: (0,) + absolute(i, s))] * 2
            + [pl.BlockSpec((3, tile, 128), lambda i, s: (0, chunk * steps + i, 0))] * 2
            + [whole(w_own.shape), whole(w_sib.shape)]
            + [
                pl.BlockSpec((tile, depth), absolute),
                pl.BlockSpec((tile, depth), lambda i, s: (chunk * steps + i, 0)),
                whole(row_vectors.shape),
            ],
            out_specs=[pl.BlockSpec((tile, depth), lambda i, s: (i, 0)), whole((8, depth))],
        ),
        compiler_params=pltpu.CompilerParams(vmem_limit_bytes=40 * MIB),
        cost_estimate=cost(3.2e9 / chunks, 10 * MIB),
        name="last",
    )(scalars, *own, *sibling, w_own, w_sib, tokens, dr, row_vectors)


def weight_grads_kernel(half_ref, n2_ref, cot_ref, da_ref, du_ref, g_ref, a0_ref, a1_ref, b0_ref, b1_ref, *refs):
    out_ref = refs[-1]
    o_refs = [r.at[0] for r in (a0_ref, a1_ref, b0_ref, b1_ref)]
    hidden = du_ref.shape[1]
    parts = [
        (n2_ref[...], [du_ref]),
        (cot_ref[...].astype(BF), [g_ref]),
        (da_ref[...], o_refs),
    ]
    at = 0
    for left, rights in parts:
        right = jnp.concatenate([r[...] for r in rights], axis=1) if len(rights) > 1 else rights[0][...]
        cols = slice(at, at + right.shape[1])
        at += right.shape[1]
        value = dot(left, right, TN)
        if len(refs) > 1:
            value = value + refs[0][:, cols].astype(F32)
        out_ref[:, cols] = value.astype(BF)


def weight_grads(side, scalars, n2, cotangent, da, du, g, heads_in, more=()):
    half, depth = n2.shape
    hidden = du.shape[1] // 2
    cols = 2 * hidden + 4 * 128
    tile = 256
    left = pl.BlockSpec((half, tile), lambda i, s: (0, i))
    right = lambda w: pl.BlockSpec((half, w), lambda i, s: (0, side), pipeline_mode=pl.Buffered(1))
    rows = pl.BlockSpec((tile, cols), lambda i, s: (i, 0))
    return pl.pallas_call(
        weight_grads_kernel,
        out_shape=jax.ShapeDtypeStruct((depth, cols), BF),
        grid_spec=pltpu.PrefetchScalarGridSpec(
            num_scalar_prefetch=1,
            grid=(depth // tile,),
            in_specs=[left, pl.BlockSpec((half, tile), lambda i, s: (s[0], i)), left]
            + [right(hidden), right(hidden)]
            + [
                pl.BlockSpec((1, half, 128), lambda i, s, flip=flip: (s[3] ^ flip, 0, 0), pipeline_mode=pl.Buffered(1))
                for flip in (side, side, side + 2, side + 2)
            ]
            + [rows] * len(more),
            out_specs=rows,
        ),
        compiler_params=pltpu.CompilerParams(vmem_limit_bytes=50 * MIB),
        cost_estimate=cost(2 * half * depth * cols, 18 * MIB),
        name="weight_grads",
    )(scalars, n2, cotangent, da, du, g, *heads_in, *heads_in, *more)


def finish_kernel(half_ref, *refs, steps):
    out_ref = refs[-1]
    for k, ref in enumerate(refs[:-1]):

        @pl.when(pl.program_id(0) // steps == k)
        def _():
            out_ref[...] = ref[...].astype(F32)


def finish(scalars, own, other):
    chunks = len(own)
    rows, depth = own[0].shape
    tile = 256
    steps = rows // tile
    span = lambda k: pl.BlockSpec((tile, depth), lambda i, s: (jnp.clip(i - k * steps, 0, steps - 1), 0))

    def out_index(i, s):
        first = i < chunks * steps
        return (jnp.where(first, s[0], 1 - s[0]) * chunks * steps + i - jnp.where(first, 0, chunks * steps), 0)

    return pl.pallas_call(
        functools.partial(finish_kernel, steps=steps),
        out_shape=jax.ShapeDtypeStruct((2 * chunks * rows, depth), F32),
        grid_spec=pltpu.PrefetchScalarGridSpec(
            num_scalar_prefetch=1,
            grid=(2 * chunks * steps,),
            in_specs=[span(k) for k in range(2 * chunks)],
            out_specs=pl.BlockSpec((tile, depth), out_index),
        ),
        compiler_params=pltpu.CompilerParams(vmem_limit_bytes=24 * MIB),
        cost_estimate=cost(0, 12 * chunks * rows * depth),
        name="finish",
    )(scalars, *own, *other)


def body(
    tokens,
    cotangent,
    lengths,
    qkv_weight,
    qkv_first,
    qkv_second,
    out_weight,
    out_first,
    out_second,
    up_weight,
    up_first,
    up_second,
    down_weight,
    down_first,
    down_second,
    row_vectors,
    row_first,
    row_second,
    col_bias,
    col_first,
    col_second,
):
    span, depth = tokens.shape
    half = span // 2
    share = qkv_weight.shape[0]
    n_dp = lax.axis_size("dp")
    device = lax.axis_index("mp")
    core = device % 2
    heads = qkv_weight.shape[2] // HEAD_DIM
    width = heads * HEAD_DIM
    hidden = up_weight.shape[1] * up_weight.shape[2]
    head_ids = device * heads + jnp.arange(heads)
    slopes = jnp.exp2(-8.0 * (head_ids.astype(F32) + 1.0) / HEADS)
    scalars = jnp.stack([core.astype(jnp.int32), jnp.int32(half), lengths[0], device.astype(jnp.int32)])

    index = ring_index(n_dp)
    out_piece = out_weight.astype(BF).T
    out_piece = jnp.concatenate([out_piece, to_chip(out_piece)], axis=1)
    qkv_ring = Gather(qkv_weight.astype(BF).reshape(share, 3 * width))
    out_ring = Gather(out_piece)
    up_ring = Gather(up_weight.astype(BF).reshape(share, hidden))
    down_ring = Gather(down_weight.astype(BF).reshape(hidden, share).T)
    gate = []
    for _ in range(n_dp // 2):
        gate.append(qkv_ring.up)
        qkv_ring.hop()
        out_ring.hop()
    up_bias = col_bias[2:].reshape(1, hidden)
    up_bias = jnp.concatenate([up_bias, to_core(up_bias)], axis=0)
    up_ring.hop(gate[-1])
    down_ring.hop(qkv_ring.up)

    unit_one, _ = norm_parts(tokens.astype(F32))
    normed = (unit_one * row_vectors[0] + row_vectors[1]).astype(BF)
    normed = after(normed, out_ring.up, out_ring.down, up_bias)
    q, k, v, qkv_w = project(normed, index, qkv_ring.finish(), col_bias, slopes, lengths)
    outs, heads_in = [], []
    for pair in range(2):
        ready = (up_ring.up,) if pair == 0 else (up_ring.up, down_ring.up)
        if pair == 0:
            up_ring.hop(q)
        q = after(q, *ready)
        o, qb, send = attend_forward(q, k, v, pair)
        outs.append((o, qb))
        heads_in.append(to_all(send))
        down_ring.hop(send)
        up_ring.hop(send)
    qkv_sib = to_core(qkv_w)
    out_w = assemble(index, out_ring.finish())
    late_w = assemble(index, up_ring.finish(), down_ring.finish())
    out_sib, late_sib = to_core(out_w), to_core(late_w)

    weights = (out_w, out_sib, late_w, late_sib)
    chunks = 2
    before, mlps, partials, sums, up_sums = (), [], [], 0.0, 0.0
    for chunk in range(chunks):
        got = middle(
            chunk,
            chunks,
            scalars,
            heads_in,
            tokens,
            cotangent,
            weights,
            row_vectors,
            up_bias,
            before,
        )
        before = got[:6]
        mlps.append(got[6])
        partials.append(to_all(got[7]))
        sums, up_sums = sums + got[8], up_sums + got[9]
    resid, n2, g, du, da, dr = before
    mlp_far = [to_chip(after(m, partials[-1])) for m in mlps]
    grad_args = (scalars, n2, cotangent, da, du, g)
    other_grads = weight_grads(1, *grad_args, heads_in)
    got_grads = to_core(other_grads)

    parts, part_sums, siblings = [], [], []
    for pair in range(2):
        o, qb = outs[pair]
        d, d_sib, s = attend_backward(scalars, after(qb, other_grads), k, v, o, partials, pair)
        parts.append(d)
        part_sums.append(s)
        siblings.append(to_core(d_sib))
        if pair == 0:
            total = weight_grads(0, *grad_args, heads_in, (after(got_grads, s),))
            middle_ring = Reduce(total, index)
            middle_ring.hop()
            outs[1] = (outs[1][0], after(outs[1][1], total))
    middle_ring.hop(part_sums[1])
    lasts = [
        last(c, chunks, scalars, parts, siblings, qkv_w, qkv_sib, tokens, dr, row_vectors)
        for c in range(chunks)
    ]
    last_sums = sum(x[1] for x in lasts)
    last_far = [to_chip(x[0]) for x in lasts]
    mlp_far = [after(f, lasts[-1][1]) for f in mlp_far]
    middle_ring.hop(lasts[-1][1])

    qkv_grad = jnp.concatenate([parts[p][kind] for kind in range(3) for p in range(2)], axis=1)
    qkv_wgrad = dot(normed, after(qkv_grad, lasts[-1][1]), TN).astype(BF)
    qkv_shard = Reduce(qkv_wgrad, index).finish().reshape(qkv_weight.shape)
    mid_shard = middle_ring.finish()
    up_shard = mid_shard[:, :hidden].reshape(up_weight.shape)
    down_shard = mid_shard[:, hidden : 2 * hidden].T.reshape(down_weight.shape)
    out_mine = mid_shard[:, 2 * hidden : 2 * hidden + width]
    out_theirs = to_chip(mid_shard[:, 2 * hidden + width :].astype(BF))
    out_shard = (out_mine + out_theirs.astype(F32)).T

    valid = ((core * half + jnp.arange(half)) < lengths[0]).astype(F32)[:, None]
    stat_out, stat_m, own_low = 0.0, 0.0, []
    for chunk, (m, f) in enumerate(zip(mlps, mlp_far)):
        rows = slice(chunk * half // chunks, (chunk + 1) * half // chunks)
        branch_m = m.astype(F32) + f.astype(F32) + row_vectors[5]
        outputs_own = resid[rows] + branch_m
        stat_out += jnp.sum(valid[rows] * outputs_own * outputs_own)
        stat_m += jnp.sum(valid[rows] * branch_m * branch_m)
        own_low.append(outputs_own.astype(BF))
    outputs = finish(scalars, own_low, [to_core(x) for x in own_low])

    summed = [(x[0].astype(F32) + f.astype(F32)).astype(BF) for x, f in zip(lasts, last_far)]
    input_grad = finish(scalars, summed, [to_core(x) for x in summed])

    stats = jnp.stack([stat_out, jnp.sum(sums[4]), stat_m, jnp.sum(valid)])
    small = jnp.concatenate(
        [
            last_sums[0:2],
            sums[2:3],
            sums[0:2],
            sums[3:4],
            jnp.pad(stats, (0, depth - 4))[None],
            jnp.pad(
                jnp.concatenate([part_sums[p][kind] for kind in range(2) for p in range(2)]),
                (0, depth - 2 * width),
            )[None],
            up_sums,
        ],
        axis=0,
    )
    every = lax.all_gather(small, ("dp", "mp"), axis=0, tiled=False)
    every = every.reshape(n_dp, -1, *small.shape)
    row_stat = jnp.sum(every[:, :, :7], axis=(0, 1))
    row_total, stat_total = row_stat[:6], row_stat[6]
    col_all = jnp.sum(every[:, :, 7:], axis=0)
    mine = lax.dynamic_index_in_dim(col_all, device, 0, keepdims=False)
    theirs = lax.dynamic_index_in_dim(col_all, device ^ 1, 0, keepdims=False)
    col_total = jnp.concatenate(
        [mine[0, : 2 * width].reshape(2, width), (mine[1] + theirs[2]).reshape(-1, width)], axis=0
    )
    rms_stats = jnp.sqrt(stat_total[:3] / (stat_total[3] * depth))

    qkv_new = adamw(qkv_weight, qkv_first, qkv_second, qkv_shard, matrix_rate, weight_decay)
    out_new = adamw(out_weight, out_first, out_second, out_shard, matrix_rate, weight_decay)
    up_new = adamw(up_weight, up_first, up_second, up_shard, matrix_rate, weight_decay)
    down_new = adamw(down_weight, down_first, down_second, down_shard, matrix_rate, weight_decay)
    row_new = adamw(row_vectors, row_first, row_second, row_total, vector_rate, 0.0)
    col_new = adamw(col_bias, col_first, col_second, col_total, vector_rate, 0.0)
    return (
        outputs,
        input_grad,
        rms_stats,
        *qkv_new,
        *out_new,
        *up_new,
        *down_new,
        *row_new,
        *col_new,
    )


def solution(mesh):
    matrices = [P("dp", None, "mp"), P("mp", "dp"), P("dp", None, "mp"), P(None, "mp", "dp")]
    vectors = [P(), P(None, "mp")]
    groups = [spec for spec in matrices + vectors for _ in range(3)]
    return jax.shard_map(
        body,
        mesh=mesh,
        in_specs=(P("dp", None), P("dp", None), P("dp"), *groups),
        out_specs=(P("dp", None), P("dp", None), P(), *groups),
        check_vma=False,
    )
```

```python
import functools

import jax
import jax.numpy as jnp
from jax import lax
from jax.experimental import pallas as pl
from jax.experimental.pallas import tpu as pltpu
from jax.sharding import PartitionSpec as P

HEADS = 16
HEAD_DIM = 64
STEP = 5

norm_eps = 1e-05
masked_score = -1e30
first_decay = 0.5
second_decay = 0.5
matrix_rate = 0.03
vector_rate = 0.4
weight_decay = 0.1
adam_eps = 1e-08
gelu_scale = 0.7978845608028654
gelu_cubic = 0.044715

F32 = jnp.float32
BF = jnp.bfloat16
NN = (((1,), (0,)), ((), ()))
NT = (((1,), (1,)), ((), ()))
TN = (((0,), (0,)), ((), ()))
MIB = 2**20


def dot(a, b, dims=NN):
    return lax.dot_general(a, b, dims, preferred_element_type=F32)


def adamw(weight, moment_one, moment_two, gradient, learn_rate, decay_rate):
    moment_one = first_decay * moment_one + (1.0 - first_decay) * gradient
    moment_two = second_decay * moment_two + (1.0 - second_decay) * gradient * gradient
    correct_one = 1.0 - first_decay**STEP
    correct_two = 1.0 - second_decay**STEP
    direction = moment_one / correct_one / (jnp.sqrt(moment_two / correct_two) + adam_eps)
    return (moment_one, moment_two, weight - learn_rate * (direction + decay_rate * weight))


def to_core(x):
    return lax.ppermute(x, "mp", [(i, i ^ 1) for i in range(lax.axis_size("mp"))])


def to_chip(x):
    return lax.ppermute(x, "mp", [(i, i ^ 2) for i in range(lax.axis_size("mp"))])


def to_all(x):
    return lax.all_to_all(x, "mp", split_axis=0, concat_axis=0, tiled=True)


def ring_order(n):
    return [0, 2, 4, 6, 7, 5, 3, 1] if n == 8 else list(range(n))


def ring_perms(n):
    order = ring_order(n)
    up = [(order[p], order[(p + 1) % n]) for p in range(n)]
    down = [(order[p], order[(p - 1) % n]) for p in range(n)]
    return up, down


def ring_index(n):
    order = ring_order(n)
    place = jnp.array([order.index(i) for i in range(n)], jnp.int32)[lax.axis_index("dp")]
    return jnp.array(order, jnp.int32)[(place + jnp.arange(n)) % n]


class Gather:
    def __init__(self, piece, turn=1):
        self.n = lax.axis_size("dp")
        self.perms = ring_perms(self.n)[::turn]
        self.turn = turn
        self.pieces = [piece] + [None] * (self.n - 1)
        self.up = self.down = piece
        self.done = 0

    def hop(self, *gates):
        if self.done == self.n // 2:
            return
        self.done += 1
        self.up = self.pieces[-self.turn * self.done % self.n] = lax.ppermute(after(self.up, *gates), "dp", self.perms[0])
        if self.done <= (self.n - 1) // 2:
            self.down = self.pieces[self.turn * self.done % self.n] = lax.ppermute(after(self.down, *gates), "dp", self.perms[1])

    def finish(self):
        while self.done < self.n // 2:
            self.hop()
        return self.pieces


class Reduce:
    def __init__(self, total, index, turn=1):
        self.n = lax.axis_size("dp")
        self.perms = ring_perms(self.n)[::turn]
        self.turn = turn
        self.total, self.index = total, index
        self.rows = total.shape[0] // self.n
        self.up = self.down = None
        self.done = 0

    def block(self, k):
        return lax.dynamic_slice_in_dim(self.total, self.index[self.turn * k % self.n] * self.rows, self.rows, 0)

    def add(self, x, k):
        if x is None:
            return self.block(k)
        return (x.astype(F32) + self.block(k).astype(F32)).astype(BF)

    def hop(self, *gates):
        ups, downs = self.n // 2, (self.n - 1) // 2
        if self.done == ups:
            return
        up = after(self.add(self.up, ups - self.done), *gates)
        if self.done < downs:
            down = after(self.add(self.down, self.done - downs), *gates)
            self.down = lax.ppermute(down, "dp", self.perms[1])
        self.up = lax.ppermute(up, "dp", self.perms[0])
        self.done += 1

    def finish(self):
        while self.done < self.n // 2:
            self.hop()
        return self.block(0).astype(F32) + self.up.astype(F32) + self.down.astype(F32)


def after(x, *others):
    return lax.optimization_barrier((x, *others))[0] if others else x


def cost(flops, nbytes):
    return pl.CostEstimate(flops=int(flops), bytes_accessed=int(nbytes), transcendentals=0)


def whole(shape):
    return pl.BlockSpec(shape, lambda *_: (0,) * len(shape), pipeline_mode=pl.Buffered(1))


def assemble_kernel(index_ref, pieces, out_ref, at):
    rows, cols = pieces[0].shape
    for k, piece in enumerate(pieces):
        row = pl.multiple_of(index_ref[k] * rows, rows)
        out_ref[pl.ds(row, rows), at : at + cols] = piece[...]


def split3(x):
    hi = x.astype(BF).astype(F32)
    rest = x - hi
    mid = rest.astype(BF).astype(F32)
    return hi, mid, rest - mid


def put3(base, lane, first, x):
    hi, mid, lo = split3(x)
    return jnp.where(
        lane == first,
        hi,
        jnp.where(lane == first + 1, mid, jnp.where(lane == first + 2, lo, base)),
    )


def project_kernel(index_ref, slope_ref, length_ref, n_ref, bias_ref, *refs, heads):
    *pieces, q_ref, k_ref, v_ref, w_ref = refs

    @pl.when(pl.program_id(0) == 0)
    def _():
        assemble_kernel(index_ref, pieces, w_ref, 0)

    rows = n_ref.shape[0]
    width = heads * HEAD_DIM
    out = dot(n_ref[...], w_ref[...])
    query = (out[:, :width] + bias_ref[0:1, :]).astype(BF).astype(F32) * (HEAD_DIM**-0.5)
    key = out[:, width : 2 * width]
    value = out[:, 2 * width :] + bias_ref[1:2, :]
    lane = lax.broadcasted_iota(jnp.int32, (rows, 128), 1)
    at = lax.broadcasted_iota(jnp.int32, (rows, 128), 0) + pl.program_id(0) * rows
    ones = ((lane >= 64) & (lane < 67)).astype(F32)
    more = ((lane >= 67) & (lane < 70)).astype(F32)
    seen = at < length_ref[0]
    zero = jnp.zeros((rows, 64), F32)
    for h in range(heads):
        cols = slice(h * HEAD_DIM, (h + 1) * HEAD_DIM)
        slope = jnp.where(seen, at.astype(F32) * slope_ref[h], masked_score)
        q_ref[h] = (jnp.concatenate([query[:, cols], zero], axis=1) + ones).astype(BF)
        wide = jnp.concatenate([key[:, cols], zero], axis=1) + more
        k_ref[h] = put3(wide, lane, 64, slope).astype(BF)
        v_ref[h] = (jnp.concatenate([value[:, cols], zero], axis=1) + ones).astype(BF)


def project(normed, index, pieces, col_bias, slopes, length):
    span, depth = normed.shape
    cols = pieces[0].shape[1]
    heads = slopes.shape[0]
    tile = 256
    shape = jax.ShapeDtypeStruct((heads, span, 128), BF)
    return pl.pallas_call(
        functools.partial(project_kernel, heads=heads),
        out_shape=(shape,) * 3 + (jax.ShapeDtypeStruct((depth, cols), BF),),
        grid=(span // tile,),
        in_specs=[pl.BlockSpec(memory_space=pltpu.SMEM)] * 3
        + [pl.BlockSpec((tile, depth), lambda i: (i, 0)), whole(col_bias.shape)]
        + [whole(piece.shape) for piece in pieces],
        out_specs=[pl.BlockSpec((heads, tile, 128), lambda i: (0, i, 0))] * 3
        + [whole((depth, cols))],
        compiler_params=pltpu.CompilerParams(vmem_limit_bytes=40 * MIB),
        cost_estimate=cost(2 * span * depth * cols, 12 * MIB),
        name="project",
    )(index, slopes, length, normed, col_bias, *pieces)


def attend_forward_kernel(q_ref, k_ref, v_ref, o_ref, qb_ref, send_ref, *, bq, span):
    lane = lax.broadcasted_iota(jnp.int32, (bq, 128), 1)
    row = lax.broadcasted_iota(jnp.int32, (bq, bq), 0)
    causal = row >= lax.broadcasted_iota(jnp.int32, (bq, bq), 1)
    for i in range(span // bq):
        outs = []
        here = pl.ds(i * bq, bq)
        for h in range(2):
            q = q_ref[h, here, :]
            near = jnp.where(causal, dot(q, k_ref[h, here, :], NT), masked_score)
            highest = jnp.max(near, axis=1, keepdims=True)
            if i:
                before = pl.ds(0, i * bq)
                far = dot(q, k_ref[h, before, :], NT)
                highest = jnp.maximum(highest, jnp.max(far, axis=1, keepdims=True))
            acc = dot(jnp.exp(near - highest).astype(BF), v_ref[h, here, :])
            if i:
                acc = acc + dot(jnp.exp(far - highest).astype(BF), v_ref[h, before, :])
            total = acc[:, 64:65]
            outs.append((acc[:, :64] * (1.0 / total)).astype(BF))
            log_sum = highest + jnp.log(total)
            qb_ref[h, here, :] = put3(q.astype(F32), lane, 67, -log_sum).astype(BF)
        o_ref[here, :] = jnp.concatenate(outs, axis=1)
    half = span // 2
    for j in range(4):
        send_ref[j] = o_ref[pl.ds(j % 2 * half, half), :]


def pair_spec(span, pair):
    return pl.BlockSpec((2, span, 128), lambda i: (pair, 0, 0), pipeline_mode=pl.Buffered(1))


def attend_forward(q, k, v, pair):
    span = q.shape[1]
    shapes = [(span, 128), (2, span, 128), (4, span // 2, 128)]
    return pl.pallas_call(
        functools.partial(attend_forward_kernel, bq=min(512, span), span=span),
        out_shape=[jax.ShapeDtypeStruct(x, BF) for x in shapes],
        grid=(1,),
        in_specs=[pair_spec(span, pair)] * 3,
        out_specs=[whole(x) for x in shapes],
        compiler_params=pltpu.CompilerParams(vmem_limit_bytes=50 * MIB),
        cost_estimate=cost(12e9, 5 * MIB),
        name="attend_forward",
    )(q, k, v)


def attend_backward_kernel(half_ref, q_ref, k_ref, v_ref, o_ref, *refs, bk, span, chunks):
    partials, (d_ref, sib_ref, sum_ref, do_ref, doa_ref, dq_ref) = refs[:-6], refs[-6:]
    half = span // 2
    rows = half // chunks
    for c, part in enumerate(partials):
        for side in range(2):
            total = part[side].astype(F32) + part[2 + side].astype(F32)
            do_ref[pl.ds(side * half + c * rows, rows), :] = total.astype(BF)
    lane = lax.broadcasted_iota(jnp.int32, (span, 128), 1)
    row = lax.broadcasted_iota(jnp.int32, (bk, bk), 0)
    causal = row <= lax.broadcasted_iota(jnp.int32, (bk, bk), 1)
    grad = do_ref[...].astype(F32)
    prod = grad * o_ref[...].astype(F32)
    for h in range(2):
        cols = slice(h * HEAD_DIM, (h + 1) * HEAD_DIM)
        delta = jnp.sum(prod[:, cols], axis=1, keepdims=True)
        base = jnp.concatenate([grad[:, cols], jnp.zeros((span, 64), F32)], axis=1)
        doa_ref[h] = put3(base, lane, 64, -delta).astype(BF)
    dq_ref[...] = jnp.zeros_like(dq_ref)
    value_sums = jnp.zeros((1, 128), F32)
    for j in range(span // bk):
        dks, dvs = [], []
        here = pl.ds(j * bk, bk)
        rest = pl.ds(j * bk, span - j * bk)
        for h in range(2):
            k = k_ref[h, here, :]
            q = q_ref[h, rest, :]
            do = doa_ref[h, rest, :]
            p = jnp.exp(dot(k, q, NT))
            near = jnp.where(causal, p[:, :bk], 0.0)
            p = jnp.concatenate([near, p[:, bk:]], axis=1) if rest.size > bk else near
            ds = (p * dot(v_ref[h, here, :], do, NT)).astype(BF)
            dvs.append(dot(p.astype(BF), do)[:, :64])
            dks.append(dot(ds, q)[:, :64])
            dq_ref[h, :, rest] += dot(k[:, :64], ds, TN)
        d_ref[1, here, :] = jnp.concatenate(dks, axis=1).astype(BF)
        value_grad = jnp.concatenate(dvs, axis=1).astype(BF)
        d_ref[2, here, :] = value_grad
        value_sums += jnp.sum(value_grad.astype(F32), axis=0, keepdims=True)
    dq = jnp.concatenate([dq_ref[0], dq_ref[1]], axis=0).T * (HEAD_DIM**-0.5)
    dq = dq.astype(BF)
    d_ref[0] = dq
    sum_ref[0:1, :] = jnp.sum(dq.astype(F32), axis=0, keepdims=True)
    sum_ref[1:2, :] = value_sums
    for kind in range(3):
        sib_ref[kind] = d_ref[kind, pl.ds(pl.multiple_of((1 - half_ref[0]) * half, half), half), :]


def attend_backward(scalars, qb, k, v, o, partials, pair):
    span = qb.shape[1]
    chunks = len(partials)
    part = pl.BlockSpec((4, span // 2 // chunks, 128), lambda i: (0, 0, pair), pipeline_mode=pl.Buffered(1))
    shapes = [((3, span, 128), BF), ((3, span // 2, 128), BF), ((2, 128), F32)]
    return pl.pallas_call(
        functools.partial(attend_backward_kernel, bk=min(256, span), span=span, chunks=chunks),
        out_shape=[jax.ShapeDtypeStruct(*x) for x in shapes],
        grid=(1,),
        in_specs=[
            pl.BlockSpec(memory_space=pltpu.SMEM),
            pair_spec(span, 0),
            pair_spec(span, pair),
            pair_spec(span, pair),
            whole((span, 128)),
        ]
        + [part] * chunks,
        out_specs=[whole(x[0]) for x in shapes],
        scratch_shapes=[
            pltpu.VMEM((span, 128), BF),
            pltpu.VMEM((2, span, 128), BF),
            pltpu.VMEM((2, 64, span), F32),
        ],
        compiler_params=pltpu.CompilerParams(vmem_limit_bytes=50 * MIB),
        cost_estimate=cost(18e9, 6 * MIB),
        name="attend_backward",
    )(scalars, qb, k, v, o, *partials)


def norm_parts(x):
    average = jnp.mean(x, axis=-1, keepdims=True)
    centred = x - average
    variance = jnp.mean(centred * centred, axis=-1, keepdims=True)
    scale = lax.rsqrt(variance + norm_eps)
    return centred * scale, scale


def norm_back(grad, unit, scale, gain):
    weighted = grad * gain
    mean_one = jnp.mean(weighted, axis=-1, keepdims=True)
    mean_two = jnp.mean(weighted * unit, axis=-1, keepdims=True)
    return scale * (weighted - mean_one - unit * mean_two)


def middle_kernel(
    scalar_ref,
    o0_ref,
    o1_ref,
    tokens_ref,
    cot_ref,
    late_own_ref,
    late_sib_ref,
    row_ref,
    bias_ref,
    *refs,
    chunk,
):
    (*mlp_refs, resid_ref, send_ref, g_ref, du_ref, da_ref, do_ref, sum_ref, up_sum_ref, out_w) = refs
    step = pl.program_id(0)
    tile, depth = tokens_ref.shape

    @pl.when(step == 0)
    def _():
        for k, ref in enumerate((late_own_ref, late_sib_ref)):
            for chip in range(2):
                for pair in range(2):
                    at = (pair * 4 + (scalar_ref[3] ^ (k + 2 * chip))) * 128
                    cols = slice(256 * chip + 128 * pair, 256 * chip + 128 * (pair + 1))
                    out_w[:, pl.ds(pl.multiple_of(at, 128), 128)] = ref[:, cols]
        sum_ref[...] = jnp.zeros_like(sum_ref)
        up_sum_ref[...] = jnp.zeros_like(up_sum_ref)

    heads = jnp.concatenate([ref[j] for ref in (o0_ref, o1_ref) for j in range(4)], axis=1)
    branch = dot(heads, out_w[...], NT) + row_ref[2:3, :]
    resid = tokens_ref[...].astype(F32) + branch
    resid_ref[...] = resid.astype(BF)
    at = lax.broadcasted_iota(jnp.int32, (tile, 1), 0) + (
        scalar_ref[0] * scalar_ref[1] + (chunk * pl.num_programs(0) + step) * tile
    )
    valid = (at < scalar_ref[2]).astype(F32)
    unit, scale = norm_parts(resid)
    n2 = (unit * row_ref[3:4, :] + row_ref[4:5, :]).astype(BF)
    send_ref[:, :depth] = n2
    cot = cot_ref[...]
    dm = cot.astype(BF)
    mlp = None
    hid = (late_own_ref.shape[1] - 512) // 2
    for half, late in enumerate((late_own_ref, late_sib_ref)):
        up, down = late.at[:, 512 : 512 + hid], late.at[:, 512 + hid :]
        u = dot(n2, up[...]) + bias_ref[half : half + 1, :]
        square = u * u
        t = jnp.tanh(gelu_scale * (u + gelu_cubic * square * u))
        plus = 0.5 * (1.0 + t)
        g = (u * plus).astype(BF)
        slope = plus + (0.5 * gelu_scale) * u * (1.0 - t * t) * (1.0 + 3.0 * gelu_cubic * square)
        du_wide = (dot(dm, down[...]) * slope).astype(BF)
        if half == 0:
            g_ref[...] = g
            du_ref[...] = du_wide
        else:
            send_ref[:, depth : depth + hid] = g
            send_ref[:, depth + hid :] = du_wide
        up_sum_ref[half : half + 1, :] += jnp.sum(du_wide.astype(F32), axis=0, keepdims=True)
        m = dot(g, down[...], NT)
        d = dot(du_wide, up[...], NT)
        mlp, dn2 = (m, d) if mlp is None else (mlp + m, dn2 + d)
    mlp = mlp.astype(BF)
    start = 0
    for ref in mlp_refs:
        stop = start + ref.shape[0]
        for k in range(start // tile, (stop - 1) // tile + 1):
            low, high = max(start, k * tile), min(stop, (k + 1) * tile)

            @pl.when(step == k)
            def _(ref=ref, at=low - start, low=low - k * tile, size=high - low):
                ref[at : at + size, :] = mlp[low : low + size, :]

        start = stop
    dr = norm_back(dn2, unit, scale, row_ref[3:4, :]) + 0.5 * cot
    da = dr.astype(BF)
    da_ref[...] = da
    do = dot(da, out_w[...]).astype(BF)
    for j in range(4):
        do_ref[j] = jnp.concatenate([do[:, 128 * (j + 4 * p) : 128 * (j + 4 * p + 1)] for p in range(2)], axis=1)
    for k, x in enumerate(
        (dn2 * unit, dn2, da.astype(F32), 0.5 * dm.astype(F32), valid * branch * branch)
    ):
        sum_ref[k : k + 1, :] += jnp.sum(x, axis=0, keepdims=True)


def middle(scalars, heads_in, tokens, cotangent, weights, row_vectors, up_bias, pieces):
    depth = tokens.shape[1]
    half = tokens.shape[0] // 2
    tile = 256
    chunk, chunks = 0, 1
    steps = half // tile
    hidden = weights[0].shape[1] - 512
    own = lambda i, s: (chunk * steps + i, 0)
    absolute = lambda i, s: (s[0] * (half // tile) + chunk * steps + i, 0)
    part = lambda i, s: (i, 0)
    parts = [(depth, BF), (depth + hidden, BF), (hidden // 2, BF), (hidden // 2, BF), (depth, BF)]
    return pl.pallas_call(
        functools.partial(middle_kernel, chunk=chunk),
        out_shape=[jax.ShapeDtypeStruct((rows, depth), BF) for rows in pieces]
        + [jax.ShapeDtypeStruct((half // chunks, w), t) for w, t in parts]
        + [jax.ShapeDtypeStruct((4, half // chunks, 256), BF)]
        + [jax.ShapeDtypeStruct((8, depth), F32), jax.ShapeDtypeStruct((2, hidden // 2), F32)],
        grid_spec=pltpu.PrefetchScalarGridSpec(
            num_scalar_prefetch=1,
            grid=(steps,),
            in_specs=[pl.BlockSpec((4, tile, 128), lambda i, s: (0, *own(i, s)))] * 2
            + [pl.BlockSpec((tile, depth), absolute)] * 2
            + [whole(w.shape) for w in weights]
            + [whole(row_vectors.shape), whole(up_bias.shape)],
            out_specs=[whole((rows, depth)) for rows in pieces]
            + [pl.BlockSpec((tile, w), part) for w, _ in parts]
            + [pl.BlockSpec((4, tile, 256), lambda i, s: (0, i, 0))]
            + [whole((8, depth)), whole((2, hidden // 2))],
            scratch_shapes=[
                pltpu.VMEM((depth, 1024), BF),
            ],
        ),
        compiler_params=pltpu.CompilerParams(vmem_limit_bytes=56 * MIB),
        cost_estimate=cost(21e9 / chunks, 24 * MIB),
        name="middle",
    )(scalars, *heads_in, tokens, cotangent, *weights, row_vectors, up_bias)


def last_kernel(
    scalar_ref, o0_ref, o1_ref, s0_ref, s1_ref, w_own_ref, w_sib_ref, tokens_ref, *refs
):
    da_ref, row_ref, *ig_refs, sum_ref = refs
    step = pl.program_id(0)

    @pl.when(step == 0)
    def _():
        sum_ref[...] = jnp.zeros_like(sum_ref)

    def side(x, y):
        return jnp.concatenate([r[k] for k in range(3) for r in (x, y)], axis=1)

    dn1 = dot(side(o0_ref, o1_ref), w_own_ref[...], NT) + dot(side(s0_ref, s1_ref), w_sib_ref[...], NT)
    unit, scale = norm_parts(tokens_ref[...].astype(F32))
    ig = (da_ref[...].astype(F32) + norm_back(dn1, unit, scale, row_ref[0:1, :])).astype(BF)
    for k, ref in enumerate(ig_refs):

        @pl.when(step == k)
        def _(ref=ref):
            ref[...] = ig

    sum_ref[0:1, :] += jnp.sum(dn1 * unit, axis=0, keepdims=True)
    sum_ref[1:2, :] += jnp.sum(dn1, axis=0, keepdims=True)


def last(scalars, own, sibling, w_own, w_sib, tokens, da, row_vectors):
    depth = tokens.shape[1]
    half = tokens.shape[0] // 2
    steps = 4
    tile = half // steps
    absolute = lambda i, s: (s[0] * steps + i, 0)
    return pl.pallas_call(
        last_kernel,
        out_shape=[jax.ShapeDtypeStruct((tile, depth), BF)] * steps + [jax.ShapeDtypeStruct((8, depth), F32)],
        grid_spec=pltpu.PrefetchScalarGridSpec(
            num_scalar_prefetch=1,
            grid=(steps,),
            in_specs=[pl.BlockSpec((3, tile, 128), lambda i, s: (0, *absolute(i, s)))] * 2
            + [pl.BlockSpec((3, tile, 128), lambda i, s: (0, i, 0))] * 2
            + [whole(w_own.shape), whole(w_sib.shape), pl.BlockSpec((tile, depth), absolute)]
            + [pl.BlockSpec((tile, depth), lambda i, s: (i, 0))]
            + [whole(row_vectors.shape)],
            out_specs=[
                *[whole((tile, depth))] * steps,
                whole((8, depth)),
            ],
        ),
        compiler_params=pltpu.CompilerParams(vmem_limit_bytes=40 * MIB),
        cost_estimate=cost(3.2e9, 20 * MIB),
        name="last",
    )(scalars, *own, *sibling, w_own, w_sib, tokens, da, row_vectors)


def out_grads_kernel(*refs, chunks):
    das, heads, out_ref = refs[1 : 1 + chunks], refs[1 + chunks : -1], refs[-1]
    out_ref[...] = sum_over_chunks(das, heads).astype(BF)


def sum_over_chunks(das, heads):
    rows = das[0].shape[0]
    total = 0.0
    for c, da in enumerate(das):
        right = jnp.concatenate([h[0, c * rows : (c + 1) * rows, :] for h in heads], axis=1)
        total = total + dot(da[...], right, TN)
    return total


def head_specs(half, side):
    return [
        pl.BlockSpec((1, half, 128), lambda i, s, flip=flip: (s[3] ^ flip, 0, 0), pipeline_mode=pl.Buffered(1))
        for flip in (side, side, side + 2, side + 2)
    ]


def out_grads(scalars, das, heads_in):
    rows, depth = das[0].shape
    tile = 256
    return pl.pallas_call(
        functools.partial(out_grads_kernel, chunks=len(das)),
        out_shape=jax.ShapeDtypeStruct((depth, 512), BF),
        grid_spec=pltpu.PrefetchScalarGridSpec(
            num_scalar_prefetch=1,
            grid=(depth // tile,),
            in_specs=[pl.BlockSpec((rows, tile), lambda i, s: (0, i))] * len(das)
            + head_specs(rows * len(das), 1),
            out_specs=pl.BlockSpec((tile, 512), lambda i, s: (i, 0)),
        ),
        compiler_params=pltpu.CompilerParams(vmem_limit_bytes=24 * MIB),
        name="out_grads",
    )(scalars, *das, *heads_in, *heads_in)


def weight_grads_kernel(scalar_ref, cot_ref, *refs, chunks):
    *refs, out_ref = refs
    groups = [refs[3 * k : 3 * k + 3] for k in range(2 * chunks)]
    das, heads, got_ref = refs[6 * chunks : 7 * chunks], refs[7 * chunks : -1], refs[-1]
    rows = groups[0][0].shape[0]
    up = down = 0.0
    for k, (n2, g, du) in enumerate(groups):
        side = scalar_ref[0] if k < chunks else 1 - scalar_ref[0]
        at = pl.multiple_of((side * chunks + k % chunks) * rows, rows)
        up = up + dot(n2[...], du[...], TN)
        down = down + dot(cot_ref[pl.ds(at, rows), :].astype(BF), g[...], TN)
    hidden = up.shape[1]
    out_ref[:, :hidden] = up.astype(BF)
    out_ref[:, hidden : 2 * hidden] = down.astype(BF)
    out_ref[:, 2 * hidden :] = (sum_over_chunks(das, heads) + got_ref[...].astype(F32)).astype(BF)


def weight_grads(scalars, cotangent, own, got, das, heads_in, got_out):
    span, depth = cotangent.shape
    chunks = len(own)
    rows, hidden = own[0][1].shape
    tile = 256
    block = lambda r, at: pl.BlockSpec((r, tile), lambda i, s: (0, i))
    fixed = lambda at: pl.BlockSpec((rows, hidden), lambda i, s: (0, at), pipeline_mode=pl.Buffered(1))
    at = depth // hidden
    specs = ([block(rows, 0), fixed(0), fixed(0)] * chunks) + ([block(rows, 0), fixed(at), fixed(at + 1)] * chunks)
    return pl.pallas_call(
        functools.partial(weight_grads_kernel, chunks=chunks),
        out_shape=jax.ShapeDtypeStruct((depth, 2 * hidden + 512), BF),
        grid_spec=pltpu.PrefetchScalarGridSpec(
            num_scalar_prefetch=1,
            grid=(depth // tile,),
            in_specs=[block(span, 0)]
            + specs
            + [block(rows, 0)] * chunks
            + head_specs(rows * chunks, 0)
            + [pl.BlockSpec((tile, 512), lambda i, s: (i, 0))],
            out_specs=pl.BlockSpec((tile, 2 * hidden + 512), lambda i, s: (i, 0)),
        ),
        compiler_params=pltpu.CompilerParams(vmem_limit_bytes=50 * MIB),
        cost_estimate=cost(2 * span * depth * (2 * hidden + 256), 30 * MIB),
        name="weight_grads",
    )(
        scalars,
        cotangent,
        *[x for group in own for x in group],
        *[x for group in got for x in (group,) * 3],
        *das,
        *heads_in,
        *heads_in,
        got_out,
    )


def qkv_grads_kernel(n_ref, p0_ref, p1_ref, out_ref):
    right = jnp.concatenate([p[k] for k in range(3) for p in (p0_ref, p1_ref)], axis=1)
    out_ref[...] = dot(n_ref[...], right, TN).astype(BF)


def qkv_grads(normed, parts):
    span, depth = normed.shape
    tile = 256
    return pl.pallas_call(
        qkv_grads_kernel,
        out_shape=jax.ShapeDtypeStruct((depth, 768), BF),
        grid=(depth // tile,),
        in_specs=[pl.BlockSpec((span, tile), lambda i: (0, i))] + [whole(p.shape) for p in parts],
        out_specs=pl.BlockSpec((tile, 768), lambda i: (i, 0)),
        compiler_params=pltpu.CompilerParams(vmem_limit_bytes=32 * MIB),
        cost_estimate=cost(2 * span * depth * 768, 10 * MIB),
        name="qkv_grads",
    )(normed, *parts)


def finish_kernel(scalar_ref, *refs, terms):
    total = refs[0][...].astype(F32)
    for ref in refs[1:terms]:
        total = total + ref[...].astype(F32)
    refs[-1][...] = total


def finish(scalars, side, terms, before=(), piece=0, pieces=1):
    rows, depth = terms[0].shape
    tile = 256
    steps = rows // tile
    out = pl.pallas_call(
        functools.partial(finish_kernel, terms=len(terms)),
        out_shape=[jax.ShapeDtypeStruct((2 * pieces * rows, depth), F32)],
        grid_spec=pltpu.PrefetchScalarGridSpec(
            num_scalar_prefetch=1,
            grid=(steps,),
            in_specs=[pl.BlockSpec((tile, depth), lambda i, s: (i, 0))] * len(terms)
            + [pl.BlockSpec(memory_space=pl.ANY)] * len(before),
            out_specs=[pl.BlockSpec((tile, depth), lambda i, s: (((s[0] ^ side) * pieces + piece) * steps + i, 0))],
        ),
        input_output_aliases={1 + len(terms): 0} if before else {},
        compiler_params=pltpu.CompilerParams(vmem_limit_bytes=24 * MIB),
        cost_estimate=cost(0, 8 * rows * depth),
        name="finish",
    )(scalars, *terms, *before)
    return out[0]


def adam_rows_kernel(g_ref, w_ref, m_ref, v_ref, nm_ref, nv_ref, nw_ref):
    kinds, width = w_ref.shape[1:]
    for k in range(kinds):
        grad = g_ref[:, k * width : (k + 1) * width]
        new = adamw(w_ref[:, k, :], m_ref[:, k, :], v_ref[:, k, :], grad, matrix_rate, weight_decay)
        nm_ref[:, k, :], nv_ref[:, k, :], nw_ref[:, k, :] = new


def adam_turned_kernel(g_ref, w_ref, m_ref, v_ref, nm_ref, nv_ref, nw_ref):
    new = adamw(w_ref[...], m_ref[...], v_ref[...], g_ref[...].T, matrix_rate, weight_decay)
    nm_ref[...], nv_ref[...], nw_ref[...] = new


def adam(kernel, grad, *state):
    return pl.pallas_call(
        kernel,
        out_shape=[jax.ShapeDtypeStruct(state[0].shape, F32)] * 3,
        grid=(1,),
        in_specs=[whole(x.shape) for x in (grad, *state)],
        out_specs=[whole(state[0].shape)] * 3,
        compiler_params=pltpu.CompilerParams(vmem_limit_bytes=24 * MIB),
        cost_estimate=cost(0, 28 * grad.size),
        name="adam",
    )(grad, *state)


def adam_turned(grad, *state):
    if grad.shape[0] % 128:
        return adamw(*state, grad.T.reshape(state[0].shape), matrix_rate, weight_decay)
    flat = [x.reshape(-1, x.shape[-1]) for x in state]
    return [x.reshape(state[0].shape) for x in adam(adam_turned_kernel, grad, *flat)]


def body(
    tokens,
    cotangent,
    lengths,
    qkv_weight,
    qkv_first,
    qkv_second,
    out_weight,
    out_first,
    out_second,
    up_weight,
    up_first,
    up_second,
    down_weight,
    down_first,
    down_second,
    row_vectors,
    row_first,
    row_second,
    col_bias,
    col_first,
    col_second,
):
    span, depth = tokens.shape
    half = span // 2
    share = qkv_weight.shape[0]
    n_dp = lax.axis_size("dp")
    device = lax.axis_index("mp")
    core = device % 2
    heads = qkv_weight.shape[2] // HEAD_DIM
    width = heads * HEAD_DIM
    hidden = up_weight.shape[1] * up_weight.shape[2]
    head_ids = device * heads + jnp.arange(heads)
    slopes = jnp.exp2(-8.0 * (head_ids.astype(F32) + 1.0) / HEADS)
    scalars = jnp.stack([core.astype(jnp.int32), jnp.int32(half), lengths[0], device.astype(jnp.int32)])

    index = ring_index(n_dp)
    out_piece = out_weight.astype(BF).T
    out_piece = jnp.concatenate([out_piece, to_chip(out_piece)], axis=1)
    qkv_ring = Gather(qkv_weight.astype(BF).reshape(share, 3 * width))
    up_piece = up_weight.astype(BF).reshape(share, hidden)
    down_piece = down_weight.astype(BF).reshape(hidden, share).T
    late_piece = jnp.concatenate([out_piece, up_piece, down_piece], axis=1)
    late_w = lax.all_gather(late_piece, "dp", axis=0, tiled=True)
    up_bias = col_bias[2:].reshape(1, hidden)
    up_bias = jnp.concatenate([up_bias, to_core(up_bias)], axis=0)
    for _ in range(n_dp // 2):
        qkv_ring.hop()

    unit_one, _ = norm_parts(tokens.astype(F32))
    normed = (unit_one * row_vectors[0] + row_vectors[1]).astype(BF)
    q, k, v, qkv_w = project(after(normed, up_bias), index, qkv_ring.finish(), col_bias, slopes, lengths)
    outs, heads_in = [], []
    for pair in range(2):
        o, qb, send = attend_forward(q, k, v, pair)
        outs.append((o, qb))
        heads_in.append(to_all(after(send, *heads_in)))
    qkv_sib = to_core(qkv_w)
    late_w = after(late_w, heads_in[1])
    late_sib = to_core(late_w)

    weights = (late_w, after(late_sib, qkv_sib))
    chunks = 1
    pieces = [half * 3 // 8, half * 3 // 8, half // 4]
    *mlps, resid, send, g, du, da, do, sums, up_sums = middle(
        scalars, heads_in, tokens, cotangent, weights, row_vectors, up_bias, pieces
    )
    resids, das = [resid], [da]
    got_send = to_core(send)
    got_out = to_core(out_grads(scalars, das, heads_in))
    partials = [to_all(do)]
    total = weight_grads(scalars, cotangent, [(send, g, du)], [got_send], das, heads_in, got_out)
    total = after(total, *partials)
    mlp_far = [to_chip(after(mlps[0], total))]
    shard = lax.psum_scatter(total, "dp", scatter_dimension=0, tiled=True)

    parts, part_sums, siblings = [], [], []
    for pair in range(2):
        o, qb = outs[pair]
        qb = after(qb, total)
        d, d_sib, s = attend_backward(scalars, qb, k, v, o, partials, pair)
        parts.append(d)
        part_sums.append(s)
        d_sib = after(d_sib, mlp_far[pair])
        if pair == 0:
            outs[1] = (outs[1][0], after(outs[1][1], mlp_far[0], s))
        mlp_far.append(to_chip(after(mlps[pair + 1], mlp_far[pair])))
        siblings.append(to_core(d_sib))
    *igs, last_sums = last(scalars, parts, siblings, qkv_w, qkv_sib, tokens, das[0], row_vectors)
    igs[0] = after(igs[0], mlp_far[2])
    ig_far = [to_chip(igs[0])]

    qkv_wgrad = after(qkv_grads(after(normed, last_sums), parts), ig_far[0])
    ig_sib = [to_core(after(x, qkv_wgrad)) for x in igs]
    qkv_ring = Reduce(qkv_wgrad, index, -1)
    for hop in range(4):
        qkv_ring.hop(*ig_far[hop : hop + 1][: 3 - hop])
        if hop < 3:
            ig_far.append(to_chip(after(igs[hop + 1], ig_far[hop])))
    qkv_shard = qkv_ring.finish()
    up_shard = shard[:, :hidden].astype(F32)
    down_shard = shard[:, hidden : 2 * hidden].astype(F32)
    out_mine = shard[:, 2 * hidden : 2 * hidden + width]
    out_theirs = to_chip(shard[:, 2 * hidden + width :])
    out_shard = out_mine.astype(F32) + out_theirs.astype(F32)

    valid = ((core * half + jnp.arange(half)) < lengths[0]).astype(F32)[:, None]
    stat_out, stat_m, own_low = 0.0, 0.0, []
    at = 0
    for m, f in zip(mlps, mlp_far):
        rows = slice(at, at + m.shape[0])
        at += m.shape[0]
        branch_m = m.astype(F32) + after(f, qkv_wgrad).astype(F32) + row_vectors[5]
        outputs_own = resid[rows].astype(F32) + branch_m
        stat_out += jnp.sum(valid[rows] * outputs_own * outputs_own)
        stat_m += jnp.sum(valid[rows] * branch_m * branch_m)
        own_low.append(after(outputs_own.astype(BF), ig_far[1]))
    own_low = jnp.concatenate(own_low, axis=0)
    outputs = after(finish(scalars, 0, [own_low]), ig_far[2])
    outputs = finish(scalars, 1, [to_core(own_low)], (outputs,))
    stat_out, stat_m = after(stat_out, ig_far[1]), after(stat_m, ig_far[1])
    qkv_new = adam(adam_rows_kernel, qkv_shard, qkv_weight, qkv_first, qkv_second)
    out_new = adam_turned(out_shard, out_weight, out_first, out_second)
    up_new = adam(adam_rows_kernel, up_shard, up_weight, up_first, up_second)
    down_new = adam_turned(down_shard, down_weight, down_first, down_second)
    input_grad = ()
    for k in range(4):
        if k == 2:
            input_grad = (after(input_grad[0], ig_far[3]),)
            ig_far[3] = after(ig_far[3], up_new[0], down_new[0], outputs)
        input_grad = (finish(scalars, 0, [igs[k], ig_far[k]], input_grad, k, 4),)
        input_grad = (finish(scalars, 1, [ig_sib[k], to_core(ig_far[k])], input_grad, k, 4),)
    input_grad = input_grad[0]

    stats = jnp.stack([stat_out, jnp.sum(sums[4]), stat_m, jnp.sum(valid)])
    small = jnp.concatenate(
        [
            last_sums[0:2],
            sums[2:3],
            sums[0:2],
            sums[3:4],
            jnp.pad(stats, (0, depth - 4))[None],
            jnp.pad(
                jnp.concatenate([part_sums[p][kind] for kind in range(2) for p in range(2)]),
                (0, depth - 2 * width),
            )[None],
            up_sums,
        ],
        axis=0,
    )
    rows, columns = small[:7], small[7:9]
    other = to_core(small)
    rows = rows + other[:7]
    columns = jnp.concatenate([columns[:1], columns[1:] + other[9:]], axis=0)
    small = jnp.concatenate([rows, columns], axis=0)
    step = 1
    while step < n_dp:
        small = small + lax.ppermute(small, "dp", [(i, i ^ step) for i in range(n_dp)])
        step *= 2
    rows = small[:7] + to_chip(after(small[:7], ig_far[3]))
    small = jnp.concatenate([rows, small[7:]], axis=0)
    row_total, stat_total = small[:6], small[6]
    col_total = jnp.concatenate(
        [small[7, : 2 * width].reshape(2, width), small[8].reshape(-1, width)], axis=0
    )
    rms_stats = jnp.sqrt(stat_total[:3] / (stat_total[3] * depth))

    row_new = adamw(row_vectors, row_first, row_second, row_total, vector_rate, 0.0)
    col_new = adamw(col_bias, col_first, col_second, col_total, vector_rate, 0.0)
    return (
        outputs,
        input_grad,
        rms_stats,
        *qkv_new,
        *out_new,
        *up_new,
        *down_new,
        *row_new,
        *col_new,
    )


def solution(mesh):
    matrices = [P("dp", None, "mp"), P("mp", "dp"), P("dp", None, "mp"), P(None, "mp", "dp")]
    vectors = [P(), P(None, "mp")]
    groups = [spec for spec in matrices + vectors for _ in range(3)]
    return jax.shard_map(
        body,
        mesh=mesh,
        in_specs=(P("dp", None), P("dp", None), P("dp"), *groups),
        out_specs=(P("dp", None), P("dp", None), P(), *groups),
        check_vma=False,
    )
```

```python
import functools

import jax
import jax.numpy as jnp
from jax import lax
from jax.experimental import pallas as pl
from jax.experimental.pallas import tpu as pltpu
from jax.sharding import PartitionSpec as P

HEADS = 16
HEAD_DIM = 64
STEP = 5

norm_eps = 1e-05
masked_score = -1e30
first_decay = 0.5
second_decay = 0.5
matrix_rate = 0.03
vector_rate = 0.4
weight_decay = 0.1
adam_eps = 1e-08
gelu_scale = 0.7978845608028654
gelu_cubic = 0.044715

F32 = jnp.float32
BF = jnp.bfloat16
NN = (((1,), (0,)), ((), ()))
NT = (((1,), (1,)), ((), ()))
TN = (((0,), (0,)), ((), ()))
MIB = 2**20


def dot(a, b, dims=NN):
    return lax.dot_general(a, b, dims, preferred_element_type=F32)


def adamw(weight, moment_one, moment_two, gradient, learn_rate, decay_rate):
    moment_one = first_decay * moment_one + (1.0 - first_decay) * gradient
    moment_two = second_decay * moment_two + (1.0 - second_decay) * gradient * gradient
    correct_one = 1.0 - first_decay**STEP
    correct_two = 1.0 - second_decay**STEP
    direction = moment_one / correct_one / (jnp.sqrt(moment_two / correct_two) + adam_eps)
    return (moment_one, moment_two, weight - learn_rate * (direction + decay_rate * weight))


def to_core(x):
    return lax.ppermute(x, "mp", [(i, i ^ 1) for i in range(lax.axis_size("mp"))])


def to_chip(x):
    return lax.ppermute(x, "mp", [(i, i ^ 2) for i in range(lax.axis_size("mp"))])


def to_all(x):
    return lax.all_to_all(x, "mp", split_axis=0, concat_axis=0, tiled=True)


def ring_order(n):
    return [0, 2, 4, 6, 7, 5, 3, 1] if n == 8 else list(range(n))


def ring_perms(n):
    order = ring_order(n)
    up = [(order[p], order[(p + 1) % n]) for p in range(n)]
    down = [(order[p], order[(p - 1) % n]) for p in range(n)]
    return up, down


def ring_index(n):
    order = ring_order(n)
    place = jnp.array([order.index(i) for i in range(n)], jnp.int32)[lax.axis_index("dp")]
    return jnp.array(order, jnp.int32)[(place + jnp.arange(n)) % n]


class Gather:
    def __init__(self, piece, turn=1):
        self.n = lax.axis_size("dp")
        self.perms = ring_perms(self.n)[::turn]
        self.turn = turn
        self.pieces = [piece] + [None] * (self.n - 1)
        self.up = self.down = piece
        self.done = 0

    def hop(self, *gates):
        if self.done == self.n // 2:
            return
        self.done += 1
        self.up = self.pieces[-self.turn * self.done % self.n] = lax.ppermute(after(self.up, *gates), "dp", self.perms[0])
        if self.done <= (self.n - 1) // 2:
            self.down = self.pieces[self.turn * self.done % self.n] = lax.ppermute(after(self.down, *gates), "dp", self.perms[1])

    def finish(self):
        while self.done < self.n // 2:
            self.hop()
        return self.pieces


class Reduce:
    def __init__(self, total, index, turn=1):
        self.n = lax.axis_size("dp")
        self.perms = ring_perms(self.n)[::turn]
        self.turn = turn
        self.total, self.index = total, index
        self.rows = total.shape[0] // self.n
        self.up = self.down = None
        self.done = 0

    def block(self, k):
        return lax.dynamic_slice_in_dim(self.total, self.index[self.turn * k % self.n] * self.rows, self.rows, 0)

    def add(self, x, k):
        if x is None:
            return self.block(k)
        return (x.astype(F32) + self.block(k).astype(F32)).astype(BF)

    def hop(self, *gates):
        ups, downs = self.n // 2, (self.n - 1) // 2
        if self.done == ups:
            return
        up = after(self.add(self.up, ups - self.done), *gates)
        if self.done < downs:
            down = after(self.add(self.down, self.done - downs), *gates)
            self.down = lax.ppermute(down, "dp", self.perms[1])
        self.up = lax.ppermute(up, "dp", self.perms[0])
        self.done += 1

    def finish(self):
        while self.done < self.n // 2:
            self.hop()
        return self.block(0).astype(F32) + self.up.astype(F32) + self.down.astype(F32)


def after(x, *others):
    return lax.optimization_barrier((x, *others))[0] if others else x


def cost(flops, nbytes):
    return pl.CostEstimate(flops=int(flops), bytes_accessed=int(nbytes), transcendentals=0)


def whole(shape):
    return pl.BlockSpec(shape, lambda *_: (0,) * len(shape), pipeline_mode=pl.Buffered(1))


def assemble_kernel(index_ref, pieces, out_ref, at):
    rows, cols = pieces[0].shape
    for k, piece in enumerate(pieces):
        row = pl.multiple_of(index_ref[k] * rows, rows)
        out_ref[pl.ds(row, rows), at : at + cols] = piece[...]


def split3(x):
    hi = x.astype(BF).astype(F32)
    rest = x - hi
    mid = rest.astype(BF).astype(F32)
    return hi, mid, rest - mid


def put3(base, lane, first, x):
    hi, mid, lo = split3(x)
    return jnp.where(
        lane == first,
        hi,
        jnp.where(lane == first + 1, mid, jnp.where(lane == first + 2, lo, base)),
    )


def project_kernel(index_ref, slope_ref, length_ref, n_ref, bias_ref, *refs, heads):
    *pieces, q_ref, k_ref, v_ref, w_ref = refs

    @pl.when(pl.program_id(0) == 0)
    def _():
        assemble_kernel(index_ref, pieces, w_ref, 0)

    rows = n_ref.shape[0]
    width = heads * HEAD_DIM
    out = dot(n_ref[...], w_ref[...])
    query = (out[:, :width] + bias_ref[0:1, :]).astype(BF).astype(F32) * (HEAD_DIM**-0.5)
    key = out[:, width : 2 * width]
    value = out[:, 2 * width :] + bias_ref[1:2, :]
    lane = lax.broadcasted_iota(jnp.int32, (rows, 128), 1)
    at = lax.broadcasted_iota(jnp.int32, (rows, 128), 0) + pl.program_id(0) * rows
    ones = ((lane >= 64) & (lane < 67)).astype(F32)
    more = ((lane >= 67) & (lane < 70)).astype(F32)
    seen = at < length_ref[0]
    zero = jnp.zeros((rows, 64), F32)
    for h in range(heads):
        cols = slice(h * HEAD_DIM, (h + 1) * HEAD_DIM)
        slope = jnp.where(seen, at.astype(F32) * slope_ref[h], masked_score)
        q_ref[h] = (jnp.concatenate([query[:, cols], zero], axis=1) + ones).astype(BF)
        wide = jnp.concatenate([key[:, cols], zero], axis=1) + more
        k_ref[h] = put3(wide, lane, 64, slope).astype(BF)
        v_ref[h] = (jnp.concatenate([value[:, cols], zero], axis=1) + ones).astype(BF)


def project(normed, index, pieces, col_bias, slopes, length):
    span, depth = normed.shape
    cols = pieces[0].shape[1]
    heads = slopes.shape[0]
    tile = 256
    shape = jax.ShapeDtypeStruct((heads, span, 128), BF)
    return pl.pallas_call(
        functools.partial(project_kernel, heads=heads),
        out_shape=(shape,) * 3 + (jax.ShapeDtypeStruct((depth, cols), BF),),
        grid=(span // tile,),
        in_specs=[pl.BlockSpec(memory_space=pltpu.SMEM)] * 3
        + [pl.BlockSpec((tile, depth), lambda i: (i, 0)), whole(col_bias.shape)]
        + [whole(piece.shape) for piece in pieces],
        out_specs=[pl.BlockSpec((heads, tile, 128), lambda i: (0, i, 0))] * 3
        + [whole((depth, cols))],
        compiler_params=pltpu.CompilerParams(vmem_limit_bytes=40 * MIB),
        cost_estimate=cost(2 * span * depth * cols, 12 * MIB),
        name="project",
    )(index, slopes, length, normed, col_bias, *pieces)


def attend_forward_kernel(q_ref, k_ref, v_ref, o_ref, qb_ref, send_ref, *, bq, span):
    lane = lax.broadcasted_iota(jnp.int32, (bq, 128), 1)
    row = lax.broadcasted_iota(jnp.int32, (bq, bq), 0)
    causal = row >= lax.broadcasted_iota(jnp.int32, (bq, bq), 1)
    for i in range(span // bq):
        outs = []
        here = pl.ds(i * bq, bq)
        for h in range(2):
            q = q_ref[h, here, :]
            near = jnp.where(causal, dot(q, k_ref[h, here, :], NT), masked_score)
            highest = jnp.max(near, axis=1, keepdims=True)
            if i:
                before = pl.ds(0, i * bq)
                far = dot(q, k_ref[h, before, :], NT)
                highest = jnp.maximum(highest, jnp.max(far, axis=1, keepdims=True))
            acc = dot(jnp.exp(near - highest).astype(BF), v_ref[h, here, :])
            if i:
                acc = acc + dot(jnp.exp(far - highest).astype(BF), v_ref[h, before, :])
            total = acc[:, 64:65]
            outs.append((acc[:, :64] * (1.0 / total)).astype(BF))
            log_sum = highest + jnp.log(total)
            qb_ref[h, here, :] = put3(q.astype(F32), lane, 67, -log_sum).astype(BF)
        o_ref[here, :] = jnp.concatenate(outs, axis=1)
    half = span // 2
    for j in range(4):
        send_ref[j] = o_ref[pl.ds(j % 2 * half, half), :]


def pair_spec(span, pair):
    return pl.BlockSpec((2, span, 128), lambda i: (pair, 0, 0), pipeline_mode=pl.Buffered(1))


def attend_forward(q, k, v, pair):
    span = q.shape[1]
    shapes = [(span, 128), (2, span, 128), (4, span // 2, 128)]
    return pl.pallas_call(
        functools.partial(attend_forward_kernel, bq=min(512, span), span=span),
        out_shape=[jax.ShapeDtypeStruct(x, BF) for x in shapes],
        grid=(1,),
        in_specs=[pair_spec(span, pair)] * 3,
        out_specs=[whole(x) for x in shapes],
        compiler_params=pltpu.CompilerParams(vmem_limit_bytes=50 * MIB),
        cost_estimate=cost(12e9, 5 * MIB),
        name="attend_forward",
    )(q, k, v)


def attend_backward_kernel(half_ref, q_ref, k_ref, v_ref, o_ref, *refs, bk, span, chunks):
    partials, (d_ref, sib_ref, sum_ref, do_ref, doa_ref, dq_ref) = refs[:-6], refs[-6:]
    half = span // 2
    rows = half // chunks
    for c, part in enumerate(partials):
        for side in range(2):
            total = part[side].astype(F32) + part[2 + side].astype(F32)
            do_ref[pl.ds(side * half + c * rows, rows), :] = total.astype(BF)
    lane = lax.broadcasted_iota(jnp.int32, (span, 128), 1)
    row = lax.broadcasted_iota(jnp.int32, (bk, bk), 0)
    causal = row <= lax.broadcasted_iota(jnp.int32, (bk, bk), 1)
    grad = do_ref[...].astype(F32)
    prod = grad * o_ref[...].astype(F32)
    for h in range(2):
        cols = slice(h * HEAD_DIM, (h + 1) * HEAD_DIM)
        delta = jnp.sum(prod[:, cols], axis=1, keepdims=True)
        base = jnp.concatenate([grad[:, cols], jnp.zeros((span, 64), F32)], axis=1)
        doa_ref[h] = put3(base, lane, 64, -delta).astype(BF)
    dq_ref[...] = jnp.zeros_like(dq_ref)
    value_sums = jnp.zeros((1, 128), F32)
    for j in range(span // bk):
        dks, dvs = [], []
        here = pl.ds(j * bk, bk)
        rest = pl.ds(j * bk, span - j * bk)
        for h in range(2):
            k = k_ref[h, here, :]
            q = q_ref[h, rest, :]
            do = doa_ref[h, rest, :]
            p = jnp.exp(dot(k, q, NT))
            near = jnp.where(causal, p[:, :bk], 0.0)
            p = jnp.concatenate([near, p[:, bk:]], axis=1) if rest.size > bk else near
            ds = (p * dot(v_ref[h, here, :], do, NT)).astype(BF)
            dvs.append(dot(p.astype(BF), do)[:, :64])
            dks.append(dot(ds, q)[:, :64])
            dq_ref[h, :, rest] += dot(k[:, :64], ds, TN)
        d_ref[1, here, :] = jnp.concatenate(dks, axis=1).astype(BF)
        value_grad = jnp.concatenate(dvs, axis=1).astype(BF)
        d_ref[2, here, :] = value_grad
        value_sums += jnp.sum(value_grad.astype(F32), axis=0, keepdims=True)
    dq = jnp.concatenate([dq_ref[0], dq_ref[1]], axis=0).T * (HEAD_DIM**-0.5)
    dq = dq.astype(BF)
    d_ref[0] = dq
    sum_ref[0:1, :] = jnp.sum(dq.astype(F32), axis=0, keepdims=True)
    sum_ref[1:2, :] = value_sums
    for kind in range(3):
        sib_ref[kind] = d_ref[kind, pl.ds(pl.multiple_of((1 - half_ref[0]) * half, half), half), :]


def attend_backward(scalars, qb, k, v, o, partials, pair):
    span = qb.shape[1]
    chunks = len(partials)
    part = pl.BlockSpec((4, span // 2 // chunks, 128), lambda i: (0, 0, pair), pipeline_mode=pl.Buffered(1))
    shapes = [((3, span, 128), BF), ((3, span // 2, 128), BF), ((2, 128), F32)]
    return pl.pallas_call(
        functools.partial(attend_backward_kernel, bk=min(256, span), span=span, chunks=chunks),
        out_shape=[jax.ShapeDtypeStruct(*x) for x in shapes],
        grid=(1,),
        in_specs=[
            pl.BlockSpec(memory_space=pltpu.SMEM),
            pair_spec(span, 0),
            pair_spec(span, pair),
            pair_spec(span, pair),
            whole((span, 128)),
        ]
        + [part] * chunks,
        out_specs=[whole(x[0]) for x in shapes],
        scratch_shapes=[
            pltpu.VMEM((span, 128), BF),
            pltpu.VMEM((2, span, 128), BF),
            pltpu.VMEM((2, 64, span), F32),
        ],
        compiler_params=pltpu.CompilerParams(vmem_limit_bytes=50 * MIB),
        cost_estimate=cost(18e9, 6 * MIB),
        name="attend_backward",
    )(scalars, qb, k, v, o, *partials)


def norm_parts(x):
    average = jnp.mean(x, axis=-1, keepdims=True)
    centred = x - average
    variance = jnp.mean(centred * centred, axis=-1, keepdims=True)
    scale = lax.rsqrt(variance + norm_eps)
    return centred * scale, scale


def norm_back(grad, unit, scale, gain):
    weighted = grad * gain
    mean_one = jnp.mean(weighted, axis=-1, keepdims=True)
    mean_two = jnp.mean(weighted * unit, axis=-1, keepdims=True)
    return scale * (weighted - mean_one - unit * mean_two)


def middle_kernel(
    scalar_ref,
    o0_ref,
    o1_ref,
    tokens_ref,
    cot_ref,
    late_own_ref,
    late_sib_ref,
    row_ref,
    bias_ref,
    *refs,
    chunk,
):
    (*mlp_refs, resid_ref, send_ref, g_ref, du_ref, da_ref, do_ref, sum_ref, up_sum_ref, out_w) = refs
    step = pl.program_id(0)
    tile, depth = tokens_ref.shape

    @pl.when(step == 0)
    def _():
        for k, ref in enumerate((late_own_ref, late_sib_ref)):
            for chip in range(2):
                for pair in range(2):
                    at = (pair * 4 + (scalar_ref[3] ^ (k + 2 * chip))) * 128
                    cols = slice(256 * chip + 128 * pair, 256 * chip + 128 * (pair + 1))
                    out_w[:, pl.ds(pl.multiple_of(at, 128), 128)] = ref[:, cols]
        sum_ref[...] = jnp.zeros_like(sum_ref)
        up_sum_ref[...] = jnp.zeros_like(up_sum_ref)

    heads = jnp.concatenate([ref[j] for ref in (o0_ref, o1_ref) for j in range(4)], axis=1)
    branch = dot(heads, out_w[...], NT) + row_ref[2:3, :]
    resid = tokens_ref[...].astype(F32) + branch
    resid_ref[...] = resid.astype(BF)
    at = lax.broadcasted_iota(jnp.int32, (tile, 1), 0) + (
        scalar_ref[0] * scalar_ref[1] + (chunk * pl.num_programs(0) + step) * tile
    )
    valid = (at < scalar_ref[2]).astype(F32)
    unit, scale = norm_parts(resid)
    n2 = (unit * row_ref[3:4, :] + row_ref[4:5, :]).astype(BF)
    send_ref[:, :depth] = n2
    cot = cot_ref[...]
    dm = cot.astype(BF)
    mlp = None
    hid = (late_own_ref.shape[1] - 512) // 2
    for half, late in enumerate((late_own_ref, late_sib_ref)):
        up, down = late.at[:, 512 : 512 + hid], late.at[:, 512 + hid :]
        u = dot(n2, up[...]) + bias_ref[half : half + 1, :]
        square = u * u
        t = jnp.tanh(gelu_scale * (u + gelu_cubic * square * u))
        plus = 0.5 * (1.0 + t)
        g = (u * plus).astype(BF)
        slope = plus + (0.5 * gelu_scale) * u * (1.0 - t * t) * (1.0 + 3.0 * gelu_cubic * square)
        du_wide = (dot(dm, down[...]) * slope).astype(BF)
        if half == 0:
            g_ref[...] = g
            du_ref[...] = du_wide
        else:
            send_ref[:, depth : depth + hid] = g
            send_ref[:, depth + hid :] = du_wide
        up_sum_ref[half : half + 1, :] += jnp.sum(du_wide.astype(F32), axis=0, keepdims=True)
        m = dot(g, down[...], NT)
        d = dot(du_wide, up[...], NT)
        mlp, dn2 = (m, d) if mlp is None else (mlp + m, dn2 + d)
    mlp = mlp.astype(BF)
    start = 0
    for ref in mlp_refs:
        stop = start + ref.shape[0]
        for k in range(start // tile, (stop - 1) // tile + 1):
            low, high = max(start, k * tile), min(stop, (k + 1) * tile)

            @pl.when(step == k)
            def _(ref=ref, at=low - start, low=low - k * tile, size=high - low):
                ref[at : at + size, :] = mlp[low : low + size, :]

        start = stop
    dr = norm_back(dn2, unit, scale, row_ref[3:4, :]) + 0.5 * cot
    da = dr.astype(BF)
    da_ref[...] = da
    do = dot(da, out_w[...]).astype(BF)
    for j in range(4):
        do_ref[j] = jnp.concatenate([do[:, 128 * (j + 4 * p) : 128 * (j + 4 * p + 1)] for p in range(2)], axis=1)
    for k, x in enumerate(
        (dn2 * unit, dn2, da.astype(F32), 0.5 * dm.astype(F32), valid * branch * branch)
    ):
        sum_ref[k : k + 1, :] += jnp.sum(x, axis=0, keepdims=True)


def middle(scalars, heads_in, tokens, cotangent, weights, row_vectors, up_bias, pieces):
    depth = tokens.shape[1]
    half = tokens.shape[0] // 2
    tile = 256
    chunk, chunks = 0, 1
    steps = half // tile
    hidden = weights[0].shape[1] - 512
    own = lambda i, s: (chunk * steps + i, 0)
    absolute = lambda i, s: (s[0] * (half // tile) + chunk * steps + i, 0)
    part = lambda i, s: (i, 0)
    parts = [(depth, BF), (depth + hidden, BF), (hidden // 2, BF), (hidden // 2, BF), (depth, BF)]
    return pl.pallas_call(
        functools.partial(middle_kernel, chunk=chunk),
        out_shape=[jax.ShapeDtypeStruct((rows, depth), BF) for rows in pieces]
        + [jax.ShapeDtypeStruct((half // chunks, w), t) for w, t in parts]
        + [jax.ShapeDtypeStruct((4, half // chunks, 256), BF)]
        + [jax.ShapeDtypeStruct((8, depth), F32), jax.ShapeDtypeStruct((2, hidden // 2), F32)],
        grid_spec=pltpu.PrefetchScalarGridSpec(
            num_scalar_prefetch=1,
            grid=(steps,),
            in_specs=[pl.BlockSpec((4, tile, 128), lambda i, s: (0, *own(i, s)))] * 2
            + [pl.BlockSpec((tile, depth), absolute)] * 2
            + [whole(w.shape) for w in weights]
            + [whole(row_vectors.shape), whole(up_bias.shape)],
            out_specs=[whole((rows, depth)) for rows in pieces]
            + [pl.BlockSpec((tile, w), part) for w, _ in parts]
            + [pl.BlockSpec((4, tile, 256), lambda i, s: (0, i, 0))]
            + [whole((8, depth)), whole((2, hidden // 2))],
            scratch_shapes=[
                pltpu.VMEM((depth, 1024), BF),
            ],
        ),
        compiler_params=pltpu.CompilerParams(vmem_limit_bytes=56 * MIB),
        cost_estimate=cost(21e9 / chunks, 24 * MIB),
        name="middle",
    )(scalars, *heads_in, tokens, cotangent, *weights, row_vectors, up_bias)


def last_kernel(
    scalar_ref, o0_ref, o1_ref, s0_ref, s1_ref, w_own_ref, w_sib_ref, tokens_ref, *refs
):
    da_ref, row_ref, *ig_refs, sum_ref = refs
    step = pl.program_id(0)

    @pl.when(step == 0)
    def _():
        sum_ref[...] = jnp.zeros_like(sum_ref)

    def side(x, y):
        return jnp.concatenate([r[k] for k in range(3) for r in (x, y)], axis=1)

    dn1 = dot(side(o0_ref, o1_ref), w_own_ref[...], NT) + dot(side(s0_ref, s1_ref), w_sib_ref[...], NT)
    unit, scale = norm_parts(tokens_ref[...].astype(F32))
    ig = (da_ref[...].astype(F32) + norm_back(dn1, unit, scale, row_ref[0:1, :])).astype(BF)
    for k, ref in enumerate(ig_refs):

        @pl.when(step == k)
        def _(ref=ref):
            ref[...] = ig

    sum_ref[0:1, :] += jnp.sum(dn1 * unit, axis=0, keepdims=True)
    sum_ref[1:2, :] += jnp.sum(dn1, axis=0, keepdims=True)


def last(scalars, own, sibling, w_own, w_sib, tokens, da, row_vectors):
    depth = tokens.shape[1]
    half = tokens.shape[0] // 2
    steps = 4
    tile = half // steps
    absolute = lambda i, s: (s[0] * steps + i, 0)
    return pl.pallas_call(
        last_kernel,
        out_shape=[jax.ShapeDtypeStruct((tile, depth), BF)] * steps + [jax.ShapeDtypeStruct((8, depth), F32)],
        grid_spec=pltpu.PrefetchScalarGridSpec(
            num_scalar_prefetch=1,
            grid=(steps,),
            in_specs=[pl.BlockSpec((3, tile, 128), lambda i, s: (0, *absolute(i, s)))] * 2
            + [pl.BlockSpec((3, tile, 128), lambda i, s: (0, i, 0))] * 2
            + [whole(w_own.shape), whole(w_sib.shape), pl.BlockSpec((tile, depth), absolute)]
            + [pl.BlockSpec((tile, depth), lambda i, s: (i, 0))]
            + [whole(row_vectors.shape)],
            out_specs=[
                *[whole((tile, depth))] * steps,
                whole((8, depth)),
            ],
        ),
        compiler_params=pltpu.CompilerParams(vmem_limit_bytes=40 * MIB),
        cost_estimate=cost(3.2e9, 20 * MIB),
        name="last",
    )(scalars, *own, *sibling, w_own, w_sib, tokens, da, row_vectors)


def out_grads_kernel(*refs, chunks):
    das, heads, out_ref = refs[1 : 1 + chunks], refs[1 + chunks : -1], refs[-1]
    out_ref[...] = sum_over_chunks(das, heads).astype(BF)


def sum_over_chunks(das, heads):
    rows = das[0].shape[0]
    total = 0.0
    for c, da in enumerate(das):
        right = jnp.concatenate([h[0, c * rows : (c + 1) * rows, :] for h in heads], axis=1)
        total = total + dot(da[...], right, TN)
    return total


def head_specs(half, side):
    return [
        pl.BlockSpec((1, half, 128), lambda i, s, flip=flip: (s[3] ^ flip, 0, 0), pipeline_mode=pl.Buffered(1))
        for flip in (side, side, side + 2, side + 2)
    ]


def out_grads(scalars, das, heads_in):
    rows, depth = das[0].shape
    tile = 256
    return pl.pallas_call(
        functools.partial(out_grads_kernel, chunks=len(das)),
        out_shape=jax.ShapeDtypeStruct((depth, 512), BF),
        grid_spec=pltpu.PrefetchScalarGridSpec(
            num_scalar_prefetch=1,
            grid=(depth // tile,),
            in_specs=[pl.BlockSpec((rows, tile), lambda i, s: (0, i))] * len(das)
            + head_specs(rows * len(das), 1),
            out_specs=pl.BlockSpec((tile, 512), lambda i, s: (i, 0)),
        ),
        compiler_params=pltpu.CompilerParams(vmem_limit_bytes=24 * MIB),
        name="out_grads",
    )(scalars, *das, *heads_in, *heads_in)


def weight_grads_kernel(scalar_ref, cot_ref, *refs, chunks):
    *refs, out_ref = refs
    groups = [refs[3 * k : 3 * k + 3] for k in range(2 * chunks)]
    das, heads, got_ref = refs[6 * chunks : 7 * chunks], refs[7 * chunks : -1], refs[-1]
    rows = groups[0][0].shape[0]
    up = down = 0.0
    for k, (n2, g, du) in enumerate(groups):
        side = scalar_ref[0] if k < chunks else 1 - scalar_ref[0]
        at = pl.multiple_of((side * chunks + k % chunks) * rows, rows)
        up = up + dot(n2[...], du[...], TN)
        down = down + dot(cot_ref[pl.ds(at, rows), :].astype(BF), g[...], TN)
    hidden = up.shape[1]
    out_ref[:, :hidden] = up.astype(BF)
    out_ref[:, hidden : 2 * hidden] = down.astype(BF)
    out_ref[:, 2 * hidden :] = (sum_over_chunks(das, heads) + got_ref[...].astype(F32)).astype(BF)


def weight_grads(scalars, cotangent, own, got, das, heads_in, got_out):
    span, depth = cotangent.shape
    chunks = len(own)
    rows, hidden = own[0][1].shape
    tile = 256
    block = lambda r, at: pl.BlockSpec((r, tile), lambda i, s: (0, i))
    fixed = lambda at: pl.BlockSpec((rows, hidden), lambda i, s: (0, at), pipeline_mode=pl.Buffered(1))
    at = depth // hidden
    specs = ([block(rows, 0), fixed(0), fixed(0)] * chunks) + ([block(rows, 0), fixed(at), fixed(at + 1)] * chunks)
    return pl.pallas_call(
        functools.partial(weight_grads_kernel, chunks=chunks),
        out_shape=jax.ShapeDtypeStruct((depth, 2 * hidden + 512), BF),
        grid_spec=pltpu.PrefetchScalarGridSpec(
            num_scalar_prefetch=1,
            grid=(depth // tile,),
            in_specs=[block(span, 0)]
            + specs
            + [block(rows, 0)] * chunks
            + head_specs(rows * chunks, 0)
            + [pl.BlockSpec((tile, 512), lambda i, s: (i, 0))],
            out_specs=pl.BlockSpec((tile, 2 * hidden + 512), lambda i, s: (i, 0)),
        ),
        compiler_params=pltpu.CompilerParams(vmem_limit_bytes=50 * MIB),
        cost_estimate=cost(2 * span * depth * (2 * hidden + 256), 30 * MIB),
        name="weight_grads",
    )(
        scalars,
        cotangent,
        *[x for group in own for x in group],
        *[x for group in got for x in (group,) * 3],
        *das,
        *heads_in,
        *heads_in,
        got_out,
    )


def qkv_grads_kernel(n_ref, p0_ref, p1_ref, out_ref):
    right = jnp.concatenate([p[k] for k in range(3) for p in (p0_ref, p1_ref)], axis=1)
    out_ref[...] = dot(n_ref[...], right, TN).astype(BF)


def qkv_grads(normed, parts):
    span, depth = normed.shape
    tile = 256
    return pl.pallas_call(
        qkv_grads_kernel,
        out_shape=jax.ShapeDtypeStruct((depth, 768), BF),
        grid=(depth // tile,),
        in_specs=[pl.BlockSpec((span, tile), lambda i: (0, i))] + [whole(p.shape) for p in parts],
        out_specs=pl.BlockSpec((tile, 768), lambda i: (i, 0)),
        compiler_params=pltpu.CompilerParams(vmem_limit_bytes=32 * MIB),
        cost_estimate=cost(2 * span * depth * 768, 10 * MIB),
        name="qkv_grads",
    )(normed, *parts)


def finish_kernel(scalar_ref, *refs, pieces, terms, cuts):
    for k in range(pieces):

        @pl.when(pl.program_id(0) // cuts == k)
        def _():
            total = refs[k * terms][...].astype(F32)
            for ref in refs[k * terms + 1 : (k + 1) * terms]:
                total = total + ref[...].astype(F32)
            refs[-1][...] = total


def finish(scalars, side, pieces, before=(), first=0, whole_pieces=4):
    rows, depth = pieces[0][0].shape
    terms = [x for piece in pieces for x in piece]
    cuts = 4 if len(pieces) == 1 else 1
    tile = rows // cuts
    spec = whole((rows, depth)) if cuts == 1 else pl.BlockSpec((tile, depth), lambda i, s: (i, 0))
    out = pl.pallas_call(
        functools.partial(finish_kernel, pieces=len(pieces), terms=len(pieces[0]), cuts=cuts),
        out_shape=[jax.ShapeDtypeStruct((2 * whole_pieces * rows, depth), F32)],
        grid_spec=pltpu.PrefetchScalarGridSpec(
            num_scalar_prefetch=1,
            grid=(len(pieces) * cuts,),
            in_specs=[spec] * len(terms) + [pl.BlockSpec(memory_space=pl.ANY)] * len(before),
            out_specs=[
                pl.BlockSpec((tile, depth), lambda i, s: ((s[0] ^ side) * whole_pieces * cuts + first + i, 0))
            ],
        ),
        input_output_aliases={1 + len(terms): 0} if before else {},
        compiler_params=pltpu.CompilerParams(vmem_limit_bytes=24 * MIB),
        cost_estimate=cost(0, 8 * rows * depth * len(pieces)),
        name="finish",
    )(scalars, *terms, *before)
    return out[0]


def adam_rows_kernel(g_ref, w_ref, m_ref, v_ref, nm_ref, nv_ref, nw_ref):
    kinds, width = w_ref.shape[1:]
    for k in range(kinds):
        grad = g_ref[:, k * width : (k + 1) * width]
        new = adamw(w_ref[:, k, :], m_ref[:, k, :], v_ref[:, k, :], grad, matrix_rate, weight_decay)
        nm_ref[:, k, :], nv_ref[:, k, :], nw_ref[:, k, :] = new


def adam_turned_kernel(g_ref, w_ref, m_ref, v_ref, nm_ref, nv_ref, nw_ref):
    new = adamw(w_ref[...], m_ref[...], v_ref[...], g_ref[...].T, matrix_rate, weight_decay)
    nm_ref[...], nv_ref[...], nw_ref[...] = new


def adam(kernel, grad, *state):
    return pl.pallas_call(
        kernel,
        out_shape=[jax.ShapeDtypeStruct(state[0].shape, F32)] * 3,
        grid=(1,),
        in_specs=[whole(x.shape) for x in (grad, *state)],
        out_specs=[whole(state[0].shape)] * 3,
        compiler_params=pltpu.CompilerParams(vmem_limit_bytes=24 * MIB),
        cost_estimate=cost(0, 28 * grad.size),
        name="adam",
    )(grad, *state)


def adam_turned(grad, *state):
    if grad.shape[0] % 128:
        return adamw(*state, grad.T.reshape(state[0].shape), matrix_rate, weight_decay)
    flat = [x.reshape(-1, x.shape[-1]) for x in state]
    return [x.reshape(state[0].shape) for x in adam(adam_turned_kernel, grad, *flat)]


def body(
    tokens,
    cotangent,
    lengths,
    qkv_weight,
    qkv_first,
    qkv_second,
    out_weight,
    out_first,
    out_second,
    up_weight,
    up_first,
    up_second,
    down_weight,
    down_first,
    down_second,
    row_vectors,
    row_first,
    row_second,
    col_bias,
    col_first,
    col_second,
):
    span, depth = tokens.shape
    half = span // 2
    share = qkv_weight.shape[0]
    n_dp = lax.axis_size("dp")
    device = lax.axis_index("mp")
    core = device % 2
    heads = qkv_weight.shape[2] // HEAD_DIM
    width = heads * HEAD_DIM
    hidden = up_weight.shape[1] * up_weight.shape[2]
    head_ids = device * heads + jnp.arange(heads)
    slopes = jnp.exp2(-8.0 * (head_ids.astype(F32) + 1.0) / HEADS)
    scalars = jnp.stack([core.astype(jnp.int32), jnp.int32(half), lengths[0], device.astype(jnp.int32)])

    index = ring_index(n_dp)
    out_piece = out_weight.astype(BF).T
    out_piece = jnp.concatenate([out_piece, to_chip(out_piece)], axis=1)
    qkv_ring = Gather(qkv_weight.astype(BF).reshape(share, 3 * width))
    up_piece = up_weight.astype(BF).reshape(share, hidden)
    down_piece = down_weight.astype(BF).reshape(hidden, share).T
    late_piece = jnp.concatenate([out_piece, up_piece, down_piece], axis=1)
    late_w = lax.all_gather(late_piece, "dp", axis=0, tiled=True)
    up_bias = col_bias[2:].reshape(1, hidden)
    up_bias = jnp.concatenate([up_bias, to_core(up_bias)], axis=0)
    for _ in range(n_dp // 2):
        qkv_ring.hop()

    unit_one, _ = norm_parts(tokens.astype(F32))
    normed = (unit_one * row_vectors[0] + row_vectors[1]).astype(BF)
    q, k, v, qkv_w = project(after(normed, up_bias), index, qkv_ring.finish(), col_bias, slopes, lengths)
    outs, heads_in = [], []
    for pair in range(2):
        o, qb, send = attend_forward(q, k, v, pair)
        outs.append((o, qb))
        heads_in.append(to_all(after(send, *heads_in)))
    qkv_sib = to_core(qkv_w)
    late_w = after(late_w, heads_in[1])
    late_sib = to_core(late_w)

    weights = (late_w, after(late_sib, qkv_sib))
    chunks = 1
    pieces = [half * 3 // 8, half * 3 // 8, half // 4]
    *mlps, resid, send, g, du, da, do, sums, up_sums = middle(
        scalars, heads_in, tokens, cotangent, weights, row_vectors, up_bias, pieces
    )
    resids, das = [resid], [da]
    got_send = to_core(send)
    got_out = to_core(out_grads(scalars, das, heads_in))
    partials = [to_all(do)]
    total = weight_grads(scalars, cotangent, [(send, g, du)], [got_send], das, heads_in, got_out)
    total = after(total, *partials)
    mlp_far = [to_chip(after(mlps[0], total))]
    shard = lax.psum_scatter(total, "dp", scatter_dimension=0, tiled=True)

    parts, part_sums, siblings = [], [], []
    for pair in range(2):
        o, qb = outs[pair]
        qb = after(qb, total)
        d, d_sib, s = attend_backward(scalars, qb, k, v, o, partials, pair)
        parts.append(d)
        part_sums.append(s)
        d_sib = after(d_sib, mlp_far[pair])
        if pair == 0:
            outs[1] = (outs[1][0], after(outs[1][1], mlp_far[0], s))
        mlp_far.append(to_chip(after(mlps[pair + 1], mlp_far[pair])))
        siblings.append(to_core(d_sib))
    qkv_wgrad = after(qkv_grads(normed, parts), *siblings)
    qkv_ring = Reduce(qkv_wgrad, index, -1)
    qkv_ring.hop()

    *igs, last_sums = last(
        scalars, parts, siblings, qkv_w, qkv_sib, after(tokens, qkv_wgrad), das[0], row_vectors
    )
    first_gates = (mlp_far[2], qkv_ring.up, qkv_ring.down)
    igs[0], last_sums = after(igs[0], *first_gates), after(last_sums, *first_gates)
    ig_far = [to_chip(igs[0])]
    ig_sib = [to_core(after(x, last_sums)) for x in igs]
    qkv_ring.hop(last_sums)
    valid = ((core * half + jnp.arange(half)) < lengths[0]).astype(F32)[:, None]
    stat_out, stat_m, own_low = 0.0, 0.0, []
    at = 0
    for m, f in zip(mlps, mlp_far):
        rows = slice(at, at + m.shape[0])
        at += m.shape[0]
        branch_m = m.astype(F32) + after(f, last_sums).astype(F32) + row_vectors[5]
        outputs_own = resid[rows].astype(F32) + branch_m
        stat_out += jnp.sum(valid[rows] * outputs_own * outputs_own)
        stat_m += jnp.sum(valid[rows] * branch_m * branch_m)
        own_low.append(outputs_own.astype(BF))
    own_low = jnp.concatenate(own_low, axis=0)
    ig_far.append(to_chip(after(igs[1], ig_far[0], own_low, stat_out, stat_m)))
    qkv_ring.hop(ig_far[0])

    stats = jnp.stack([stat_out, jnp.sum(sums[4]), stat_m, jnp.sum(valid)])
    small = jnp.concatenate(
        [
            last_sums[0:2],
            sums[2:3],
            sums[0:2],
            sums[3:4],
            jnp.pad(stats, (0, depth - 4))[None],
            jnp.pad(
                jnp.concatenate([part_sums[p][kind] for kind in range(2) for p in range(2)]),
                (0, depth - 2 * width),
            )[None],
            up_sums,
        ],
        axis=0,
    )
    rows, columns = small[:7], small[7:9]
    other = to_core(small)
    rows = rows + other[:7]
    columns = jnp.concatenate([columns[:1], columns[1:] + other[9:]], axis=0)
    small = jnp.concatenate([rows, columns], axis=0)
    meet = lambda x, step: x + lax.ppermute(x, "dp", [(i, i ^ step) for i in range(n_dp)])
    outputs = finish(scalars, 0, [[own_low]], (), 0, 1)
    ig_far.append(to_chip(after(igs[2], ig_far[1], outputs, small)))
    qkv_ring.hop(ig_far[1])
    small = meet(after(small, ig_far[1]), 1)
    outputs = finish(scalars, 1, [[to_core(own_low)]], (outputs,), 0, 1)
    ig_cross = [to_core(x) for x in ig_far[:2]]
    front, back = slice(0, 2), slice(2, 4)
    input_grad = finish(scalars, 0, list(zip(igs, ig_far))[front])
    ig_far.append(to_chip(after(igs[3], ig_far[2], outputs, input_grad, small)))
    qkv_shard = after(qkv_ring.finish(), ig_far[2])
    step = 2
    while step < n_dp:
        small = meet(after(small, *ig_far[2 : step]), step)
        step *= 2
    input_grad = finish(scalars, 1, list(zip(ig_sib, ig_cross))[front], (input_grad,))
    up_shard = shard[:, :hidden].astype(F32)
    down_shard = shard[:, hidden : 2 * hidden].astype(F32)
    out_mine = shard[:, 2 * hidden : 2 * hidden + width]
    out_theirs = to_chip(shard[:, 2 * hidden + width :])
    out_shard = out_mine.astype(F32) + out_theirs.astype(F32)

    qkv_new = adam(adam_rows_kernel, qkv_shard, qkv_weight, qkv_first, qkv_second)
    out_new = adam_turned(out_shard, out_weight, out_first, out_second)
    up_new = adam(adam_rows_kernel, up_shard, up_weight, up_first, up_second)
    down_new = adam_turned(down_shard, down_weight, down_first, down_second)
    ig_cross += [to_core(x) for x in ig_far[2:]]
    input_grad = after(input_grad, ig_far[3], up_new[0], down_new[0], qkv_new[0])
    input_grad = finish(scalars, 0, list(zip(igs, ig_far))[back], (input_grad,), 2)
    input_grad = finish(scalars, 1, list(zip(ig_sib, ig_cross))[back], (input_grad,), 2)
    rows = small[:7] + to_chip(after(small[:7], ig_far[3]))
    small = jnp.concatenate([rows, small[7:]], axis=0)
    row_total, stat_total = small[:6], small[6]
    col_total = jnp.concatenate(
        [small[7, : 2 * width].reshape(2, width), small[8].reshape(-1, width)], axis=0
    )
    rms_stats = jnp.sqrt(stat_total[:3] / (stat_total[3] * depth))

    row_new = adamw(row_vectors, row_first, row_second, row_total, vector_rate, 0.0)
    col_new = adamw(col_bias, col_first, col_second, col_total, vector_rate, 0.0)
    return (
        outputs,
        input_grad,
        rms_stats,
        *qkv_new,
        *out_new,
        *up_new,
        *down_new,
        *row_new,
        *col_new,
    )


def solution(mesh):
    matrices = [P("dp", None, "mp"), P("mp", "dp"), P("dp", None, "mp"), P(None, "mp", "dp")]
    vectors = [P(), P(None, "mp")]
    groups = [spec for spec in matrices + vectors for _ in range(3)]
    return jax.shard_map(
        body,
        mesh=mesh,
        in_specs=(P("dp", None), P("dp", None), P("dp"), *groups),
        out_specs=(P("dp", None), P("dp", None), P(), *groups),
        check_vma=False,
    )
```

```python
import functools

import jax
import jax.numpy as jnp
from jax import lax
from jax.experimental import pallas as pl
from jax.experimental.pallas import tpu as pltpu
from jax.sharding import PartitionSpec as P

HEADS = 16
HEAD_DIM = 64
STEP = 5

norm_eps = 1e-05
masked_score = -1e30
first_decay = 0.5
second_decay = 0.5
matrix_rate = 0.03
vector_rate = 0.4
weight_decay = 0.1
adam_eps = 1e-08
gelu_scale = 0.7978845608028654
gelu_cubic = 0.044715

F32 = jnp.float32
BF = jnp.bfloat16
NN = (((1,), (0,)), ((), ()))
NT = (((1,), (1,)), ((), ()))
TN = (((0,), (0,)), ((), ()))
MIB = 2**20


def dot(a, b, dims=NN):
    return lax.dot_general(a, b, dims, preferred_element_type=F32)


def adamw(weight, moment_one, moment_two, gradient, learn_rate, decay_rate):
    moment_one = first_decay * moment_one + (1.0 - first_decay) * gradient
    moment_two = second_decay * moment_two + (1.0 - second_decay) * gradient * gradient
    correct_one = 1.0 - first_decay**STEP
    correct_two = 1.0 - second_decay**STEP
    direction = moment_one / correct_one / (jnp.sqrt(moment_two / correct_two) + adam_eps)
    return (moment_one, moment_two, weight - learn_rate * (direction + decay_rate * weight))


def to_core(x):
    return lax.ppermute(x, "mp", [(i, i ^ 1) for i in range(lax.axis_size("mp"))])


def to_chip(x):
    return lax.ppermute(x, "mp", [(i, i ^ 2) for i in range(lax.axis_size("mp"))])


def to_all(x):
    return lax.all_to_all(x, "mp", split_axis=0, concat_axis=0, tiled=True)


def ring_order(n):
    return [0, 2, 4, 6, 7, 5, 3, 1] if n == 8 else list(range(n))


def ring_perms(n):
    order = ring_order(n)
    up = [(order[p], order[(p + 1) % n]) for p in range(n)]
    down = [(order[p], order[(p - 1) % n]) for p in range(n)]
    return up, down


def ring_index(n):
    order = ring_order(n)
    place = jnp.array([order.index(i) for i in range(n)], jnp.int32)[lax.axis_index("dp")]
    return jnp.array(order, jnp.int32)[(place + jnp.arange(n)) % n]


class Gather:
    def __init__(self, piece, turn=1):
        self.n = lax.axis_size("dp")
        self.perms = ring_perms(self.n)[::turn]
        self.turn = turn
        self.pieces = [piece] + [None] * (self.n - 1)
        self.up = self.down = piece
        self.done = 0

    def hop(self, *gates):
        if self.done == self.n // 2:
            return
        self.done += 1
        self.up = self.pieces[-self.turn * self.done % self.n] = lax.ppermute(after(self.up, *gates), "dp", self.perms[0])
        if self.done <= (self.n - 1) // 2:
            self.down = self.pieces[self.turn * self.done % self.n] = lax.ppermute(after(self.down, *gates), "dp", self.perms[1])

    def finish(self):
        while self.done < self.n // 2:
            self.hop()
        return self.pieces


class Reduce:
    def __init__(self, total, index, turn=1):
        self.n = lax.axis_size("dp")
        self.perms = ring_perms(self.n)[::turn]
        self.turn = turn
        self.total, self.index = total, index
        self.rows = total.shape[0] // self.n
        self.up = self.down = None
        self.done = 0

    def block(self, k):
        return lax.dynamic_slice_in_dim(self.total, self.index[self.turn * k % self.n] * self.rows, self.rows, 0)

    def add(self, x, k):
        if x is None:
            return self.block(k)
        return (x.astype(F32) + self.block(k).astype(F32)).astype(BF)

    def hop(self, *gates):
        ups, downs = self.n // 2, (self.n - 1) // 2
        if self.done == ups:
            return
        up = after(self.add(self.up, ups - self.done), *gates)
        if self.done < downs:
            down = after(self.add(self.down, self.done - downs), *gates)
            self.down = lax.ppermute(down, "dp", self.perms[1])
        self.up = lax.ppermute(up, "dp", self.perms[0])
        self.done += 1

    def finish(self):
        while self.done < self.n // 2:
            self.hop()
        return self.block(0).astype(F32) + self.up.astype(F32) + self.down.astype(F32)


def after(x, *others):
    return lax.optimization_barrier((x, *others))[0] if others else x


def cost(flops, nbytes):
    return pl.CostEstimate(flops=int(flops), bytes_accessed=int(nbytes), transcendentals=0)


def whole(shape):
    return pl.BlockSpec(shape, lambda *_: (0,) * len(shape), pipeline_mode=pl.Buffered(1))


def assemble_kernel(index_ref, pieces, out_ref, at):
    rows, cols = pieces[0].shape
    for k, piece in enumerate(pieces):
        row = pl.multiple_of(index_ref[k] * rows, rows)
        out_ref[pl.ds(row, rows), at : at + cols] = piece[...]


def split3(x):
    hi = x.astype(BF).astype(F32)
    rest = x - hi
    mid = rest.astype(BF).astype(F32)
    return hi, mid, rest - mid


def put3(base, lane, first, x):
    hi, mid, lo = split3(x)
    return jnp.where(
        lane == first,
        hi,
        jnp.where(lane == first + 1, mid, jnp.where(lane == first + 2, lo, base)),
    )


def project_kernel(index_ref, slope_ref, length_ref, n_ref, bias_ref, *refs, heads):
    *pieces, q_ref, k_ref, v_ref, w_ref = refs

    @pl.when(pl.program_id(0) == 0)
    def _():
        assemble_kernel(index_ref, pieces, w_ref, 0)

    rows = n_ref.shape[0]
    width = heads * HEAD_DIM
    out = dot(n_ref[...], w_ref[...])
    query = (out[:, :width] + bias_ref[0:1, :]).astype(BF).astype(F32) * (HEAD_DIM**-0.5)
    key = out[:, width : 2 * width]
    value = out[:, 2 * width :] + bias_ref[1:2, :]
    lane = lax.broadcasted_iota(jnp.int32, (rows, 128), 1)
    at = lax.broadcasted_iota(jnp.int32, (rows, 128), 0) + pl.program_id(0) * rows
    ones = ((lane >= 64) & (lane < 67)).astype(F32)
    more = ((lane >= 67) & (lane < 70)).astype(F32)
    seen = at < length_ref[0]
    zero = jnp.zeros((rows, 64), F32)
    for h in range(heads):
        cols = slice(h * HEAD_DIM, (h + 1) * HEAD_DIM)
        slope = jnp.where(seen, at.astype(F32) * slope_ref[h], masked_score)
        q_ref[h] = (jnp.concatenate([query[:, cols], zero], axis=1) + ones).astype(BF)
        wide = jnp.concatenate([key[:, cols], zero], axis=1) + more
        k_ref[h] = put3(wide, lane, 64, slope).astype(BF)
        v_ref[h] = (jnp.concatenate([value[:, cols], zero], axis=1) + ones).astype(BF)


def project(normed, index, pieces, col_bias, slopes, length):
    span, depth = normed.shape
    cols = pieces[0].shape[1]
    heads = slopes.shape[0]
    tile = 256
    shape = jax.ShapeDtypeStruct((heads, span, 128), BF)
    return pl.pallas_call(
        functools.partial(project_kernel, heads=heads),
        out_shape=(shape,) * 3 + (jax.ShapeDtypeStruct((depth, cols), BF),),
        grid=(span // tile,),
        in_specs=[pl.BlockSpec(memory_space=pltpu.SMEM)] * 3
        + [pl.BlockSpec((tile, depth), lambda i: (i, 0)), whole(col_bias.shape)]
        + [whole(piece.shape) for piece in pieces],
        out_specs=[pl.BlockSpec((heads, tile, 128), lambda i: (0, i, 0))] * 3
        + [whole((depth, cols))],
        compiler_params=pltpu.CompilerParams(vmem_limit_bytes=40 * MIB),
        cost_estimate=cost(2 * span * depth * cols, 12 * MIB),
        name="project",
    )(index, slopes, length, normed, col_bias, *pieces)


def attend_forward_kernel(q_ref, k_ref, v_ref, o_ref, qb_ref, send_ref, *, bq, span):
    lane = lax.broadcasted_iota(jnp.int32, (bq, 128), 1)
    row = lax.broadcasted_iota(jnp.int32, (bq, bq), 0)
    causal = row >= lax.broadcasted_iota(jnp.int32, (bq, bq), 1)
    for i in range(span // bq):
        outs = []
        here = pl.ds(i * bq, bq)
        for h in range(2):
            q = q_ref[h, here, :]
            near = jnp.where(causal, dot(q, k_ref[h, here, :], NT), masked_score)
            highest = jnp.max(near, axis=1, keepdims=True)
            if i:
                before = pl.ds(0, i * bq)
                far = dot(q, k_ref[h, before, :], NT)
                highest = jnp.maximum(highest, jnp.max(far, axis=1, keepdims=True))
            acc = dot(jnp.exp(near - highest).astype(BF), v_ref[h, here, :])
            if i:
                acc = acc + dot(jnp.exp(far - highest).astype(BF), v_ref[h, before, :])
            total = acc[:, 64:65]
            outs.append((acc[:, :64] * (1.0 / total)).astype(BF))
            log_sum = highest + jnp.log(total)
            qb_ref[h, here, :] = put3(q.astype(F32), lane, 67, -log_sum).astype(BF)
        o_ref[here, :] = jnp.concatenate(outs, axis=1)
    half = span // 2
    for j in range(4):
        send_ref[j] = o_ref[pl.ds(j % 2 * half, half), :]


def pair_spec(span, pair):
    return pl.BlockSpec((2, span, 128), lambda i: (pair, 0, 0), pipeline_mode=pl.Buffered(1))


def attend_forward(q, k, v, pair):
    span = q.shape[1]
    shapes = [(span, 128), (2, span, 128), (4, span // 2, 128)]
    return pl.pallas_call(
        functools.partial(attend_forward_kernel, bq=min(512, span), span=span),
        out_shape=[jax.ShapeDtypeStruct(x, BF) for x in shapes],
        grid=(1,),
        in_specs=[pair_spec(span, pair)] * 3,
        out_specs=[whole(x) for x in shapes],
        compiler_params=pltpu.CompilerParams(vmem_limit_bytes=50 * MIB),
        cost_estimate=cost(12e9, 5 * MIB),
        name="attend_forward",
    )(q, k, v)


def attend_backward_kernel(half_ref, q_ref, k_ref, v_ref, o_ref, *refs, bk, span, chunks):
    partials, (d_ref, sib_ref, sum_ref, do_ref, doa_ref, dq_ref) = refs[:-6], refs[-6:]
    half = span // 2
    rows = half // chunks
    for c, part in enumerate(partials):
        for side in range(2):
            total = part[side].astype(F32) + part[2 + side].astype(F32)
            do_ref[pl.ds(side * half + c * rows, rows), :] = total.astype(BF)
    lane = lax.broadcasted_iota(jnp.int32, (span, 128), 1)
    row = lax.broadcasted_iota(jnp.int32, (bk, bk), 0)
    causal = row <= lax.broadcasted_iota(jnp.int32, (bk, bk), 1)
    grad = do_ref[...].astype(F32)
    prod = grad * o_ref[...].astype(F32)
    for h in range(2):
        cols = slice(h * HEAD_DIM, (h + 1) * HEAD_DIM)
        delta = jnp.sum(prod[:, cols], axis=1, keepdims=True)
        base = jnp.concatenate([grad[:, cols], jnp.zeros((span, 64), F32)], axis=1)
        doa_ref[h] = put3(base, lane, 64, -delta).astype(BF)
    dq_ref[...] = jnp.zeros_like(dq_ref)
    value_sums = jnp.zeros((1, 128), F32)
    for j in range(span // bk):
        dks, dvs = [], []
        here = pl.ds(j * bk, bk)
        rest = pl.ds(j * bk, span - j * bk)
        for h in range(2):
            k = k_ref[h, here, :]
            q = q_ref[h, rest, :]
            do = doa_ref[h, rest, :]
            p = jnp.exp(dot(k, q, NT))
            near = jnp.where(causal, p[:, :bk], 0.0)
            p = jnp.concatenate([near, p[:, bk:]], axis=1) if rest.size > bk else near
            ds = (p * dot(v_ref[h, here, :], do, NT)).astype(BF)
            dvs.append(dot(p.astype(BF), do)[:, :64])
            dks.append(dot(ds, q)[:, :64])
            dq_ref[h, :, rest] += dot(k[:, :64], ds, TN)
        d_ref[1, here, :] = jnp.concatenate(dks, axis=1).astype(BF)
        value_grad = jnp.concatenate(dvs, axis=1).astype(BF)
        d_ref[2, here, :] = value_grad
        value_sums += jnp.sum(value_grad.astype(F32), axis=0, keepdims=True)
    dq = jnp.concatenate([dq_ref[0], dq_ref[1]], axis=0).T * (HEAD_DIM**-0.5)
    dq = dq.astype(BF)
    d_ref[0] = dq
    sum_ref[0:1, :] = jnp.sum(dq.astype(F32), axis=0, keepdims=True)
    sum_ref[1:2, :] = value_sums
    for kind in range(3):
        sib_ref[kind] = d_ref[kind, pl.ds(pl.multiple_of((1 - half_ref[0]) * half, half), half), :]


def attend_backward(scalars, qb, k, v, o, partials, pair):
    span = qb.shape[1]
    chunks = len(partials)
    part = pl.BlockSpec((4, span // 2 // chunks, 128), lambda i: (0, 0, pair), pipeline_mode=pl.Buffered(1))
    shapes = [((3, span, 128), BF), ((3, span // 2, 128), BF), ((2, 128), F32)]
    return pl.pallas_call(
        functools.partial(attend_backward_kernel, bk=min(256, span), span=span, chunks=chunks),
        out_shape=[jax.ShapeDtypeStruct(*x) for x in shapes],
        grid=(1,),
        in_specs=[
            pl.BlockSpec(memory_space=pltpu.SMEM),
            pair_spec(span, 0),
            pair_spec(span, pair),
            pair_spec(span, pair),
            whole((span, 128)),
        ]
        + [part] * chunks,
        out_specs=[whole(x[0]) for x in shapes],
        scratch_shapes=[
            pltpu.VMEM((span, 128), BF),
            pltpu.VMEM((2, span, 128), BF),
            pltpu.VMEM((2, 64, span), F32),
        ],
        compiler_params=pltpu.CompilerParams(vmem_limit_bytes=50 * MIB),
        cost_estimate=cost(18e9, 6 * MIB),
        name="attend_backward",
    )(scalars, qb, k, v, o, *partials)


def norm_parts(x):
    average = jnp.mean(x, axis=-1, keepdims=True)
    centred = x - average
    variance = jnp.mean(centred * centred, axis=-1, keepdims=True)
    scale = lax.rsqrt(variance + norm_eps)
    return centred * scale, scale


def norm_back(grad, unit, scale, gain):
    weighted = grad * gain
    mean_one = jnp.mean(weighted, axis=-1, keepdims=True)
    mean_two = jnp.mean(weighted * unit, axis=-1, keepdims=True)
    return scale * (weighted - mean_one - unit * mean_two)


def middle_kernel(
    scalar_ref,
    o0_ref,
    o1_ref,
    tokens_ref,
    cot_ref,
    late_own_ref,
    late_sib_ref,
    row_ref,
    bias_ref,
    *refs,
    chunk,
):
    (*mlp_refs, resid_ref, send_ref, g_ref, du_ref, da_ref, do_ref, sum_ref, up_sum_ref, out_w) = refs
    step = pl.program_id(0)
    tile, depth = tokens_ref.shape

    @pl.when(step == 0)
    def _():
        for k, ref in enumerate((late_own_ref, late_sib_ref)):
            for chip in range(2):
                for pair in range(2):
                    at = (pair * 4 + (scalar_ref[3] ^ (k + 2 * chip))) * 128
                    cols = slice(256 * chip + 128 * pair, 256 * chip + 128 * (pair + 1))
                    out_w[:, pl.ds(pl.multiple_of(at, 128), 128)] = ref[:, cols]
        sum_ref[...] = jnp.zeros_like(sum_ref)
        up_sum_ref[...] = jnp.zeros_like(up_sum_ref)

    heads = jnp.concatenate([ref[j] for ref in (o0_ref, o1_ref) for j in range(4)], axis=1)
    branch = dot(heads, out_w[...], NT) + row_ref[2:3, :]
    resid = tokens_ref[...].astype(F32) + branch
    resid_ref[...] = resid.astype(BF)
    at = lax.broadcasted_iota(jnp.int32, (tile, 1), 0) + (
        scalar_ref[0] * scalar_ref[1] + (chunk * pl.num_programs(0) + step) * tile
    )
    valid = (at < scalar_ref[2]).astype(F32)
    unit, scale = norm_parts(resid)
    n2 = (unit * row_ref[3:4, :] + row_ref[4:5, :]).astype(BF)
    send_ref[:, :depth] = n2
    cot = cot_ref[...]
    dm = cot.astype(BF)
    mlp = None
    hid = (late_own_ref.shape[1] - 512) // 2
    for half, late in enumerate((late_own_ref, late_sib_ref)):
        up, down = late.at[:, 512 : 512 + hid], late.at[:, 512 + hid :]
        u = dot(n2, up[...]) + bias_ref[half : half + 1, :]
        square = u * u
        t = jnp.tanh(gelu_scale * (u + gelu_cubic * square * u))
        plus = 0.5 * (1.0 + t)
        g = (u * plus).astype(BF)
        slope = plus + (0.5 * gelu_scale) * u * (1.0 - t * t) * (1.0 + 3.0 * gelu_cubic * square)
        du_wide = (dot(dm, down[...]) * slope).astype(BF)
        if half == 0:
            g_ref[...] = g
            du_ref[...] = du_wide
        else:
            send_ref[:, depth : depth + hid] = g
            send_ref[:, depth + hid :] = du_wide
        up_sum_ref[half : half + 1, :] += jnp.sum(du_wide.astype(F32), axis=0, keepdims=True)
        m = dot(g, down[...], NT)
        d = dot(du_wide, up[...], NT)
        mlp, dn2 = (m, d) if mlp is None else (mlp + m, dn2 + d)
    mlp = mlp.astype(BF)
    start = 0
    for ref in mlp_refs:
        stop = start + ref.shape[0]
        for k in range(start // tile, (stop - 1) // tile + 1):
            low, high = max(start, k * tile), min(stop, (k + 1) * tile)

            @pl.when(step == k)
            def _(ref=ref, at=low - start, low=low - k * tile, size=high - low):
                ref[at : at + size, :] = mlp[low : low + size, :]

        start = stop
    dr = norm_back(dn2, unit, scale, row_ref[3:4, :]) + 0.5 * cot
    da = dr.astype(BF)
    da_ref[...] = da
    do = dot(da, out_w[...]).astype(BF)
    for j in range(4):
        do_ref[j] = jnp.concatenate([do[:, 128 * (j + 4 * p) : 128 * (j + 4 * p + 1)] for p in range(2)], axis=1)
    for k, x in enumerate(
        (dn2 * unit, dn2, da.astype(F32), 0.5 * dm.astype(F32), valid * branch * branch)
    ):
        sum_ref[k : k + 1, :] += jnp.sum(x, axis=0, keepdims=True)


def middle(scalars, heads_in, tokens, cotangent, weights, row_vectors, up_bias, pieces):
    depth = tokens.shape[1]
    half = tokens.shape[0] // 2
    tile = 256
    chunk, chunks = 0, 1
    steps = half // tile
    hidden = weights[0].shape[1] - 512
    own = lambda i, s: (chunk * steps + i, 0)
    absolute = lambda i, s: (s[0] * (half // tile) + chunk * steps + i, 0)
    part = lambda i, s: (i, 0)
    parts = [(depth, BF), (depth + hidden, BF), (hidden // 2, BF), (hidden // 2, BF), (depth, BF)]
    return pl.pallas_call(
        functools.partial(middle_kernel, chunk=chunk),
        out_shape=[jax.ShapeDtypeStruct((rows, depth), BF) for rows in pieces]
        + [jax.ShapeDtypeStruct((half // chunks, w), t) for w, t in parts]
        + [jax.ShapeDtypeStruct((4, half // chunks, 256), BF)]
        + [jax.ShapeDtypeStruct((8, depth), F32), jax.ShapeDtypeStruct((2, hidden // 2), F32)],
        grid_spec=pltpu.PrefetchScalarGridSpec(
            num_scalar_prefetch=1,
            grid=(steps,),
            in_specs=[pl.BlockSpec((4, tile, 128), lambda i, s: (0, *own(i, s)))] * 2
            + [pl.BlockSpec((tile, depth), absolute)] * 2
            + [whole(w.shape) for w in weights]
            + [whole(row_vectors.shape), whole(up_bias.shape)],
            out_specs=[whole((rows, depth)) for rows in pieces]
            + [pl.BlockSpec((tile, w), part) for w, _ in parts]
            + [pl.BlockSpec((4, tile, 256), lambda i, s: (0, i, 0))]
            + [whole((8, depth)), whole((2, hidden // 2))],
            scratch_shapes=[
                pltpu.VMEM((depth, 1024), BF),
            ],
        ),
        compiler_params=pltpu.CompilerParams(vmem_limit_bytes=56 * MIB),
        cost_estimate=cost(21e9 / chunks, 24 * MIB),
        name="middle",
    )(scalars, *heads_in, tokens, cotangent, *weights, row_vectors, up_bias)


def last_kernel(
    scalar_ref, o0_ref, o1_ref, s0_ref, s1_ref, w_own_ref, w_sib_ref, tokens_ref, *refs
):
    da_ref, row_ref, *ig_refs, sum_ref = refs
    step = pl.program_id(0)

    @pl.when(step == 0)
    def _():
        sum_ref[...] = jnp.zeros_like(sum_ref)

    def side(x, y):
        return jnp.concatenate([r[k] for k in range(3) for r in (x, y)], axis=1)

    dn1 = dot(side(o0_ref, o1_ref), w_own_ref[...], NT) + dot(side(s0_ref, s1_ref), w_sib_ref[...], NT)
    unit, scale = norm_parts(tokens_ref[...].astype(F32))
    ig = (da_ref[...].astype(F32) + norm_back(dn1, unit, scale, row_ref[0:1, :])).astype(BF)
    for k, ref in enumerate(ig_refs):

        @pl.when(step == k)
        def _(ref=ref):
            ref[...] = ig

    sum_ref[0:1, :] += jnp.sum(dn1 * unit, axis=0, keepdims=True)
    sum_ref[1:2, :] += jnp.sum(dn1, axis=0, keepdims=True)


def last(scalars, own, sibling, w_own, w_sib, tokens, da, row_vectors):
    depth = tokens.shape[1]
    half = tokens.shape[0] // 2
    steps = 4
    tile = half // steps
    absolute = lambda i, s: (s[0] * steps + i, 0)
    return pl.pallas_call(
        last_kernel,
        out_shape=[jax.ShapeDtypeStruct((tile, depth), BF)] * steps + [jax.ShapeDtypeStruct((8, depth), F32)],
        grid_spec=pltpu.PrefetchScalarGridSpec(
            num_scalar_prefetch=1,
            grid=(steps,),
            in_specs=[pl.BlockSpec((3, tile, 128), lambda i, s: (0, *absolute(i, s)))] * 2
            + [pl.BlockSpec((3, tile, 128), lambda i, s: (0, i, 0))] * 2
            + [whole(w_own.shape), whole(w_sib.shape), pl.BlockSpec((tile, depth), absolute)]
            + [pl.BlockSpec((tile, depth), lambda i, s: (i, 0))]
            + [whole(row_vectors.shape)],
            out_specs=[
                *[whole((tile, depth))] * steps,
                whole((8, depth)),
            ],
        ),
        compiler_params=pltpu.CompilerParams(vmem_limit_bytes=40 * MIB),
        cost_estimate=cost(3.2e9, 20 * MIB),
        name="last",
    )(scalars, *own, *sibling, w_own, w_sib, tokens, da, row_vectors)


def out_grads_kernel(*refs, chunks):
    das, heads, out_ref = refs[1 : 1 + chunks], refs[1 + chunks : -1], refs[-1]
    out_ref[...] = sum_over_chunks(das, heads).astype(BF)


def sum_over_chunks(das, heads):
    rows = das[0].shape[0]
    total = 0.0
    for c, da in enumerate(das):
        right = jnp.concatenate([h[0, c * rows : (c + 1) * rows, :] for h in heads], axis=1)
        total = total + dot(da[...], right, TN)
    return total


def head_specs(half, side):
    return [
        pl.BlockSpec((1, half, 128), lambda i, s, flip=flip: (s[3] ^ flip, 0, 0), pipeline_mode=pl.Buffered(1))
        for flip in (side, side, side + 2, side + 2)
    ]


def out_grads(scalars, das, heads_in):
    rows, depth = das[0].shape
    tile = 256
    return pl.pallas_call(
        functools.partial(out_grads_kernel, chunks=len(das)),
        out_shape=jax.ShapeDtypeStruct((depth, 512), BF),
        grid_spec=pltpu.PrefetchScalarGridSpec(
            num_scalar_prefetch=1,
            grid=(depth // tile,),
            in_specs=[pl.BlockSpec((rows, tile), lambda i, s: (0, i))] * len(das)
            + head_specs(rows * len(das), 1),
            out_specs=pl.BlockSpec((tile, 512), lambda i, s: (i, 0)),
        ),
        compiler_params=pltpu.CompilerParams(vmem_limit_bytes=24 * MIB),
        name="out_grads",
    )(scalars, *das, *heads_in, *heads_in)


def weight_grads_kernel(scalar_ref, cot_ref, *refs, chunks):
    *refs, out_ref = refs
    groups = [refs[3 * k : 3 * k + 3] for k in range(2 * chunks)]
    das, heads, got_ref = refs[6 * chunks : 7 * chunks], refs[7 * chunks : -1], refs[-1]
    rows = groups[0][0].shape[0]
    up = down = 0.0
    for k, (n2, g, du) in enumerate(groups):
        side = scalar_ref[0] if k < chunks else 1 - scalar_ref[0]
        at = pl.multiple_of((side * chunks + k % chunks) * rows, rows)
        up = up + dot(n2[...], du[...], TN)
        down = down + dot(cot_ref[pl.ds(at, rows), :].astype(BF), g[...], TN)
    hidden = up.shape[1]
    out_ref[:, :hidden] = up.astype(BF)
    out_ref[:, hidden : 2 * hidden] = down.astype(BF)
    out_ref[:, 2 * hidden :] = (sum_over_chunks(das, heads) + got_ref[...].astype(F32)).astype(BF)


def weight_grads(scalars, cotangent, own, got, das, heads_in, got_out):
    span, depth = cotangent.shape
    chunks = len(own)
    rows, hidden = own[0][1].shape
    tile = 256
    block = lambda r, at: pl.BlockSpec((r, tile), lambda i, s: (0, i))
    fixed = lambda at: pl.BlockSpec((rows, hidden), lambda i, s: (0, at), pipeline_mode=pl.Buffered(1))
    at = depth // hidden
    specs = ([block(rows, 0), fixed(0), fixed(0)] * chunks) + ([block(rows, 0), fixed(at), fixed(at + 1)] * chunks)
    return pl.pallas_call(
        functools.partial(weight_grads_kernel, chunks=chunks),
        out_shape=jax.ShapeDtypeStruct((depth, 2 * hidden + 512), BF),
        grid_spec=pltpu.PrefetchScalarGridSpec(
            num_scalar_prefetch=1,
            grid=(depth // tile,),
            in_specs=[block(span, 0)]
            + specs
            + [block(rows, 0)] * chunks
            + head_specs(rows * chunks, 0)
            + [pl.BlockSpec((tile, 512), lambda i, s: (i, 0))],
            out_specs=pl.BlockSpec((tile, 2 * hidden + 512), lambda i, s: (i, 0)),
        ),
        compiler_params=pltpu.CompilerParams(vmem_limit_bytes=50 * MIB),
        cost_estimate=cost(2 * span * depth * (2 * hidden + 256), 30 * MIB),
        name="weight_grads",
    )(
        scalars,
        cotangent,
        *[x for group in own for x in group],
        *[x for group in got for x in (group,) * 3],
        *das,
        *heads_in,
        *heads_in,
        got_out,
    )


def qkv_grads_kernel(n_ref, p0_ref, p1_ref, out_ref):
    right = jnp.concatenate([p[k] for k in range(3) for p in (p0_ref, p1_ref)], axis=1)
    out_ref[...] = dot(n_ref[...], right, TN).astype(BF)


def qkv_grads(normed, parts):
    span, depth = normed.shape
    tile = 256
    return pl.pallas_call(
        qkv_grads_kernel,
        out_shape=jax.ShapeDtypeStruct((depth, 768), BF),
        grid=(depth // tile,),
        in_specs=[pl.BlockSpec((span, tile), lambda i: (0, i))] + [whole(p.shape) for p in parts],
        out_specs=pl.BlockSpec((tile, 768), lambda i: (i, 0)),
        compiler_params=pltpu.CompilerParams(vmem_limit_bytes=32 * MIB),
        cost_estimate=cost(2 * span * depth * 768, 10 * MIB),
        name="qkv_grads",
    )(normed, *parts)


def finish_kernel(scalar_ref, *refs, pieces, terms, cuts):
    for k in range(pieces):

        @pl.when(pl.program_id(0) // cuts == k)
        def _():
            total = refs[k * terms][...].astype(F32)
            for ref in refs[k * terms + 1 : (k + 1) * terms]:
                total = total + ref[...].astype(F32)
            refs[-1][...] = total


def finish(scalars, side, pieces, before=(), first=0, whole_pieces=4):
    rows, depth = pieces[0][0].shape
    terms = [x for piece in pieces for x in piece]
    cuts = 4 if len(pieces) == 1 else 1
    tile = rows // cuts
    spec = whole((rows, depth)) if cuts == 1 else pl.BlockSpec((tile, depth), lambda i, s: (i, 0))
    out = pl.pallas_call(
        functools.partial(finish_kernel, pieces=len(pieces), terms=len(pieces[0]), cuts=cuts),
        out_shape=[jax.ShapeDtypeStruct((2 * whole_pieces * rows, depth), F32)],
        grid_spec=pltpu.PrefetchScalarGridSpec(
            num_scalar_prefetch=1,
            grid=(len(pieces) * cuts,),
            in_specs=[spec] * len(terms) + [pl.BlockSpec(memory_space=pl.ANY)] * len(before),
            out_specs=[
                pl.BlockSpec((tile, depth), lambda i, s: ((s[0] ^ side) * whole_pieces * cuts + first + i, 0))
            ],
        ),
        input_output_aliases={1 + len(terms): 0} if before else {},
        compiler_params=pltpu.CompilerParams(vmem_limit_bytes=24 * MIB),
        cost_estimate=cost(0, 8 * rows * depth * len(pieces)),
        name="finish",
    )(scalars, *terms, *before)
    return out[0]


def adam_rows_kernel(g_ref, w_ref, m_ref, v_ref, nm_ref, nv_ref, nw_ref):
    kinds, width = w_ref.shape[1:]
    for k in range(kinds):
        grad = g_ref[:, k * width : (k + 1) * width]
        new = adamw(w_ref[:, k, :], m_ref[:, k, :], v_ref[:, k, :], grad, matrix_rate, weight_decay)
        nm_ref[:, k, :], nv_ref[:, k, :], nw_ref[:, k, :] = new


def adam_turned_kernel(g_ref, w_ref, m_ref, v_ref, nm_ref, nv_ref, nw_ref):
    new = adamw(w_ref[...], m_ref[...], v_ref[...], g_ref[...].T, matrix_rate, weight_decay)
    nm_ref[...], nv_ref[...], nw_ref[...] = new


def adam(kernel, grad, *state):
    return pl.pallas_call(
        kernel,
        out_shape=[jax.ShapeDtypeStruct(state[0].shape, F32)] * 3,
        grid=(1,),
        in_specs=[whole(x.shape) for x in (grad, *state)],
        out_specs=[whole(state[0].shape)] * 3,
        compiler_params=pltpu.CompilerParams(vmem_limit_bytes=24 * MIB),
        cost_estimate=cost(0, 28 * grad.size),
        name="adam",
    )(grad, *state)


def adam_turned(grad, *state):
    if grad.shape[0] % 128:
        return adamw(*state, grad.T.reshape(state[0].shape), matrix_rate, weight_decay)
    flat = [x.reshape(-1, x.shape[-1]) for x in state]
    return [x.reshape(state[0].shape) for x in adam(adam_turned_kernel, grad, *flat)]


def body(
    tokens,
    cotangent,
    lengths,
    qkv_weight,
    qkv_first,
    qkv_second,
    out_weight,
    out_first,
    out_second,
    up_weight,
    up_first,
    up_second,
    down_weight,
    down_first,
    down_second,
    row_vectors,
    row_first,
    row_second,
    col_bias,
    col_first,
    col_second,
):
    span, depth = tokens.shape
    half = span // 2
    share = qkv_weight.shape[0]
    n_dp = lax.axis_size("dp")
    device = lax.axis_index("mp")
    core = device % 2
    heads = qkv_weight.shape[2] // HEAD_DIM
    width = heads * HEAD_DIM
    hidden = up_weight.shape[1] * up_weight.shape[2]
    head_ids = device * heads + jnp.arange(heads)
    slopes = jnp.exp2(-8.0 * (head_ids.astype(F32) + 1.0) / HEADS)
    scalars = jnp.stack([core.astype(jnp.int32), jnp.int32(half), lengths[0], device.astype(jnp.int32)])

    index = ring_index(n_dp)
    out_piece = out_weight.astype(BF).T
    out_piece = jnp.concatenate([out_piece, to_chip(out_piece)], axis=1)
    qkv_ring = Gather(qkv_weight.astype(BF).reshape(share, 3 * width))
    up_piece = up_weight.astype(BF).reshape(share, hidden)
    down_piece = down_weight.astype(BF).reshape(hidden, share).T
    late_piece = jnp.concatenate([out_piece, up_piece, down_piece], axis=1)
    late_w = lax.all_gather(late_piece, "dp", axis=0, tiled=True)
    up_bias = col_bias[2:].reshape(1, hidden)
    up_bias = jnp.concatenate([up_bias, to_core(up_bias)], axis=0)
    for _ in range(n_dp // 2):
        qkv_ring.hop()

    unit_one, _ = norm_parts(tokens.astype(F32))
    normed = (unit_one * row_vectors[0] + row_vectors[1]).astype(BF)
    q, k, v, qkv_w = project(after(normed, up_bias), index, qkv_ring.finish(), col_bias, slopes, lengths)
    outs, heads_in = [], []
    for pair in range(2):
        o, qb, send = attend_forward(q, k, v, pair)
        outs.append((o, qb))
        heads_in.append(to_all(after(send, *heads_in)))
    qkv_sib = to_core(qkv_w)
    late_w = after(late_w, heads_in[1])
    late_sib = to_core(late_w)

    weights = (late_w, after(late_sib, qkv_sib))
    chunks = 1
    pieces = [half * 3 // 8, half * 3 // 8, half // 4]
    *mlps, resid, send, g, du, da, do, sums, up_sums = middle(
        scalars, heads_in, tokens, cotangent, weights, row_vectors, up_bias, pieces
    )
    resids, das = [resid], [da]
    got_send = to_core(send)
    got_out = to_core(out_grads(scalars, das, heads_in))
    partials = [to_all(do)]
    total = weight_grads(scalars, cotangent, [(send, g, du)], [got_send], das, heads_in, got_out)
    total = after(total, *partials)
    mlp_far = [to_chip(after(mlps[0], total))]
    shard = lax.psum_scatter(total, "dp", scatter_dimension=0, tiled=True)

    parts, part_sums, siblings = [], [], []
    for pair in range(2):
        o, qb = outs[pair]
        qb = after(qb, total)
        d, d_sib, s = attend_backward(scalars, qb, k, v, o, partials, pair)
        parts.append(d)
        part_sums.append(s)
        d_sib = after(d_sib, mlp_far[pair])
        if pair == 0:
            outs[1] = (outs[1][0], after(outs[1][1], mlp_far[0], s))
        mlp_far.append(to_chip(after(mlps[pair + 1], mlp_far[pair])))
        siblings.append(to_core(d_sib))
    qkv_wgrad = after(qkv_grads(normed, parts), *siblings)
    qkv_ring = Reduce(qkv_wgrad, index, -1)
    qkv_ring.hop()

    *igs, last_sums = last(
        scalars, parts, siblings, qkv_w, qkv_sib, after(tokens, qkv_wgrad), das[0], row_vectors
    )
    first_gates = (mlp_far[2], qkv_ring.up, qkv_ring.down)
    igs[0], last_sums = after(igs[0], *first_gates), after(last_sums, *first_gates)
    ig_far = [to_chip(igs[0])]
    ig_sib = [to_core(after(x, last_sums)) for x in igs]
    qkv_ring.hop(last_sums)
    valid = ((core * half + jnp.arange(half)) < lengths[0]).astype(F32)[:, None]
    stat_out, stat_m, own_low = 0.0, 0.0, []
    at = 0
    for m, f in zip(mlps, mlp_far):
        rows = slice(at, at + m.shape[0])
        at += m.shape[0]
        branch_m = m.astype(F32) + after(f, last_sums).astype(F32) + row_vectors[5]
        outputs_own = resid[rows].astype(F32) + branch_m
        stat_out += jnp.sum(valid[rows] * outputs_own * outputs_own)
        stat_m += jnp.sum(valid[rows] * branch_m * branch_m)
        own_low.append(outputs_own.astype(BF))
    own_low = jnp.concatenate(own_low, axis=0)
    ig_far.append(to_chip(after(igs[1], ig_far[0], own_low, stat_out, stat_m)))
    qkv_ring.hop(ig_far[0])

    stats = jnp.stack([stat_out, jnp.sum(sums[4]), stat_m, jnp.sum(valid)])
    small = jnp.concatenate(
        [
            last_sums[0:2],
            sums[2:3],
            sums[0:2],
            sums[3:4],
            jnp.pad(stats, (0, depth - 4))[None],
            jnp.pad(
                jnp.concatenate([part_sums[p][kind] for kind in range(2) for p in range(2)]),
                (0, depth - 2 * width),
            )[None],
            up_sums,
        ],
        axis=0,
    )
    rows, columns = small[:7], small[7:9]
    other = to_core(small)
    rows = rows + other[:7]
    columns = jnp.concatenate([columns[:1], columns[1:] + other[9:]], axis=0)
    small = jnp.concatenate([rows, columns], axis=0)
    meet = lambda x, step: x + lax.ppermute(x, "dp", [(i, i ^ step) for i in range(n_dp)])
    outputs = finish(scalars, 0, [[own_low]], (), 0, 1)
    outputs = finish(scalars, 1, [[to_core(own_low)]], (outputs,), 0, 1)
    ig_far.append(to_chip(after(igs[2], ig_far[1], outputs, small)))
    qkv_ring.hop(ig_far[1])
    small = meet(after(small, ig_far[1]), 1)
    ig_cross = [to_core(x) for x in ig_far[:2]]
    front, back = slice(0, 2), slice(2, 4)
    input_grad = finish(scalars, 0, list(zip(igs, ig_far))[front])
    input_grad = finish(scalars, 1, list(zip(ig_sib, ig_cross))[front], (input_grad,))
    ig_far.append(to_chip(after(igs[3], ig_far[2], input_grad, small)))
    qkv_shard = after(qkv_ring.finish(), ig_far[2])
    step = 2
    while step < n_dp:
        small = meet(after(small, *ig_far[2 : step]), step)
        step *= 2
    up_shard = shard[:, :hidden].astype(F32)
    down_shard = shard[:, hidden : 2 * hidden].astype(F32)
    out_mine = shard[:, 2 * hidden : 2 * hidden + width]
    out_theirs = to_chip(shard[:, 2 * hidden + width :])
    out_shard = out_mine.astype(F32) + out_theirs.astype(F32)

    qkv_new = adam(adam_rows_kernel, qkv_shard, qkv_weight, qkv_first, qkv_second)
    out_new = adam_turned(out_shard, out_weight, out_first, out_second)
    up_new = adam(adam_rows_kernel, up_shard, up_weight, up_first, up_second)
    down_new = adam_turned(down_shard, down_weight, down_first, down_second)
    ig_cross += [to_core(x) for x in ig_far[2:]]
    input_grad = after(input_grad, ig_far[3], up_new[0], down_new[0], qkv_new[0])
    input_grad = finish(scalars, 0, list(zip(igs, ig_far))[back], (input_grad,), 2)
    input_grad = finish(scalars, 1, list(zip(ig_sib, ig_cross))[back], (input_grad,), 2)
    rows = small[:7] + to_chip(after(small[:7], ig_far[3], up_new[0], down_new[0], qkv_new[0]))
    small = jnp.concatenate([rows, small[7:]], axis=0)
    row_total, stat_total = small[:6], small[6]
    col_total = jnp.concatenate(
        [small[7, : 2 * width].reshape(2, width), small[8].reshape(-1, width)], axis=0
    )
    rms_stats = jnp.sqrt(stat_total[:3] / (stat_total[3] * depth))

    row_new = adamw(row_vectors, row_first, row_second, row_total, vector_rate, 0.0)
    col_new = adamw(col_bias, col_first, col_second, col_total, vector_rate, 0.0)
    return (
        outputs,
        input_grad,
        rms_stats,
        *qkv_new,
        *out_new,
        *up_new,
        *down_new,
        *row_new,
        *col_new,
    )


def solution(mesh):
    matrices = [P("dp", None, "mp"), P("mp", "dp"), P("dp", None, "mp"), P(None, "mp", "dp")]
    vectors = [P(), P(None, "mp")]
    groups = [spec for spec in matrices + vectors for _ in range(3)]
    return jax.shard_map(
        body,
        mesh=mesh,
        in_specs=(P("dp", None), P("dp", None), P("dp"), *groups),
        out_specs=(P("dp", None), P("dp", None), P(), *groups),
        check_vma=False,
    )
```

```python
import functools

import jax
import jax.numpy as jnp
from jax import lax
from jax.experimental import pallas as pl
from jax.experimental.pallas import tpu as pltpu
from jax.sharding import PartitionSpec as P

HEADS = 16
HEAD_DIM = 64
STEP = 5

norm_eps = 1e-05
masked_score = -1e30
first_decay = 0.5
second_decay = 0.5
matrix_rate = 0.03
vector_rate = 0.4
weight_decay = 0.1
adam_eps = 1e-08
gelu_scale = 0.7978845608028654
gelu_cubic = 0.044715

F32 = jnp.float32
BF = jnp.bfloat16
NN = (((1,), (0,)), ((), ()))
NT = (((1,), (1,)), ((), ()))
TN = (((0,), (0,)), ((), ()))
MIB = 2**20


def dot(a, b, dims=NN):
    return lax.dot_general(a, b, dims, preferred_element_type=F32)


def adamw(weight, moment_one, moment_two, gradient, learn_rate, decay_rate):
    moment_one = first_decay * moment_one + (1.0 - first_decay) * gradient
    moment_two = second_decay * moment_two + (1.0 - second_decay) * gradient * gradient
    correct_one = 1.0 - first_decay**STEP
    correct_two = 1.0 - second_decay**STEP
    direction = moment_one / correct_one / (jnp.sqrt(moment_two / correct_two) + adam_eps)
    return (moment_one, moment_two, weight - learn_rate * (direction + decay_rate * weight))


def to_core(x):
    return lax.ppermute(x, "mp", [(i, i ^ 1) for i in range(lax.axis_size("mp"))])


def to_chip(x):
    return lax.ppermute(x, "mp", [(i, i ^ 2) for i in range(lax.axis_size("mp"))])


def to_all(x):
    return lax.all_to_all(x, "mp", split_axis=0, concat_axis=0, tiled=True)


def ring_order(n):
    return [0, 2, 4, 6, 7, 5, 3, 1] if n == 8 else list(range(n))


def ring_perms(n):
    order = ring_order(n)
    up = [(order[p], order[(p + 1) % n]) for p in range(n)]
    down = [(order[p], order[(p - 1) % n]) for p in range(n)]
    return up, down


def ring_index(n):
    order = ring_order(n)
    place = jnp.array([order.index(i) for i in range(n)], jnp.int32)[lax.axis_index("dp")]
    return jnp.array(order, jnp.int32)[(place + jnp.arange(n)) % n]


class Gather:
    def __init__(self, piece, turn=1):
        self.n = lax.axis_size("dp")
        self.perms = ring_perms(self.n)[::turn]
        self.turn = turn
        self.pieces = [piece] + [None] * (self.n - 1)
        self.up = self.down = piece
        self.done = 0

    def hop(self, *gates):
        if self.done == self.n // 2:
            return
        self.done += 1
        self.up = self.pieces[-self.turn * self.done % self.n] = lax.ppermute(after(self.up, *gates), "dp", self.perms[0])
        if self.done <= (self.n - 1) // 2:
            self.down = self.pieces[self.turn * self.done % self.n] = lax.ppermute(after(self.down, *gates), "dp", self.perms[1])

    def finish(self):
        while self.done < self.n // 2:
            self.hop()
        return self.pieces


class Reduce:
    def __init__(self, total, index, turn=1):
        self.n = lax.axis_size("dp")
        self.perms = ring_perms(self.n)[::turn]
        self.turn = turn
        self.total, self.index = total, index
        self.rows = total.shape[0] // self.n
        self.up = self.down = None
        self.done = 0

    def block(self, k):
        return lax.dynamic_slice_in_dim(self.total, self.index[self.turn * k % self.n] * self.rows, self.rows, 0)

    def add(self, x, k):
        if x is None:
            return self.block(k)
        return (x.astype(F32) + self.block(k).astype(F32)).astype(BF)

    def hop(self, *gates):
        ups, downs = self.n // 2, (self.n - 1) // 2
        if self.done == ups:
            return
        up = after(self.add(self.up, ups - self.done), *gates)
        if self.done < downs:
            down = after(self.add(self.down, self.done - downs), *gates)
            self.down = lax.ppermute(down, "dp", self.perms[1])
        self.up = lax.ppermute(up, "dp", self.perms[0])
        self.done += 1

    def finish(self):
        while self.done < self.n // 2:
            self.hop()
        return self.block(0).astype(F32) + self.up.astype(F32) + self.down.astype(F32)


def after(x, *others):
    return lax.optimization_barrier((x, *others))[0] if others else x


def cost(flops, nbytes):
    return pl.CostEstimate(flops=int(flops), bytes_accessed=int(nbytes), transcendentals=0)


def whole(shape):
    return pl.BlockSpec(shape, lambda *_: (0,) * len(shape), pipeline_mode=pl.Buffered(1))


def assemble_kernel(index_ref, pieces, out_ref, at):
    rows, cols = pieces[0].shape
    for k, piece in enumerate(pieces):
        row = pl.multiple_of(index_ref[k] * rows, rows)
        out_ref[pl.ds(row, rows), at : at + cols] = piece[...]


def split3(x):
    hi = x.astype(BF).astype(F32)
    rest = x - hi
    mid = rest.astype(BF).astype(F32)
    return hi, mid, rest - mid


def put3(base, lane, first, x):
    hi, mid, lo = split3(x)
    return jnp.where(
        lane == first,
        hi,
        jnp.where(lane == first + 1, mid, jnp.where(lane == first + 2, lo, base)),
    )


def project_kernel(index_ref, slope_ref, length_ref, n_ref, bias_ref, *refs, heads):
    *pieces, q_ref, k_ref, v_ref, w_ref = refs

    @pl.when(pl.program_id(0) == 0)
    def _():
        assemble_kernel(index_ref, pieces, w_ref, 0)

    rows = n_ref.shape[0]
    width = heads * HEAD_DIM
    out = dot(n_ref[...], w_ref[...])
    query = (out[:, :width] + bias_ref[0:1, :]).astype(BF).astype(F32) * (HEAD_DIM**-0.5)
    key = out[:, width : 2 * width]
    value = out[:, 2 * width :] + bias_ref[1:2, :]
    lane = lax.broadcasted_iota(jnp.int32, (rows, 128), 1)
    at = lax.broadcasted_iota(jnp.int32, (rows, 128), 0) + pl.program_id(0) * rows
    ones = ((lane >= 64) & (lane < 67)).astype(F32)
    more = ((lane >= 67) & (lane < 70)).astype(F32)
    seen = at < length_ref[0]
    zero = jnp.zeros((rows, 64), F32)
    for h in range(heads):
        cols = slice(h * HEAD_DIM, (h + 1) * HEAD_DIM)
        slope = jnp.where(seen, at.astype(F32) * slope_ref[h], masked_score)
        q_ref[h] = (jnp.concatenate([query[:, cols], zero], axis=1) + ones).astype(BF)
        wide = jnp.concatenate([key[:, cols], zero], axis=1) + more
        k_ref[h] = put3(wide, lane, 64, slope).astype(BF)
        v_ref[h] = (jnp.concatenate([value[:, cols], zero], axis=1) + ones).astype(BF)


def project(normed, index, pieces, col_bias, slopes, length):
    span, depth = normed.shape
    cols = pieces[0].shape[1]
    heads = slopes.shape[0]
    tile = 256
    shape = jax.ShapeDtypeStruct((heads, span, 128), BF)
    return pl.pallas_call(
        functools.partial(project_kernel, heads=heads),
        out_shape=(shape,) * 3 + (jax.ShapeDtypeStruct((depth, cols), BF),),
        grid=(span // tile,),
        in_specs=[pl.BlockSpec(memory_space=pltpu.SMEM)] * 3
        + [pl.BlockSpec((tile, depth), lambda i: (i, 0)), whole(col_bias.shape)]
        + [whole(piece.shape) for piece in pieces],
        out_specs=[pl.BlockSpec((heads, tile, 128), lambda i: (0, i, 0))] * 3
        + [whole((depth, cols))],
        compiler_params=pltpu.CompilerParams(vmem_limit_bytes=40 * MIB),
        cost_estimate=cost(2 * span * depth * cols, 12 * MIB),
        name="project",
    )(index, slopes, length, normed, col_bias, *pieces)


def attend_forward_kernel(q_ref, k_ref, v_ref, o_ref, qb_ref, send_ref, *, bq, span):
    lane = lax.broadcasted_iota(jnp.int32, (bq, 128), 1)
    row = lax.broadcasted_iota(jnp.int32, (bq, bq), 0)
    causal = row >= lax.broadcasted_iota(jnp.int32, (bq, bq), 1)
    for i in range(span // bq):
        outs = []
        here = pl.ds(i * bq, bq)
        for h in range(2):
            q = q_ref[h, here, :]
            near = jnp.where(causal, dot(q, k_ref[h, here, :], NT), masked_score)
            highest = jnp.max(near, axis=1, keepdims=True)
            if i:
                before = pl.ds(0, i * bq)
                far = dot(q, k_ref[h, before, :], NT)
                highest = jnp.maximum(highest, jnp.max(far, axis=1, keepdims=True))
            acc = dot(jnp.exp(near - highest).astype(BF), v_ref[h, here, :])
            if i:
                acc = acc + dot(jnp.exp(far - highest).astype(BF), v_ref[h, before, :])
            total = acc[:, 64:65]
            outs.append((acc[:, :64] * (1.0 / total)).astype(BF))
            log_sum = highest + jnp.log(total)
            qb_ref[h, here, :] = put3(q.astype(F32), lane, 67, -log_sum).astype(BF)
        o_ref[here, :] = jnp.concatenate(outs, axis=1)
    half = span // 2
    for j in range(4):
        send_ref[j] = o_ref[pl.ds(j % 2 * half, half), :]


def pair_spec(span, pair):
    return pl.BlockSpec((2, span, 128), lambda i: (pair, 0, 0), pipeline_mode=pl.Buffered(1))


def attend_forward(q, k, v, pair):
    span = q.shape[1]
    shapes = [(span, 128), (2, span, 128), (4, span // 2, 128)]
    return pl.pallas_call(
        functools.partial(attend_forward_kernel, bq=min(512, span), span=span),
        out_shape=[jax.ShapeDtypeStruct(x, BF) for x in shapes],
        grid=(1,),
        in_specs=[pair_spec(span, pair)] * 3,
        out_specs=[whole(x) for x in shapes],
        compiler_params=pltpu.CompilerParams(vmem_limit_bytes=60 * MIB),
        cost_estimate=cost(12e9, 5 * MIB),
        name="attend_forward",
    )(q, k, v)


def attend_backward_kernel(half_ref, q_ref, k_ref, v_ref, o_ref, *refs, bk, span, chunks):
    partials, (d_ref, sib_ref, sum_ref, do_ref, doa_ref, dq_ref) = refs[:-6], refs[-6:]
    half = span // 2
    rows = half // chunks
    for c, part in enumerate(partials):
        for side in range(2):
            total = part[side].astype(F32) + part[2 + side].astype(F32)
            do_ref[pl.ds(side * half + c * rows, rows), :] = total.astype(BF)
    lane = lax.broadcasted_iota(jnp.int32, (span, 128), 1)
    row = lax.broadcasted_iota(jnp.int32, (bk, bk), 0)
    causal = row <= lax.broadcasted_iota(jnp.int32, (bk, bk), 1)
    grad = do_ref[...].astype(F32)
    prod = grad * o_ref[...].astype(F32)
    for h in range(2):
        cols = slice(h * HEAD_DIM, (h + 1) * HEAD_DIM)
        delta = jnp.sum(prod[:, cols], axis=1, keepdims=True)
        base = jnp.concatenate([grad[:, cols], jnp.zeros((span, 64), F32)], axis=1)
        doa_ref[h] = put3(base, lane, 64, -delta).astype(BF)
    dq_ref[...] = jnp.zeros_like(dq_ref)
    value_sums = jnp.zeros((1, 128), F32)
    for j in range(span // bk):
        dks, dvs = [], []
        here = pl.ds(j * bk, bk)
        rest = pl.ds(j * bk, span - j * bk)
        for h in range(2):
            k = k_ref[h, here, :]
            q = q_ref[h, rest, :]
            do = doa_ref[h, rest, :]
            p = jnp.exp(dot(k, q, NT))
            near = jnp.where(causal, p[:, :bk], 0.0)
            p = jnp.concatenate([near, p[:, bk:]], axis=1) if rest.size > bk else near
            ds = (p * dot(v_ref[h, here, :], do, NT)).astype(BF)
            dvs.append(dot(p.astype(BF), do)[:, :64])
            dks.append(dot(ds, q)[:, :64])
            dq_ref[h, :, rest] += dot(k[:, :64], ds, TN)
        d_ref[1, here, :] = jnp.concatenate(dks, axis=1).astype(BF)
        value_grad = jnp.concatenate(dvs, axis=1).astype(BF)
        d_ref[2, here, :] = value_grad
        value_sums += jnp.sum(value_grad.astype(F32), axis=0, keepdims=True)
    dq = jnp.concatenate([dq_ref[0], dq_ref[1]], axis=0).T * (HEAD_DIM**-0.5)
    dq = dq.astype(BF)
    d_ref[0] = dq
    sum_ref[0:1, :] = jnp.sum(dq.astype(F32), axis=0, keepdims=True)
    sum_ref[1:2, :] = value_sums
    for kind in range(3):
        sib_ref[kind] = d_ref[kind, pl.ds(pl.multiple_of((1 - half_ref[0]) * half, half), half), :]


def attend_backward(scalars, qb, k, v, o, partials, pair):
    span = qb.shape[1]
    chunks = len(partials)
    part = pl.BlockSpec((4, span // 2 // chunks, 128), lambda i: (0, 0, pair), pipeline_mode=pl.Buffered(1))
    shapes = [((3, span, 128), BF), ((3, span // 2, 128), BF), ((2, 128), F32)]
    return pl.pallas_call(
        functools.partial(attend_backward_kernel, bk=min(256, span), span=span, chunks=chunks),
        out_shape=[jax.ShapeDtypeStruct(*x) for x in shapes],
        grid=(1,),
        in_specs=[
            pl.BlockSpec(memory_space=pltpu.SMEM),
            pair_spec(span, 0),
            pair_spec(span, pair),
            pair_spec(span, pair),
            whole((span, 128)),
        ]
        + [part] * chunks,
        out_specs=[whole(x[0]) for x in shapes],
        scratch_shapes=[
            pltpu.VMEM((span, 128), BF),
            pltpu.VMEM((2, span, 128), BF),
            pltpu.VMEM((2, 64, span), F32),
        ],
        compiler_params=pltpu.CompilerParams(vmem_limit_bytes=60 * MIB),
        cost_estimate=cost(18e9, 6 * MIB),
        name="attend_backward",
    )(scalars, qb, k, v, o, *partials)


def norm_parts(x):
    average = jnp.mean(x, axis=-1, keepdims=True)
    centred = x - average
    variance = jnp.mean(centred * centred, axis=-1, keepdims=True)
    scale = lax.rsqrt(variance + norm_eps)
    return centred * scale, scale


def norm_back(grad, unit, scale, gain):
    weighted = grad * gain
    mean_one = jnp.mean(weighted, axis=-1, keepdims=True)
    mean_two = jnp.mean(weighted * unit, axis=-1, keepdims=True)
    return scale * (weighted - mean_one - unit * mean_two)


def middle_kernel(
    scalar_ref,
    o0_ref,
    o1_ref,
    tokens_ref,
    cot_ref,
    late_own_ref,
    late_sib_ref,
    row_ref,
    bias_ref,
    *refs,
    chunk,
):
    (*mlp_refs, resid_ref, send_ref, g_ref, du_ref, da_ref, do_ref, sum_ref, up_sum_ref, out_w) = refs
    step = pl.program_id(0)
    tile, depth = tokens_ref.shape

    @pl.when(step == 0)
    def _():
        for k, ref in enumerate((late_own_ref, late_sib_ref)):
            for chip in range(2):
                for pair in range(2):
                    at = (pair * 4 + (scalar_ref[3] ^ (k + 2 * chip))) * 128
                    cols = slice(256 * chip + 128 * pair, 256 * chip + 128 * (pair + 1))
                    out_w[:, pl.ds(pl.multiple_of(at, 128), 128)] = ref[:, cols]
        sum_ref[...] = jnp.zeros_like(sum_ref)
        up_sum_ref[...] = jnp.zeros_like(up_sum_ref)

    heads = jnp.concatenate([ref[j] for ref in (o0_ref, o1_ref) for j in range(4)], axis=1)
    branch = dot(heads, out_w[...], NT) + row_ref[2:3, :]
    resid = tokens_ref[...].astype(F32) + branch
    resid_ref[...] = resid.astype(BF)
    at = lax.broadcasted_iota(jnp.int32, (tile, 1), 0) + (
        scalar_ref[0] * scalar_ref[1] + (chunk * pl.num_programs(0) + step) * tile
    )
    valid = (at < scalar_ref[2]).astype(F32)
    unit, scale = norm_parts(resid)
    n2 = (unit * row_ref[3:4, :] + row_ref[4:5, :]).astype(BF)
    send_ref[:, :depth] = n2
    cot = cot_ref[...]
    dm = cot.astype(BF)
    mlp = None
    hid = (late_own_ref.shape[1] - 512) // 2
    for half, late in enumerate((late_own_ref, late_sib_ref)):
        up, down = late.at[:, 512 : 512 + hid], late.at[:, 512 + hid :]
        u = dot(n2, up[...]) + bias_ref[half : half + 1, :]
        square = u * u
        t = jnp.tanh(gelu_scale * (u + gelu_cubic * square * u))
        plus = 0.5 * (1.0 + t)
        g = (u * plus).astype(BF)
        slope = plus + (0.5 * gelu_scale) * u * (1.0 - t * t) * (1.0 + 3.0 * gelu_cubic * square)
        du_wide = (dot(dm, down[...]) * slope).astype(BF)
        if half == 0:
            g_ref[...] = g
            du_ref[...] = du_wide
        else:
            send_ref[:, depth : depth + hid] = g
            send_ref[:, depth + hid :] = du_wide
        up_sum_ref[half : half + 1, :] += jnp.sum(du_wide.astype(F32), axis=0, keepdims=True)
        m = dot(g, down[...], NT)
        d = dot(du_wide, up[...], NT)
        mlp, dn2 = (m, d) if mlp is None else (mlp + m, dn2 + d)
    mlp = mlp.astype(BF)
    start = 0
    for ref in mlp_refs:
        stop = start + ref.shape[0]
        for k in range(start // tile, (stop - 1) // tile + 1):
            low, high = max(start, k * tile), min(stop, (k + 1) * tile)

            @pl.when(step == k)
            def _(ref=ref, at=low - start, low=low - k * tile, size=high - low):
                ref[at : at + size, :] = mlp[low : low + size, :]

        start = stop
    dr = norm_back(dn2, unit, scale, row_ref[3:4, :]) + 0.5 * cot
    da = dr.astype(BF)
    da_ref[...] = da
    do = dot(da, out_w[...]).astype(BF)
    for j in range(4):
        do_ref[j] = jnp.concatenate([do[:, 128 * (j + 4 * p) : 128 * (j + 4 * p + 1)] for p in range(2)], axis=1)
    for k, x in enumerate(
        (dn2 * unit, dn2, da.astype(F32), 0.5 * dm.astype(F32), valid * branch * branch)
    ):
        sum_ref[k : k + 1, :] += jnp.sum(x, axis=0, keepdims=True)


def middle(scalars, heads_in, tokens, cotangent, weights, row_vectors, up_bias, pieces):
    depth = tokens.shape[1]
    half = tokens.shape[0] // 2
    tile = 256
    chunk, chunks = 0, 1
    steps = half // tile
    hidden = weights[0].shape[1] - 512
    own = lambda i, s: (chunk * steps + i, 0)
    absolute = lambda i, s: (s[0] * (half // tile) + chunk * steps + i, 0)
    part = lambda i, s: (i, 0)
    parts = [(depth, BF), (depth + hidden, BF), (hidden // 2, BF), (hidden // 2, BF), (depth, BF)]
    return pl.pallas_call(
        functools.partial(middle_kernel, chunk=chunk),
        out_shape=[jax.ShapeDtypeStruct((rows, depth), BF) for rows in pieces]
        + [jax.ShapeDtypeStruct((half // chunks, w), t) for w, t in parts]
        + [jax.ShapeDtypeStruct((4, half // chunks, 256), BF)]
        + [jax.ShapeDtypeStruct((8, depth), F32), jax.ShapeDtypeStruct((2, hidden // 2), F32)],
        grid_spec=pltpu.PrefetchScalarGridSpec(
            num_scalar_prefetch=1,
            grid=(steps,),
            in_specs=[pl.BlockSpec((4, tile, 128), lambda i, s: (0, *own(i, s)))] * 2
            + [pl.BlockSpec((tile, depth), absolute)] * 2
            + [whole(w.shape) for w in weights]
            + [whole(row_vectors.shape), whole(up_bias.shape)],
            out_specs=[whole((rows, depth)) for rows in pieces]
            + [pl.BlockSpec((tile, w), part) for w, _ in parts]
            + [pl.BlockSpec((4, tile, 256), lambda i, s: (0, i, 0))]
            + [whole((8, depth)), whole((2, hidden // 2))],
            scratch_shapes=[
                pltpu.VMEM((depth, 1024), BF),
            ],
        ),
        compiler_params=pltpu.CompilerParams(vmem_limit_bytes=56 * MIB),
        cost_estimate=cost(21e9 / chunks, 24 * MIB),
        name="middle",
    )(scalars, *heads_in, tokens, cotangent, *weights, row_vectors, up_bias)


def last_kernel(
    scalar_ref, o0_ref, o1_ref, s0_ref, s1_ref, w_own_ref, w_sib_ref, tokens_ref, *refs
):
    da_ref, row_ref, *ig_refs, sum_ref = refs
    step = pl.program_id(0)

    @pl.when(step == 0)
    def _():
        sum_ref[...] = jnp.zeros_like(sum_ref)

    def side(x, y):
        return jnp.concatenate([r[k] for k in range(3) for r in (x, y)], axis=1)

    dn1 = dot(side(o0_ref, o1_ref), w_own_ref[...], NT) + dot(side(s0_ref, s1_ref), w_sib_ref[...], NT)
    unit, scale = norm_parts(tokens_ref[...].astype(F32))
    ig = (da_ref[...].astype(F32) + norm_back(dn1, unit, scale, row_ref[0:1, :])).astype(BF)
    for k, ref in enumerate(ig_refs):

        @pl.when(step == k)
        def _(ref=ref):
            ref[...] = ig

    sum_ref[0:1, :] += jnp.sum(dn1 * unit, axis=0, keepdims=True)
    sum_ref[1:2, :] += jnp.sum(dn1, axis=0, keepdims=True)


def last(scalars, own, sibling, w_own, w_sib, tokens, da, row_vectors):
    depth = tokens.shape[1]
    half = tokens.shape[0] // 2
    steps = 4
    tile = half // steps
    absolute = lambda i, s: (s[0] * steps + i, 0)
    return pl.pallas_call(
        last_kernel,
        out_shape=[jax.ShapeDtypeStruct((tile, depth), BF)] * steps + [jax.ShapeDtypeStruct((8, depth), F32)],
        grid_spec=pltpu.PrefetchScalarGridSpec(
            num_scalar_prefetch=1,
            grid=(steps,),
            in_specs=[pl.BlockSpec((3, tile, 128), lambda i, s: (0, *absolute(i, s)))] * 2
            + [pl.BlockSpec((3, tile, 128), lambda i, s: (0, i, 0))] * 2
            + [whole(w_own.shape), whole(w_sib.shape), pl.BlockSpec((tile, depth), absolute)]
            + [pl.BlockSpec((tile, depth), lambda i, s: (i, 0))]
            + [whole(row_vectors.shape)],
            out_specs=[
                *[whole((tile, depth))] * steps,
                whole((8, depth)),
            ],
        ),
        compiler_params=pltpu.CompilerParams(vmem_limit_bytes=40 * MIB),
        cost_estimate=cost(3.2e9, 20 * MIB),
        name="last",
    )(scalars, *own, *sibling, w_own, w_sib, tokens, da, row_vectors)


def out_grads_kernel(*refs, chunks):
    das, heads, out_ref = refs[1 : 1 + chunks], refs[1 + chunks : -1], refs[-1]
    out_ref[...] = sum_over_chunks(das, heads).astype(BF)


def sum_over_chunks(das, heads):
    rows = das[0].shape[0]
    total = 0.0
    for c, da in enumerate(das):
        right = jnp.concatenate([h[0, c * rows : (c + 1) * rows, :] for h in heads], axis=1)
        total = total + dot(da[...], right, TN)
    return total


def head_specs(half, side):
    return [
        pl.BlockSpec((1, half, 128), lambda i, s, flip=flip: (s[3] ^ flip, 0, 0), pipeline_mode=pl.Buffered(1))
        for flip in (side, side, side + 2, side + 2)
    ]


def out_grads(scalars, das, heads_in):
    rows, depth = das[0].shape
    tile = 256
    return pl.pallas_call(
        functools.partial(out_grads_kernel, chunks=len(das)),
        out_shape=jax.ShapeDtypeStruct((depth, 512), BF),
        grid_spec=pltpu.PrefetchScalarGridSpec(
            num_scalar_prefetch=1,
            grid=(depth // tile,),
            in_specs=[pl.BlockSpec((rows, tile), lambda i, s: (0, i))] * len(das)
            + head_specs(rows * len(das), 1),
            out_specs=pl.BlockSpec((tile, 512), lambda i, s: (i, 0)),
        ),
        compiler_params=pltpu.CompilerParams(vmem_limit_bytes=24 * MIB),
        name="out_grads",
    )(scalars, *das, *heads_in, *heads_in)


def weight_grads_kernel(scalar_ref, cot_ref, *refs, chunks):
    *refs, out_ref = refs
    groups = [refs[3 * k : 3 * k + 3] for k in range(2 * chunks)]
    das, heads, got_ref = refs[6 * chunks : 7 * chunks], refs[7 * chunks : -1], refs[-1]
    rows = groups[0][0].shape[0]
    up = down = 0.0
    for k, (n2, g, du) in enumerate(groups):
        side = scalar_ref[0] if k < chunks else 1 - scalar_ref[0]
        at = pl.multiple_of((side * chunks + k % chunks) * rows, rows)
        up = up + dot(n2[...], du[...], TN)
        down = down + dot(cot_ref[pl.ds(at, rows), :].astype(BF), g[...], TN)
    hidden = up.shape[1]
    out_ref[:, :hidden] = up.astype(BF)
    out_ref[:, hidden : 2 * hidden] = down.astype(BF)
    out_ref[:, 2 * hidden :] = (sum_over_chunks(das, heads) + got_ref[...].astype(F32)).astype(BF)


def weight_grads(scalars, cotangent, own, got, das, heads_in, got_out):
    span, depth = cotangent.shape
    chunks = len(own)
    rows, hidden = own[0][1].shape
    tile = 256
    block = lambda r, at: pl.BlockSpec((r, tile), lambda i, s: (0, i))
    fixed = lambda at: pl.BlockSpec((rows, hidden), lambda i, s: (0, at), pipeline_mode=pl.Buffered(1))
    at = depth // hidden
    specs = ([block(rows, 0), fixed(0), fixed(0)] * chunks) + ([block(rows, 0), fixed(at), fixed(at + 1)] * chunks)
    return pl.pallas_call(
        functools.partial(weight_grads_kernel, chunks=chunks),
        out_shape=jax.ShapeDtypeStruct((depth, 2 * hidden + 512), BF),
        grid_spec=pltpu.PrefetchScalarGridSpec(
            num_scalar_prefetch=1,
            grid=(depth // tile,),
            in_specs=[block(span, 0)]
            + specs
            + [block(rows, 0)] * chunks
            + head_specs(rows * chunks, 0)
            + [pl.BlockSpec((tile, 512), lambda i, s: (i, 0))],
            out_specs=pl.BlockSpec((tile, 2 * hidden + 512), lambda i, s: (i, 0)),
        ),
        compiler_params=pltpu.CompilerParams(vmem_limit_bytes=60 * MIB),
        cost_estimate=cost(2 * span * depth * (2 * hidden + 256), 30 * MIB),
        name="weight_grads",
    )(
        scalars,
        cotangent,
        *[x for group in own for x in group],
        *[x for group in got for x in (group,) * 3],
        *das,
        *heads_in,
        *heads_in,
        got_out,
    )


def qkv_grads_kernel(n_ref, p0_ref, p1_ref, out_ref):
    right = jnp.concatenate([p[k] for k in range(3) for p in (p0_ref, p1_ref)], axis=1)
    out_ref[...] = dot(n_ref[...], right, TN).astype(BF)


def qkv_grads(normed, parts):
    span, depth = normed.shape
    tile = 256
    return pl.pallas_call(
        qkv_grads_kernel,
        out_shape=jax.ShapeDtypeStruct((depth, 768), BF),
        grid=(depth // tile,),
        in_specs=[pl.BlockSpec((span, tile), lambda i: (0, i))] + [whole(p.shape) for p in parts],
        out_specs=pl.BlockSpec((tile, 768), lambda i: (i, 0)),
        compiler_params=pltpu.CompilerParams(vmem_limit_bytes=32 * MIB),
        cost_estimate=cost(2 * span * depth * 768, 10 * MIB),
        name="qkv_grads",
    )(normed, *parts)


def finish_kernel(scalar_ref, *refs, pieces, terms, cuts):
    for k in range(pieces):

        @pl.when(pl.program_id(0) // cuts == k)
        def _():
            total = refs[k * terms][...].astype(F32)
            for ref in refs[k * terms + 1 : (k + 1) * terms]:
                total = total + ref[...].astype(F32)
            refs[-1][...] = total


def finish(scalars, side, pieces, before=(), first=0, whole_pieces=4):
    rows, depth = pieces[0][0].shape
    terms = [x for piece in pieces for x in piece]
    cuts = 4 if len(pieces) == 1 else 1
    tile = rows // cuts
    spec = whole((rows, depth)) if cuts == 1 else pl.BlockSpec((tile, depth), lambda i, s: (i, 0))
    out = pl.pallas_call(
        functools.partial(finish_kernel, pieces=len(pieces), terms=len(pieces[0]), cuts=cuts),
        out_shape=[jax.ShapeDtypeStruct((2 * whole_pieces * rows, depth), F32)],
        grid_spec=pltpu.PrefetchScalarGridSpec(
            num_scalar_prefetch=1,
            grid=(len(pieces) * cuts,),
            in_specs=[spec] * len(terms) + [pl.BlockSpec(memory_space=pl.ANY)] * len(before),
            out_specs=[
                pl.BlockSpec((tile, depth), lambda i, s: ((s[0] ^ side) * whole_pieces * cuts + first + i, 0))
            ],
        ),
        input_output_aliases={1 + len(terms): 0} if before else {},
        compiler_params=pltpu.CompilerParams(vmem_limit_bytes=24 * MIB),
        cost_estimate=cost(0, 8 * rows * depth * len(pieces)),
        name="finish",
    )(scalars, *terms, *before)
    return out[0]


def adam_rows_kernel(g_ref, w_ref, m_ref, v_ref, nm_ref, nv_ref, nw_ref):
    kinds, width = w_ref.shape[1:]
    for k in range(kinds):
        grad = g_ref[:, k * width : (k + 1) * width]
        new = adamw(w_ref[:, k, :], m_ref[:, k, :], v_ref[:, k, :], grad, matrix_rate, weight_decay)
        nm_ref[:, k, :], nv_ref[:, k, :], nw_ref[:, k, :] = new


def adam_turned_kernel(g_ref, w_ref, m_ref, v_ref, nm_ref, nv_ref, nw_ref):
    new = adamw(w_ref[...], m_ref[...], v_ref[...], g_ref[...].T, matrix_rate, weight_decay)
    nm_ref[...], nv_ref[...], nw_ref[...] = new


def adam(kernel, grad, *state):
    return pl.pallas_call(
        kernel,
        out_shape=[jax.ShapeDtypeStruct(state[0].shape, F32)] * 3,
        grid=(1,),
        in_specs=[whole(x.shape) for x in (grad, *state)],
        out_specs=[whole(state[0].shape)] * 3,
        compiler_params=pltpu.CompilerParams(vmem_limit_bytes=24 * MIB),
        cost_estimate=cost(0, 28 * grad.size),
        name="adam",
    )(grad, *state)


def adam_turned(grad, *state):
    if grad.shape[0] % 128:
        return adamw(*state, grad.T.reshape(state[0].shape), matrix_rate, weight_decay)
    flat = [x.reshape(-1, x.shape[-1]) for x in state]
    return [x.reshape(state[0].shape) for x in adam(adam_turned_kernel, grad, *flat)]


def body(
    tokens,
    cotangent,
    lengths,
    qkv_weight,
    qkv_first,
    qkv_second,
    out_weight,
    out_first,
    out_second,
    up_weight,
    up_first,
    up_second,
    down_weight,
    down_first,
    down_second,
    row_vectors,
    row_first,
    row_second,
    col_bias,
    col_first,
    col_second,
):
    span, depth = tokens.shape
    half = span // 2
    share = qkv_weight.shape[0]
    n_dp = lax.axis_size("dp")
    device = lax.axis_index("mp")
    core = device % 2
    heads = qkv_weight.shape[2] // HEAD_DIM
    width = heads * HEAD_DIM
    hidden = up_weight.shape[1] * up_weight.shape[2]
    head_ids = device * heads + jnp.arange(heads)
    slopes = jnp.exp2(-8.0 * (head_ids.astype(F32) + 1.0) / HEADS)
    scalars = jnp.stack([core.astype(jnp.int32), jnp.int32(half), lengths[0], device.astype(jnp.int32)])

    index = ring_index(n_dp)
    out_piece = out_weight.astype(BF).T
    out_piece = jnp.concatenate([out_piece, to_chip(out_piece)], axis=1)
    qkv_ring = Gather(qkv_weight.astype(BF).reshape(share, 3 * width))
    up_piece = up_weight.astype(BF).reshape(share, hidden)
    down_piece = down_weight.astype(BF).reshape(hidden, share).T
    late_piece = jnp.concatenate([out_piece, up_piece, down_piece], axis=1)
    late_w = lax.all_gather(late_piece, "dp", axis=0, tiled=True)
    up_bias = col_bias[2:].reshape(1, hidden)
    up_bias = jnp.concatenate([up_bias, to_core(up_bias)], axis=0)
    for _ in range(n_dp // 2):
        qkv_ring.hop()

    unit_one, _ = norm_parts(tokens.astype(F32))
    normed = (unit_one * row_vectors[0] + row_vectors[1]).astype(BF)
    q, k, v, qkv_w = project(after(normed, up_bias), index, qkv_ring.finish(), col_bias, slopes, lengths)
    outs, heads_in = [], []
    for pair in range(2):
        o, qb, send = attend_forward(q, k, v, pair)
        outs.append((o, qb))
        heads_in.append(to_all(after(send, *heads_in)))
    qkv_sib = to_core(qkv_w)
    late_w = after(late_w, heads_in[1])
    late_sib = to_core(late_w)

    weights = (late_w, after(late_sib, qkv_sib))
    chunks = 1
    pieces = [half * 3 // 8, half * 3 // 8, half // 4]
    *mlps, resid, send, g, du, da, do, sums, up_sums = middle(
        scalars, heads_in, tokens, cotangent, weights, row_vectors, up_bias, pieces
    )
    resids, das = [resid], [da]
    got_send = to_core(send)
    got_out = to_core(out_grads(scalars, das, heads_in))
    partials = [to_all(do)]
    total = weight_grads(scalars, cotangent, [(send, g, du)], [got_send], das, heads_in, got_out)
    total = after(total, *partials)
    mlp_far = [to_chip(after(mlps[0], total))]
    shard = lax.psum_scatter(total, "dp", scatter_dimension=0, tiled=True)

    parts, part_sums, siblings = [], [], []
    for pair in range(2):
        o, qb = outs[pair]
        qb = after(qb, total)
        d, d_sib, s = attend_backward(scalars, qb, k, v, o, partials, pair)
        parts.append(d)
        part_sums.append(s)
        d_sib = after(d_sib, mlp_far[pair])
        if pair == 0:
            outs[1] = (outs[1][0], after(outs[1][1], mlp_far[0], s))
        mlp_far.append(to_chip(after(mlps[pair + 1], mlp_far[pair])))
        siblings.append(to_core(d_sib))
    qkv_wgrad = after(qkv_grads(normed, parts), *siblings)
    qkv_ring = Reduce(qkv_wgrad, index, -1)
    qkv_ring.hop()

    *igs, last_sums = last(
        scalars, parts, siblings, qkv_w, qkv_sib, after(tokens, qkv_wgrad), das[0], row_vectors
    )
    first_gates = (mlp_far[2], qkv_ring.up, qkv_ring.down)
    igs[0], last_sums = after(igs[0], *first_gates), after(last_sums, *first_gates)
    ig_far = [to_chip(igs[0])]
    ig_sib = [to_core(after(x, last_sums)) for x in igs]
    qkv_ring.hop(last_sums)
    valid = ((core * half + jnp.arange(half)) < lengths[0]).astype(F32)[:, None]
    stat_out, stat_m, own_low = 0.0, 0.0, []
    at = 0
    for m, f in zip(mlps, mlp_far):
        rows = slice(at, at + m.shape[0])
        at += m.shape[0]
        branch_m = m.astype(F32) + after(f, last_sums).astype(F32) + row_vectors[5]
        outputs_own = resid[rows].astype(F32) + branch_m
        stat_out += jnp.sum(valid[rows] * outputs_own * outputs_own)
        stat_m += jnp.sum(valid[rows] * branch_m * branch_m)
        own_low.append(outputs_own.astype(BF))
    own_low = jnp.concatenate(own_low, axis=0)
    ig_far.append(to_chip(after(igs[1], ig_far[0], own_low, stat_out, stat_m)))
    qkv_ring.hop(ig_far[0])

    stats = jnp.stack([stat_out, jnp.sum(sums[4]), stat_m, jnp.sum(valid)])
    small = jnp.concatenate(
        [
            last_sums[0:2],
            sums[2:3],
            sums[0:2],
            sums[3:4],
            jnp.pad(stats, (0, depth - 4))[None],
            jnp.pad(
                jnp.concatenate([part_sums[p][kind] for kind in range(2) for p in range(2)]),
                (0, depth - 2 * width),
            )[None],
            up_sums,
        ],
        axis=0,
    )
    rows, columns = small[:7], small[7:9]
    other = to_core(small)
    rows = rows + other[:7]
    columns = jnp.concatenate([columns[:1], columns[1:] + other[9:]], axis=0)
    small = jnp.concatenate([rows, columns], axis=0)
    meet = lambda x, step: x + lax.ppermute(x, "dp", [(i, i ^ step) for i in range(n_dp)])
    outputs = finish(scalars, 0, [[own_low]], (), 0, 1)
    outputs = finish(scalars, 1, [[to_core(own_low)]], (outputs,), 0, 1)
    ig_far.append(to_chip(after(igs[2], ig_far[1], outputs, small)))
    qkv_ring.hop(ig_far[1])
    small = meet(after(small, ig_far[1]), 1)
    ig_cross = [to_core(x) for x in ig_far[:2]]
    front, back = slice(0, 2), slice(2, 4)
    input_grad = finish(scalars, 0, list(zip(igs, ig_far))[front])
    input_grad = finish(scalars, 1, list(zip(ig_sib, ig_cross))[front], (input_grad,))
    ig_far.append(to_chip(after(igs[3], ig_far[2], input_grad, small)))
    qkv_shard = after(qkv_ring.finish(), ig_far[2])
    step = 2
    while step < n_dp:
        small = meet(after(small, *ig_far[2 : step]), step)
        step *= 2
    up_shard = shard[:, :hidden].astype(F32)
    down_shard = shard[:, hidden : 2 * hidden].astype(F32)
    out_mine = shard[:, 2 * hidden : 2 * hidden + width]
    out_theirs = to_chip(shard[:, 2 * hidden + width :])
    out_shard = out_mine.astype(F32) + out_theirs.astype(F32)

    qkv_new = adam(adam_rows_kernel, qkv_shard, qkv_weight, qkv_first, qkv_second)
    out_new = adam_turned(out_shard, out_weight, out_first, out_second)
    up_new = adam(adam_rows_kernel, up_shard, up_weight, up_first, up_second)
    down_new = adam_turned(down_shard, down_weight, down_first, down_second)
    ig_cross += [to_core(x) for x in ig_far[2:]]
    input_grad = after(input_grad, ig_far[3], up_new[0], down_new[0], qkv_new[0])
    input_grad = finish(scalars, 0, list(zip(igs, ig_far))[back], (input_grad,), 2)
    input_grad = finish(scalars, 1, list(zip(ig_sib, ig_cross))[back], (input_grad,), 2)
    rows = small[:7] + to_chip(after(small[:7], ig_far[3], up_new[0], down_new[0], qkv_new[0]))
    small = jnp.concatenate([rows, small[7:]], axis=0)
    row_total, stat_total = small[:6], small[6]
    col_total = jnp.concatenate(
        [small[7, : 2 * width].reshape(2, width), small[8].reshape(-1, width)], axis=0
    )
    rms_stats = jnp.sqrt(stat_total[:3] / (stat_total[3] * depth))

    row_new = adamw(row_vectors, row_first, row_second, row_total, vector_rate, 0.0)
    col_new = adamw(col_bias, col_first, col_second, col_total, vector_rate, 0.0)
    return (
        outputs,
        input_grad,
        rms_stats,
        *qkv_new,
        *out_new,
        *up_new,
        *down_new,
        *row_new,
        *col_new,
    )


def solution(mesh):
    matrices = [P("dp", None, "mp"), P("mp", "dp"), P("dp", None, "mp"), P(None, "mp", "dp")]
    vectors = [P(), P(None, "mp")]
    groups = [spec for spec in matrices + vectors for _ in range(3)]
    return jax.shard_map(
        body,
        mesh=mesh,
        in_specs=(P("dp", None), P("dp", None), P("dp"), *groups),
        out_specs=(P("dp", None), P("dp", None), P(), *groups),
        check_vma=False,
    )
```
